32 devices in a mesh: expert: 8 (over y, x, core), shard: 4 (over z).
Axes of the slice: x: 2, y: 2, z: 4, core: 2. Of those that a mesh axis runs over, the one named last changes fastest.
Arguments:
- tokens: bfloat16 [4096, 768], P(('expert', 'shard')), may hold values from -6 to 6
- w_qkv: bfloat16 [768, 2304], P('shard'), may hold values from -0.21875 to 0.21875
- w_out: bfloat16 [768, 768], P('shard'), may hold values from -1.25 to 1.25
- w_router: bfloat16 [768, 16], P('shard'), may hold values from -0.15625 to 0.15625
- gain_attn: bfloat16 [768], P('shard'), may hold values from 0.25 to 1.75
- gain_ffn: bfloat16 [768], P('shard'), may hold values from 0.25 to 1.75
- bias_table: bfloat16 [32, 12], P('shard'), may hold values from -3 to 3
- w_in: bfloat16 [16, 768, 3072], P('expert', None, 'shard'), may hold values from -0.21875 to 0.21875
- w_down: bfloat16 [16, 3072, 768], P('expert', 'shard'), may hold values from -0.109375 to 0.109375
- routes: int32 [4096, 2], P(('expert', 'shard')), may hold values from 0 to 15, as said below
- slots: int32 [4096, 2], P(('expert', 'shard')), may hold values from 0 to 23, as said below
- bucket_ids: int32 [128, 128], replicated, may hold values from 0 to 31
- cotangent: bfloat16 [4096, 768], P(('expert', 'shard')), may hold values from -6 to 6
Outputs:
- result: bfloat16 [4096, 768], P(('expert', 'shard'))
- grad_tokens: float32 [4096, 768], P(('expert', 'shard'))
- grad_qkv: float32 [768, 2304], P('shard')
- grad_out: float32 [768, 768], P('shard')
- grad_router: float32 [768, 16], P('shard')
- grad_gain_attn: float32 [768], P('shard')
- grad_gain_ffn: float32 [768], P('shard')
- grad_table: float32 [32, 12], P('shard')
- grad_w_in: float32 [16, 768, 3072], P('expert', None, 'shard')
- grad_w_down: float32 [16, 3072, 768], P('expert', 'shard')
The draws below stay inside these ranges and needn't reach their ends.
Inputs may be any that keep to these rules, and one draw needn't show every extreme that they name: `routes`: the two experts of a token differ. Over the rows of one device, a quarter of the 16 experts are named 24 times, half of them 2 * 24 / 3 times and a quarter 24 / 3 times; one expert is named 24 times by the rows of every device. Over the rows of one device, the choices that name one expert hold the slots 0 up to their number minus one, each once.
All inputs are finite; a program needn't handle non-finite values.
Results may differ from the reference program's by a relative error of at most 0.019.
Values may be sent and summed in bfloat16 or wider, within the bound.
No kernel may reach another device: no remote copies, remote signals or barrier semaphores. Data moves between devices by JAX's collectives and lax.ppermute only.
A program may use at most 128 MiB of HBM per device.

```python
import math
from functools import partial
import jax
import jax.numpy as jnp
from jax import lax

D = 768
HEADS = 12
HEAD_DIM = 64
FF = 3072
BUCKETS = 32
TOK_DEV = 128
EXPERTS = 16
TOKENS = 4096
CAP = 24
N_EXPERT = 8
N_SHARD = 4


def assignment(key):
    hot_expert = jax.random.randint(jax.random.fold_in(key, 1), (), 0, EXPERTS)
    blocks = TOKENS // TOK_DEV
    quarter = EXPERTS // 4
    position = jnp.arange(EXPERTS, dtype=jnp.int32)
    counts = jnp.where(position < quarter, CAP, jnp.where(position < 3 * quarter, 2 * CAP // 3, CAP // 3)).astype(jnp.int32)
    ends = jnp.cumsum(counts)
    starts = ends - counts
    places = jnp.arange(2 * TOK_DEV, dtype=jnp.int32)
    run_index = jnp.sum((ends[None, :] <= places[:, None]).astype(jnp.int32), axis=1)
    slot_list = places - starts[run_index]

    def one_block(number):
        block_key = jax.random.fold_in(key, number + 2)
        order = jax.random.permutation(jax.random.fold_in(block_key, 0), EXPERTS).astype(jnp.int32)
        order = jnp.where(position == 0, hot_expert, jnp.where(order == hot_expert, order[0], order))
        expert_list = order[run_index]
        pair_expert = jnp.stack([expert_list[:TOK_DEV], expert_list[TOK_DEV:]], axis=1)
        pair_slot = jnp.stack([slot_list[:TOK_DEV], slot_list[TOK_DEV:]], axis=1)
        flip = jax.random.randint(jax.random.fold_in(block_key, 1), (TOK_DEV, 1), 0, 2)
        pair_expert = jnp.where(flip == 1, pair_expert[:, ::-1], pair_expert)
        pair_slot = jnp.where(flip == 1, pair_slot[:, ::-1], pair_slot)
        shuffle = jax.random.permutation(jax.random.fold_in(block_key, 2), TOK_DEV)
        return (pair_expert[shuffle], pair_slot[shuffle])
    route_all, slot_all = jax.vmap(one_block)(jnp.arange(blocks, dtype=jnp.int32))
    return (route_all.reshape(TOKENS, 2).astype(jnp.int32), slot_all.reshape(TOKENS, 2).astype(jnp.int32))


def draw_routes(key, part):
    shared = assignment(key)
    return shared[0]


def draw_slots(key, part):
    shared = assignment(key)
    return shared[1]


def plant(entries, stream_key, low, top_value):
    shape = entries.shape
    spot = [jax.random.randint(jax.random.fold_in(stream_key, axis), (), 0, shape[axis]) for axis in range(len(shape))]
    entries = entries.at[tuple(spot)].set(low)
    longest = shape.index(max(shape))
    spot[longest] = (spot[longest] + 1) % shape[longest]
    return entries.at[tuple(spot)].set(top_value)


def block_levels(rng, dims, pieces, smallest, high):
    gain = 1.0
    for dim, parts in pieces:
        draws = jax.random.uniform(jax.random.fold_in(jax.random.fold_in(rng, 6), dim), (parts,), jnp.float32, smallest / len(pieces), high / len(pieces))
        gain = gain * jnp.repeat(jnp.exp(draws), dims[dim] // parts).reshape((-1,) + (1,) * (len(dims) - 1 - dim))
    return gain


def bell_draw(rng, extent, spread, bound, split=(), kind=jnp.bfloat16):
    entries = spread * jax.random.normal(rng, extent, jnp.float32)
    if split:
        entries = entries * block_levels(rng, extent, split, -0.22, 0.18)
    return jnp.clip(entries, -bound, bound).astype(kind)


def setup_inputs(seed: int = 0) -> dict:
    arg_keys = jax.random.split(jax.random.key(seed), 14)
    return {
        "tokens": bell_draw(arg_keys[0], (TOKENS, D), 1.0, 6.0, ((0, 32),)),
        "w_qkv": bell_draw(arg_keys[1], (D, 3 * D), D ** -0.5, 0.21875, ((0, 4),)),
        "w_out": bell_draw(arg_keys[2], (D, D), (4 * D // TOK_DEV) ** -0.5, 1.25, ((0, 4),)),
        "w_router": bell_draw(arg_keys[3], (D, EXPERTS), (2 * D) ** -0.5, 0.15625, ((0, 4),)),
        "gain_attn": jnp.clip(1.0 + 0.15 * jax.random.normal(arg_keys[4], (D,), jnp.float32), 0.25, 1.75).astype(jnp.bfloat16),
        "gain_ffn": jnp.clip(1.0 + 0.15 * jax.random.normal(arg_keys[5], (D,), jnp.float32), 0.25, 1.75).astype(jnp.bfloat16),
        "bias_table": bell_draw(arg_keys[6], (BUCKETS, HEADS), 0.5, 3.0, ((0, 4),)),
        "w_in": bell_draw(arg_keys[7], (EXPERTS, D, FF), D ** -0.5, 0.21875, ((0, 8), (2, 4))),
        "w_down": bell_draw(arg_keys[8], (EXPERTS, FF, D), FF ** -0.5, 0.109375, ((0, 8), (1, 4))),
        "routes": draw_routes(jax.random.fold_in(arg_keys[13], 71), 0),
        "slots": draw_slots(jax.random.fold_in(arg_keys[13], 71), 0),
        "bucket_ids": plant(jax.random.randint(arg_keys[11], (TOK_DEV, TOK_DEV), 0, BUCKETS), jax.random.fold_in(arg_keys[11], 1), 0, BUCKETS - 1).astype(jnp.int32),
        "cotangent": bell_draw(arg_keys[12], (TOKENS, D), 1.0, 6.0, ((0, 32),)),
    }


exact_prec = lax.Precision.HIGHEST
norm_eps = 1e-06

@jax.custom_vjp
def low(v):
    return lax.optimization_barrier(v.astype(jnp.bfloat16)).astype(jnp.float32)

@jax.custom_vjp
def low_back(v):
    return v

def low_keep(v):
    return (low(v), None)

def low_pass(kept, grad):
    return (grad,)

def back_keep(v):
    return (v, None)

def back_low(kept, grad):
    return (low(grad),)
low.defvjp(low_keep, low_pass)
low_back.defvjp(back_keep, back_low)

def attend(block_rows, w_qkv, w_out, gain_attn, bias_table, bucket_ids):
    seq_count = block_rows.shape[0]
    length = block_rows.shape[1]
    inverse_rms = lax.rsqrt(lax.optimization_barrier(jnp.mean(block_rows * block_rows, axis=-1, keepdims=True)) + norm_eps)
    attn_in = low(block_rows * inverse_rms * gain_attn)
    proj_qkv = low(low_back(jnp.einsum('gtd,de->gte', attn_in, w_qkv, precision=exact_prec)))
    queries = proj_qkv[..., :D].reshape(seq_count, length, HEADS, HEAD_DIM)
    key_rows = proj_qkv[..., D:2 * D].reshape(seq_count, length, HEADS, HEAD_DIM)
    values = proj_qkv[..., 2 * D:].reshape(seq_count, length, HEADS, HEAD_DIM)
    pair_bias = jnp.transpose(bias_table[bucket_ids], (2, 0, 1))
    raw_scores = jnp.einsum('gqhe,gkhe->ghqk', queries, key_rows, precision=exact_prec) * 0.125 + pair_bias[None]
    scores = low_back(raw_scores)
    causal = jnp.arange(length)[:, None] >= jnp.arange(length)[None, :]
    attn_probs = jax.nn.softmax(jnp.where(causal, scores, -1e+30), axis=-1)
    weights_low = low(attn_probs)
    mixed_heads = jnp.einsum('ghqk,gkhe->gqhe', weights_low, values, precision=exact_prec)
    mixed_heads = low(low_back(mixed_heads.reshape(seq_count, length, D)))
    branch = low_back(jnp.einsum('gtd,de->gte', mixed_heads, w_out, precision=exact_prec))
    return block_rows + branch

def expert(packed):
    row_block, w_first, w_second = packed
    pre_act = low_back(jnp.dot(row_block, w_first, precision=exact_prec))
    hidden = low(jax.nn.gelu(pre_act))
    return low(low_back(jnp.dot(hidden, w_second, precision=exact_prec)))

def forward(tokens, w_qkv, w_out, w_router, gain_attn, gain_ffn, bias_table, w_in, w_down, routes, slots, bucket_ids):
    seq_count = TOKENS // TOK_DEV
    per_step = math.gcd(seq_count, max(1, 4096 // TOK_DEV))
    grouped = tokens.reshape(seq_count // per_step, per_step, TOK_DEV, D)
    step_fn = jax.checkpoint(partial(attend, w_qkv=w_qkv, w_out=w_out, gain_attn=gain_attn, bias_table=bias_table, bucket_ids=bucket_ids))
    residual = lax.map(step_fn, grouped).reshape(TOKENS, D)
    inverse_rms = lax.rsqrt(lax.optimization_barrier(jnp.mean(residual * residual, axis=-1, keepdims=True)) + norm_eps)
    ffn_in = low(residual * inverse_rms * gain_ffn)
    logits = low_back(jnp.dot(ffn_in, w_router, precision=exact_prec))
    router_probs = jax.nn.softmax(logits, axis=-1)
    picked = jnp.take_along_axis(router_probs, routes, axis=1)
    gate_vals = picked / lax.optimization_barrier(jnp.sum(picked, axis=1, keepdims=True))
    devices = N_EXPERT * N_SHARD
    source = (jnp.arange(TOKENS, dtype=jnp.int32) // TOK_DEV)[:, None]
    slot_index = (routes * (devices * CAP) + source * CAP + slots).astype(jnp.int32).reshape(-1)
    buffer = jnp.zeros((EXPERTS * devices * CAP, D), jnp.float32).at[slot_index].set(jnp.repeat(ffn_in, 2, axis=0))
    buffer = buffer.reshape(EXPERTS, devices * CAP, D)
    outputs = lax.map(jax.checkpoint(expert), (buffer, w_in, w_down)).reshape(EXPERTS * devices * CAP, D)
    returned = outputs[slot_index].reshape(TOKENS, 2, D)
    return residual + lax.optimization_barrier(jnp.sum(gate_vals[:, :, None] * returned, axis=1))

def reference(tokens, w_qkv, w_out, w_router, gain_attn, gain_ffn, bias_table, w_in, w_down, routes, slots, bucket_ids, cotangent):
    floats = [item.astype(jnp.float32) for item in (tokens, w_qkv, w_out, w_router, gain_attn, gain_ffn, bias_table, w_in, w_down)]

    def closed(*params):
        return forward(*params, routes, slots, bucket_ids)
    result, pullback = jax.vjp(closed, *floats)
    gradients = pullback(cotangent.astype(jnp.float32))
    return (result.astype(jnp.bfloat16), gradients[0], gradients[1], gradients[2], gradients[3], gradients[4], gradients[5], gradients[6], gradients[7], gradients[8])
```

```python
import jax
import jax.numpy as jnp
from jax import lax
from jax.sharding import PartitionSpec as P

norm_eps = 1e-06
f32 = jnp.float32
bf16 = jnp.bfloat16


def inverse_rms(values):
    return lax.rsqrt(jnp.mean(values * values, axis=-1, keepdims=True) + norm_eps)


def dot(a, b, ca=1, cb=0):
    return lax.dot_general(a, b, (((ca,), (cb,)), ((), ())), preferred_element_type=f32)


def split_two(v):
    high = v.astype(bf16)
    return high, (v - high.astype(f32)).astype(bf16)


def body(
    tokens,
    w_qkv,
    w_out,
    w_router,
    gain_attn,
    gain_ffn,
    bias_table,
    w_in,
    w_down,
    routes,
    slots,
    bucket_ids,
    cotangent,
):
    length, width = tokens.shape
    ne = lax.axis_size("expert")
    ns = lax.axis_size("shard")
    me_e = lax.axis_index("expert")
    me_s = lax.axis_index("shard")
    core = lax.rem(me_e, 2)
    exp_dev = w_in.shape[0]
    experts = exp_dev * ne
    cap = 3 * length // experts
    block = exp_dev * ns * cap
    total_rows = ne * block
    heads = bias_table.shape[1]
    buckets = bias_table.shape[0] * ns
    head_dim = width // heads
    part = width // ns
    pairs = [(i, i ^ 1) for i in range(ne)]

    def from_shift(v, k):
        return lax.ppermute(v, "shard", [(i, (i + k) % ns) for i in range(ns)])

    def to_shift(v, k):
        return lax.ppermute(v, "shard", [(i, (i - k) % ns) for i in range(ns)])

    def plane(v):
        return lax.all_to_all(v, "expert", split_axis=0, concat_axis=0, tiled=True)

    def gather_weight(w):
        half = w.shape[0] // 2
        own = lax.all_gather(
            lax.dynamic_slice_in_dim(w, core * half, half, 0), "shard", axis=0, tiled=False
        )
        other = lax.ppermute(own, "expert", pairs)
        first = jnp.where(core == 0, own, other)
        second = jnp.where(core == 0, other, own)
        return jnp.stack([first, second], axis=1).reshape(width, w.shape[1])

    smalls = (w_router, gain_attn, gain_ffn, bias_table, routes.astype(bf16), slots.astype(bf16))
    small = jnp.concatenate([v.reshape(-1) for v in smalls])
    small_rows = -(-small.size // width)
    small_rows += -small_rows % 16
    small = jnp.pad(small, (0, small_rows * width - small.size)).reshape(small_rows, width)
    packed = jnp.concatenate([cotangent, small], axis=0)
    line = [packed] + [from_shift(packed, k) for k in range(1, ns)]
    line_small = jnp.stack([v[length:].reshape(-1) for v in line])
    line_g = jnp.concatenate([v[:length] for v in line], axis=0)
    order = lax.rem(me_s - jnp.arange(ns, dtype=jnp.int32) + ns, ns)
    in_order = jnp.take(line_small, order, axis=0)
    full_qkv = gather_weight(w_qkv)
    full_out = gather_weight(w_out)

    cuts = []
    at = 0
    for v in smalls:
        cuts.append((at, at + v.size))
        at += v.size

    def cut(v, i):
        return v[:, cuts[i][0] : cuts[i][1]]

    full_router = cut(in_order, 0).reshape(width, experts)
    gain_one = cut(in_order, 1).reshape(width)
    gain_two = cut(in_order, 2).reshape(width)
    table = cut(in_order, 3).reshape(buckets, heads)
    line_routes = cut(line_small, 4).astype(jnp.int32).reshape(ns * length, 2)
    line_slots = cut(line_small, 5).astype(jnp.int32).reshape(ns * length, 2)
    place = line_routes * (ns * cap) + jnp.repeat(order, length)[:, None] * cap + line_slots
    row_ids = jnp.arange(total_rows, dtype=jnp.int32)
    hot0 = (row_ids[:, None] == place[None, :, 0]).astype(bf16)
    hot1 = (row_ids[:, None] == place[None, :, 1]).astype(bf16)
    hot = hot0 + hot1

    g_rows = dot(hot, line_g).astype(bf16).reshape(ne, block, width)
    low_routes = line_routes.astype(bf16)
    other_route = dot(low_routes[:, 1][None], hot0, 1, 1) + dot(low_routes[:, 0][None], hot1, 1, 1)
    extra = jnp.pad(other_route.astype(bf16).reshape(ne, 1, block), ((0, 0), (0, 15), (0, width - block)))
    g_arrived = plane(jnp.concatenate([g_rows, extra], axis=1))

    x_float = tokens.astype(f32)
    scale_one = inverse_rms(x_float)
    normed_one = x_float * scale_one
    attn_in = (normed_one * gain_one.astype(f32)).astype(bf16)
    bucket_hot = (
        jnp.arange(buckets, dtype=jnp.int32)[:, None] == bucket_ids.reshape(1, -1)
    ).astype(bf16)
    pair_bias = dot(table, bucket_hot, 0, 0).reshape(heads, length, length)
    causal = jnp.arange(length)[:, None] >= jnp.arange(length)[None, :]
    proj_qkv = dot(attn_in, full_qkv).astype(bf16)
    queries = proj_qkv[:, :width].reshape(length, heads, head_dim)
    key_rows = proj_qkv[:, width : 2 * width].reshape(length, heads, head_dim)
    values = proj_qkv[:, 2 * width :].reshape(length, heads, head_dim)
    scores = (
        jnp.einsum("qhe,khe->hqk", queries, key_rows, preferred_element_type=f32) * 0.125
        + pair_bias
    )
    scores = jnp.where(causal[None], scores, -1e30)
    top_score = jnp.max(scores, axis=-1, keepdims=True)
    unnorm = jnp.exp(scores - top_score)
    attn_probs = unnorm / jnp.sum(unnorm, axis=-1, keepdims=True)
    low_probs = attn_probs.astype(bf16)
    mixed_heads = jnp.einsum("hqk,khe->qhe", low_probs, values, preferred_element_type=f32)
    mixed_low = mixed_heads.reshape(length, width).astype(bf16)
    residual = x_float + dot(mixed_low, full_out)
    scale_two = inverse_rms(residual)
    normed_two = residual * scale_two
    ffn_in = (normed_two * gain_two.astype(f32)).astype(bf16)

    line_ffn = jnp.concatenate([ffn_in] + [from_shift(ffn_in, k) for k in range(1, ns)], axis=0)
    sent = dot(hot, line_ffn).astype(bf16).reshape(ne, block, width)
    arrived = plane(sent)
    split_e = 3 * ne // 4
    factors = plane(
        jnp.concatenate(
            [
                jnp.broadcast_to(attn_in[None], (split_e, length, width)),
                jnp.broadcast_to(mixed_low[None], (ne - split_e, length, width)),
            ],
            axis=0,
        )
    ).reshape(ne * length, width)

    logits = dot(ffn_in, full_router)
    router_probs = jax.nn.softmax(logits, axis=-1)
    route_hot = (routes[:, :, None] == jnp.arange(experts, dtype=jnp.int32)[None, None, :]).astype(f32)
    picked = jnp.sum(route_hot * router_probs[:, None, :], axis=-1)
    picked_total = jnp.sum(picked, axis=1, keepdims=True)

    def by_expert(v):
        return v.reshape(ne, exp_dev, ns * cap, -1).transpose(1, 0, 2, 3).reshape(
            exp_dev, ne * ns * cap, -1
        )

    def by_source(v):
        return v.reshape(exp_dev, ne, ns * cap, -1).transpose(1, 0, 2, 3).reshape(ne, block, -1)

    rows = by_expert(arrived)
    g_in = by_expert(g_arrived[:, :block]).astype(f32)
    row_other = by_expert(g_arrived[:, block, :block]).astype(jnp.int32)
    row_logits = jnp.einsum("jrd,de->jre", rows, full_router, preferred_element_type=f32)
    ids = jnp.arange(experts, dtype=jnp.int32)
    own_ids = me_e * exp_dev + jnp.arange(exp_dev, dtype=jnp.int32)
    own_logit = jnp.sum(jnp.where(ids == own_ids[:, None, None], row_logits, 0.0), -1, keepdims=True)
    other_logit = jnp.sum(jnp.where(ids == row_other, row_logits, 0.0), -1, keepdims=True)
    gate = 1.0 / (1.0 + jnp.exp(other_logit - own_logit))
    d_y = (gate * g_in).astype(bf16)
    pre_act = jnp.einsum("jrd,jdf->jrf", rows, w_in, preferred_element_type=f32)
    hidden_full, gelu_back = jax.vjp(jax.nn.gelu, pre_act)
    hidden = hidden_full.astype(bf16)
    y_part = jnp.einsum("jrf,jfd->jrd", hidden, w_down, preferred_element_type=f32)
    d_gate_part = jnp.sum(g_in * y_part, axis=-1, keepdims=True)
    y_send = by_source((gate * y_part).astype(bf16))
    d_hidden = jnp.einsum("jrd,jfd->jrf", d_y, w_down, preferred_element_type=f32)
    d_pre = gelu_back(d_hidden)[0].astype(bf16)
    d_rows = jnp.einsum("jrf,jdf->jrd", d_pre, w_in, preferred_element_type=f32).astype(bf16)
    dg_rows = by_source(d_gate_part).reshape(ne, 1, block)
    dg_high, dg_low = split_two(dg_rows)
    extra = jnp.pad(
        jnp.concatenate([dg_high, dg_low], axis=1), ((0, 0), (0, 14), (0, width - block))
    )
    d_back = plane(jnp.concatenate([by_source(d_rows), extra], axis=1))
    d_back, y_send = lax.optimization_barrier((d_back, y_send))
    y_back = plane(y_send)
    grad_w_down = jnp.einsum("jrf,jrd->jfd", hidden, d_y, preferred_element_type=f32)
    grad_w_in = jnp.einsum("jrd,jrf->jdf", rows, d_pre, preferred_element_type=f32)

    d_line = dot(hot, d_back[:, :block].reshape(total_rows, width), 0, 0)
    dg_flat = d_back[:, block : block + 2, :block].astype(f32).sum(axis=1).reshape(1, total_rows)
    dg_high, dg_low = split_two(dg_flat)
    dg_pair = jnp.concatenate([dg_high, dg_low], axis=0)
    dg_line = jnp.concatenate(
        [dot(dg_pair, h, 1, 0).sum(axis=0, keepdims=True) for h in (hot0, hot1)], axis=0
    )
    own_d = d_line[:length]
    own_dg = dg_line[:, :length]
    for k in range(1, ns):
        lines = slice(k * length, (k + 1) * length)
        high, low = split_two(dg_line[:, lines])
        extra = jnp.pad(jnp.concatenate([high, low], axis=0), ((0, 12), (0, width - length)))
        got = to_shift(jnp.concatenate([d_line[lines].astype(bf16), extra], axis=0), k).astype(f32)
        own_d = own_d + got[:length]
        own_dg = own_dg + got[length : length + 2, :length] + got[length + 2 : length + 4, :length]
    d_from_experts = own_d
    d_gates = own_dg.T
    y_line = dot(hot, y_back.reshape(total_rows, width), 0, 0)
    y_sum = y_line[:length]
    for k in range(1, ns):
        y_sum = y_sum + to_shift(y_line[k * length : (k + 1) * length].astype(bf16), k).astype(f32)
    result = (residual + y_sum).astype(bf16)

    d_result = cotangent.astype(f32)
    d_picked = d_gates / picked_total - jnp.sum(d_gates * picked, axis=1, keepdims=True) / (
        picked_total * picked_total
    )
    d_router = jnp.sum(route_hot * d_picked[:, :, None], axis=1)
    d_logits = (
        router_probs * (d_router - jnp.sum(router_probs * d_router, axis=-1, keepdims=True))
    ).astype(bf16)
    grad_router = dot(ffn_in, d_logits, 0, 0)
    d_ffn_in = d_from_experts + dot(d_logits, full_router, 1, 1)
    grad_gain_two = jnp.sum(d_ffn_in * normed_two, axis=0)
    d_norm_two = d_ffn_in * gain_two.astype(f32)
    d_residual = d_result + scale_two * (
        d_norm_two - normed_two * jnp.mean(d_norm_two * normed_two, axis=-1, keepdims=True)
    )
    d_branch = d_residual.astype(bf16)
    d_heads = dot(d_branch, full_out, 1, 1).astype(bf16).reshape(length, heads, head_dim)
    d_values = jnp.einsum("hqk,qhe->khe", low_probs, d_heads, preferred_element_type=f32)
    d_probs = jnp.einsum("qhe,khe->hqk", d_heads, values, preferred_element_type=f32)
    d_scores = attn_probs * (d_probs - jnp.sum(attn_probs * d_probs, axis=-1, keepdims=True))
    d_scores = d_scores.astype(bf16)
    d_queries = jnp.einsum("hqk,khe->qhe", d_scores, key_rows, preferred_element_type=f32) * 0.125
    d_keys = jnp.einsum("hqk,qhe->khe", d_scores, queries, preferred_element_type=f32) * 0.125
    grad_table = dot(bucket_hot, d_scores.reshape(heads, length * length), 1, 1)
    d_proj = jnp.concatenate(
        [v.reshape(length, width) for v in (d_queries, d_keys, d_values)], axis=1
    ).astype(bf16)
    d_attn_in = dot(d_proj, full_qkv, 1, 1)
    grad_gain_one = jnp.sum(d_attn_in * normed_one, axis=0)
    d_norm_one = d_attn_in * gain_one.astype(f32)
    grad_tokens = d_residual + scale_one * (
        d_norm_one - normed_one * jnp.mean(d_norm_one * normed_one, axis=-1, keepdims=True)
    )

    columns = 4 * width // ne
    small_parts = [
        grad_router.reshape(ns, -1),
        grad_gain_one.reshape(ns, -1),
        grad_gain_two.reshape(ns, -1),
        grad_table.reshape(ns, -1),
    ]
    sizes = [v.shape[1] for v in small_parts]
    small = jnp.concatenate(small_parts, axis=1)
    each = -(-small.shape[1] // ne)
    srows = -(-each // columns)
    while ns * srows % 16:
        srows += 1
    room = srows * columns
    small = jnp.pad(small, ((0, 0), (0, ne * each - small.shape[1]))).reshape(ns, ne, each)
    small = jnp.pad(small, ((0, 0), (0, 0), (0, room - each))).transpose(1, 0, 2)
    small = small.reshape(ne, ns * srows, columns).astype(bf16)
    wide = jnp.concatenate([d_proj, d_branch], axis=1).reshape(length, ne, columns).transpose(1, 0, 2)
    wide = plane(jnp.concatenate([wide, small], axis=1))
    small = jnp.sum(wide[:, length:].astype(f32), axis=0).reshape(ns, srows, columns)
    pad_rows = -srows % 16
    product = dot(factors, wide[:, :length].reshape(ne * length, columns), 0, 0)
    product = jnp.concatenate(
        [
            product.reshape(ns, part, columns),
            jnp.pad(small, ((0, 0), (0, pad_rows), (0, 0))),
        ],
        axis=1,
    )
    low_product = product.astype(bf16)
    share = lax.dynamic_index_in_dim(product, me_s, 0, keepdims=False)
    for k in range(1, ns):
        other = lax.dynamic_index_in_dim(
            low_product, lax.rem(me_s - k + ns, ns), 0, keepdims=False
        )
        share = share + to_shift(other, k).astype(f32)
    share = share.astype(bf16)
    whole = plane(jnp.broadcast_to(share[None], (ne,) + share.shape)).astype(f32)
    grads = whole[:, :part]
    out_qkv = grads[:split_e].transpose(1, 0, 2).reshape(part, 3 * width)
    out_out = grads[split_e:].transpose(1, 0, 2).reshape(part, width)
    small = whole[:, part : part + srows].reshape(ne, room)[:, :each].reshape(-1)
    pieces = []
    at = 0
    for size in sizes:
        pieces.append(small[at : at + size])
        at += size
    return (
        result,
        grad_tokens,
        out_qkv,
        out_out,
        pieces[0].reshape(part, experts),
        pieces[1],
        pieces[2],
        pieces[3].reshape(buckets // ns, heads),
        grad_w_in,
        grad_w_down,
    )


def solution(mesh):
    in_specs = (
        P(("expert", "shard"), None),
        P("shard", None),
        P("shard", None),
        P("shard", None),
        P("shard"),
        P("shard"),
        P("shard", None),
        P("expert", None, "shard"),
        P("expert", "shard", None),
        P(("expert", "shard"), None),
        P(("expert", "shard"), None),
        P(),
        P(("expert", "shard"), None),
    )
    out_specs = (
        P(("expert", "shard"), None),
        P(("expert", "shard"), None),
        P("shard", None),
        P("shard", None),
        P("shard", None),
        P("shard"),
        P("shard"),
        P("shard", None),
        P("expert", None, "shard"),
        P("expert", "shard", None),
    )
    return jax.shard_map(body, mesh=mesh, in_specs=in_specs, out_specs=out_specs, check_vma=False)
```

```python
import functools

import jax
import jax.numpy as jnp
from jax import lax
from jax.experimental import pallas as pl
from jax.experimental.pallas import tpu as pltpu
from jax.sharding import PartitionSpec as P

norm_eps = 1e-06
f32 = jnp.float32
bf16 = jnp.bfloat16
lane = 128


def inverse_rms(values):
    return lax.rsqrt(jnp.mean(values * values, axis=-1, keepdims=True) + norm_eps)


def dot(a, b, ca=1, cb=0):
    return lax.dot_general(a, b, (((ca,), (cb,)), ((), ())), preferred_element_type=f32)


def split_two(v):
    high = v.astype(bf16)
    return high, (v - high.astype(f32)).astype(bf16)


def local_call(kernel, outs, args, scalars=0, views=None, flops=0, moved=0):
    specs = [pl.BlockSpec(memory_space=pltpu.SMEM)] * scalars
    specs += [pl.BlockSpec(memory_space=pltpu.VMEM)] * (len(args) - scalars)
    for n, (shape, where) in (views or {}).items():
        specs[n] = pl.BlockSpec(shape, lambda i, where=where: where)
    return pl.pallas_call(
        kernel,
        out_shape=[jax.ShapeDtypeStruct(shape, kind) for shape, kind in outs],
        grid=(1,),
        in_specs=specs,
        out_specs=[pl.BlockSpec(memory_space=pltpu.VMEM)] * len(outs),
        compiler_params=pltpu.CompilerParams(vmem_limit_bytes=48 << 20),
        cost_estimate=pl.CostEstimate(flops=flops, bytes_accessed=moved, transcendentals=0),
    )(*args)


def join_blocks(e, s, parts, full_ref):
    count = 2 * parts[0].shape[1]
    rows, cols = parts[0].shape[2], parts[0].shape[3]
    for n, ref in enumerate(parts):
        bits = ((2, 4), (4, 2))[n // 2]
        for i in range(ref.shape[0]):
            differ = (i & 1) * bits[0] + (i >> 1) * bits[1] + n % 2
            col = pl.multiple_of(((e & 7) ^ differ) * cols, lane)
            for q in range(count // 2):
                source = lax.rem(s - (q + (n // 2) * (count // 2)) + count, count)
                row = pl.multiple_of(source * rows, 16)
                full_ref[pl.ds(row, rows), pl.ds(col, cols)] = ref[i, q]


def head_mask(shape, h, head_dim):
    return lax.broadcasted_iota(jnp.int32, shape, 1) // head_dim == h


def attend_kernel(
    ids_ref, tok_ref, gain_ref, gain_two_ref, a_ref, a_other_ref, b_ref, b_other_ref, bias_ref,
    attn_ref, proj_ref, probs_ref, mixed_ref, res_ref, ffn_ref, full_ref,
):
    join_blocks(ids_ref[0], ids_ref[1], (a_ref, a_other_ref, b_ref, b_other_ref), full_ref)
    length, width = tok_ref.shape
    heads = bias_ref.shape[0]
    head_dim = width // heads
    pack = lane // head_dim
    x = tok_ref[...].astype(f32)
    low = (x * inverse_rms(x) * gain_ref[...]).astype(bf16)
    attn_ref[...] = low
    step = width // 2
    for c in range(6):
        cols = slice(c * step, (c + 1) * step)
        proj_ref[:, cols] = dot(low, full_ref[:, cols]).astype(bf16)
    for g in range(heads // pack):
        q = proj_ref[:, g * lane : (g + 1) * lane]
        k = proj_ref[:, width + g * lane : width + (g + 1) * lane]
        v = proj_ref[:, 2 * width + g * lane : 2 * width + (g + 1) * lane]
        total = jnp.zeros((length, lane), f32)
        for h in range(pack):
            keep = head_mask((length, lane), h, head_dim)
            s = dot(q, jnp.where(keep, k, jnp.zeros_like(k)), 1, 1) * 0.125 + bias_ref[g * pack + h]
            e = jnp.exp(s - jnp.max(s, axis=-1, keepdims=True))
            p = e / jnp.sum(e, axis=-1, keepdims=True)
            probs_ref[g * pack + h] = p
            total = total + dot(p.astype(bf16), jnp.where(keep, v, jnp.zeros_like(v)))
        mixed_ref[:, g * lane : (g + 1) * lane] = total.astype(bf16)
    res = x + dot(mixed_ref[...], full_ref[:, 3 * width :])
    res_ref[...] = res
    ffn_ref[...] = (res * inverse_rms(res) * gain_two_ref[...]).astype(bf16)


def expert_kernel(
    ids_ref, rows_ref, g_ref, wi_ref, wd_ref, router_ref,
    send_ref, y_ref, rows_out, hidden_out, dpre_out, dy_out,
):
    j = pl.program_id(0)
    count, per, width = rows_ref.shape
    total = count * per
    experts = router_ref.shape[1]
    x = rows_ref[...].reshape(total, width)
    rows_out[0] = x
    g = g_ref[:, :, :width].reshape(total, width).astype(f32)
    tags = g_ref[:, :, width:].reshape(total, lane).astype(f32)
    other, choice = tags[:, 0:1], tags[:, 1:2]
    logits = dot(x, router_ref[...])
    ids = lax.broadcasted_iota(jnp.int32, (total, experts), 1)
    own_logit = jnp.sum(jnp.where(ids == ids_ref[0] + j, logits, 0.0), -1, keepdims=True)
    other_logit = jnp.sum(jnp.where(ids.astype(f32) == other, logits, 0.0), -1, keepdims=True)
    gate = 1.0 / (1.0 + jnp.exp(other_logit - own_logit))
    d_y = (gate * g).astype(bf16)
    dy_out[0] = d_y
    pre = dot(x, wi_ref[0])
    square = pre * pre
    tanh = jnp.tanh(0.7978845608028654 * pre * (1.0 + 0.044715 * square))
    hidden = (0.5 * pre * (1.0 + tanh)).astype(bf16)
    hidden_out[0] = hidden
    slope = 0.5 * (1.0 + tanh) + 0.5 * pre * (1.0 - tanh * tanh) * (
        0.7978845608028654 * (1.0 + 3.0 * 0.044715 * square)
    )
    d_pre = (dot(d_y, wd_ref[0], 1, 1) * slope).astype(bf16)
    dpre_out[0] = d_pre
    at = pl.multiple_of(j * per, 16)
    d_rows = dot(d_pre, wi_ref[0], 1, 1).astype(bf16)
    send_ref[:, pl.ds(at, per), :width] = d_rows.reshape(count, per, width)
    y = dot(hidden, wd_ref[0])
    y_ref[:, pl.ds(at, per), :] = (gate * y).astype(bf16).reshape(count, per, width)
    d_gate = jnp.sum(g * y, axis=-1, keepdims=True)
    high = d_gate.astype(bf16).astype(f32)
    cols = lax.broadcasted_iota(jnp.int32, (total, lane), 1).astype(f32)
    tail = jnp.where(cols == choice, high, jnp.where(cols == choice + 2.0, d_gate - high, 0.0))
    send_ref[:, pl.ds(at, per), width:] = tail.astype(bf16).reshape(count, per, lane)


def collect_kernel(back_ref, hot_ref, own_ref, *pay_refs):
    length = own_ref.shape[0]
    rows = back_ref[...].reshape(-1, back_ref.shape[2])
    for k in range(len(pay_refs) + 1):
        got = dot(hot_ref[k * length : (k + 1) * length, :], rows)
        if k == 0:
            own_ref[...] = got
        else:
            pay_refs[k - 1][...] = got.astype(bf16)


def backward_kernel(count, *refs):
    own_ref = refs[0]
    got_refs = refs[1 : 1 + count]
    (
        ffn_ref, res_ref, cot_ref, router_ref, routes_ref, gain_ref, full_ref, proj_ref, probs_ref,
        wide_ref, dres_ref, dlog_ref, gain_grad_ref, ds_ref, dproj_ref,
    ) = refs[1 + count :]
    length, width = ffn_ref.shape
    heads = probs_ref.shape[0]
    head_dim = width // heads
    pack = lane // head_dim
    experts = router_ref.shape[1]
    d = own_ref[...]
    for ref in got_refs:
        d = d + ref[...].astype(f32)
    tail = d[:, width:]
    d = d[:, :width]
    dg = [tail[:, i : i + 1] + tail[:, i + 2 : i + 3] for i in range(2)]
    logits = dot(ffn_ref[...], router_ref[...])
    e = jnp.exp(logits - jnp.max(logits, axis=-1, keepdims=True))
    router = e / jnp.sum(e, axis=-1, keepdims=True)
    ids = lax.broadcasted_iota(jnp.int32, (length, experts), 1)
    hots = [ids == routes_ref[:, i : i + 1] for i in range(2)]
    picked = [jnp.sum(jnp.where(h, router, 0.0), -1, keepdims=True) for h in hots]
    both = picked[0] + picked[1]
    mean = (dg[0] * picked[0] + dg[1] * picked[1]) / (both * both)
    d_router = sum(jnp.where(h, v / both - mean, 0.0) for h, v in zip(hots, dg))
    d_logits = router * (d_router - jnp.sum(router * d_router, -1, keepdims=True))
    d_logits = d_logits.astype(bf16)
    dlog_ref[...] = d_logits
    d_ffn = d + dot(d_logits, router_ref[...], 1, 1)
    res = res_ref[...]
    inv = inverse_rms(res)
    normed = res * inv
    gain_grad_ref[...] = jnp.sum(d_ffn * normed, axis=0, keepdims=True)
    d_norm = d_ffn * gain_ref[...]
    d_res = cot_ref[...].astype(f32) + inv * (
        d_norm - normed * jnp.mean(d_norm * normed, axis=-1, keepdims=True)
    )
    dres_ref[...] = d_res
    d_branch = d_res.astype(bf16)
    d_heads = dot(d_branch, full_ref[...], 1, 1).astype(bf16)
    for g in range(heads // pack):
        q = proj_ref[:, g * lane : (g + 1) * lane]
        k = proj_ref[:, width + g * lane : width + (g + 1) * lane]
        v = proj_ref[:, 2 * width + g * lane : 2 * width + (g + 1) * lane]
        dh = d_heads[:, g * lane : (g + 1) * lane]
        zero = jnp.zeros_like(q)
        sums = [jnp.zeros((length, lane), f32) for _ in range(3)]
        for h in range(pack):
            keep = head_mask((length, lane), h, head_dim)
            p = probs_ref[g * pack + h]
            dh_one = jnp.where(keep, dh, zero)
            d_probs = dot(dh_one, v, 1, 1)
            ds = p * (d_probs - jnp.sum(p * d_probs, axis=-1, keepdims=True))
            ds = ds.astype(bf16)
            ds_ref[g * pack + h] = ds
            sums[0] = sums[0] + dot(ds, jnp.where(keep, k, zero))
            sums[1] = sums[1] + dot(ds, jnp.where(keep, q, zero), 0, 0)
            sums[2] = sums[2] + dot(p.astype(bf16), dh_one, 0, 0)
        for i, scale in enumerate((0.125, 0.125, 1.0)):
            dproj_ref[:, i * width + g * lane : i * width + (g + 1) * lane] = (sums[i] * scale).astype(bf16)
    columns = wide_ref.shape[2]
    split = 3 * width // columns
    for b in range(wide_ref.shape[0]):
        if b < split:
            wide_ref[b] = dproj_ref[:, b * columns : (b + 1) * columns]
        else:
            wide_ref[b] = d_branch[:, (b - split) * columns : (b - split + 1) * columns]


def unpack_kernel(whole_ref, qkv_ref, out_ref, small_ref):
    count, _, cols = whole_ref.shape
    part, width = out_ref.shape
    split = 3 * width // cols
    for b in range(count):
        got = whole_ref[b, :part, :].astype(f32)
        if b < split:
            qkv_ref[:, b * cols : (b + 1) * cols] = got
        else:
            out_ref[:, (b - split) * cols : (b - split + 1) * cols] = got
    small_ref[...] = jnp.sum(whole_ref[:, part:, :].astype(f32), axis=0)


def tokens_kernel(dproj_ref, full_ref, tok_ref, gain_ref, dres_ref, out_ref, gain_grad_ref):
    d_in = dot(dproj_ref[...], full_ref[...], 1, 1)
    x = tok_ref[...].astype(f32)
    inv = inverse_rms(x)
    normed = x * inv
    gain_grad_ref[...] = jnp.sum(d_in * normed, axis=0, keepdims=True)
    d_norm = d_in * gain_ref[...]
    out_ref[...] = dres_ref[...] + inv * (
        d_norm - normed * jnp.mean(d_norm * normed, axis=-1, keepdims=True)
    )


def body(
    tokens,
    w_qkv,
    w_out,
    w_router,
    gain_attn,
    gain_ffn,
    bias_table,
    w_in,
    w_down,
    routes,
    slots,
    bucket_ids,
    cotangent,
):
    length, width = tokens.shape
    ne = lax.axis_size("expert")
    ns = lax.axis_size("shard")
    me_e = lax.axis_index("expert")
    me_s = lax.axis_index("shard")
    place_ids = jnp.stack([me_e, me_s]).astype(jnp.int32)
    exp_dev = w_in.shape[0]
    hidden_units = w_in.shape[2]
    experts = exp_dev * ne
    cap = 3 * length // experts
    per = ns * cap
    block = exp_dev * per
    total_rows = ne * block
    group_rows = ne * per
    heads = bias_table.shape[1]
    buckets = bias_table.shape[0] * ns
    part = width // ns

    def from_shift(v, k):
        return lax.ppermute(v, "shard", [(i, (i + k) % ns) for i in range(ns)])

    def to_shift(v, k):
        return lax.ppermute(v, "shard", [(i, (i - k) % ns) for i in range(ns)])

    def plane(v):
        return lax.all_to_all(v, "expert", split_axis=0, concat_axis=0, tiled=True)

    def across(v, bit):
        return lax.ppermute(v, "expert", [(i, i ^ bit) for i in range(ne)])

    cols = width // 2
    mine = me_e & 7
    weight = jnp.where(
        mine < 6,
        lax.dynamic_slice_in_dim(w_qkv, jnp.minimum(mine, 5) * cols, cols, 1),
        lax.dynamic_slice_in_dim(w_out, (jnp.maximum(mine, 6) - 6) * cols, cols, 1),
    )
    line = [weight] + [from_shift(weight, k) for k in range(1, ns)]

    smalls = (w_router, gain_attn, gain_ffn, bias_table, routes.astype(bf16), slots.astype(bf16))
    small = jnp.concatenate([v.reshape(-1) for v in smalls])
    small_rows = -(-small.size // width)
    small_rows += -small_rows % 16
    small = jnp.pad(small, (0, small_rows * width - small.size)).reshape(small_rows, width)
    packed = jnp.concatenate([cotangent, small], axis=0)
    packed, line = lax.optimization_barrier((packed, line))
    pieces = []
    for half, bits in ((line[: ns // 2], (2, 4)), (line[ns // 2 :], (4, 2))):
        held = jnp.stack(half)[None]
        for bit in bits:
            held = jnp.concatenate([held, across(held, bit)], axis=0)
        pieces += [held, across(held, 1)]
    line = [packed] + [from_shift(packed, k) for k in range(1, ns)]
    line_small = jnp.stack([v[length:].reshape(-1) for v in line])
    line_g = jnp.concatenate([v[:length] for v in line], axis=0)
    order = lax.rem(me_s - jnp.arange(ns, dtype=jnp.int32) + ns, ns)
    in_order = jnp.take(line_small, order, axis=0)

    cuts = []
    at = 0
    for v in smalls:
        cuts.append((at, at + v.size))
        at += v.size

    def cut(v, i):
        return v[:, cuts[i][0] : cuts[i][1]]

    full_router = cut(in_order, 0).reshape(width, experts)
    gain_one = cut(in_order, 1).reshape(1, width).astype(f32)
    gain_two = cut(in_order, 2).reshape(1, width).astype(f32)
    table = cut(in_order, 3).reshape(buckets, heads)
    line_routes = cut(line_small, 4).reshape(ns * length, 2)
    line_slots = cut(line_small, 5).reshape(ns * length, 2).astype(jnp.int32)
    place = (
        line_routes.astype(jnp.int32) * per + jnp.repeat(order, length)[:, None] * cap + line_slots
    )
    row_ids = jnp.arange(total_rows, dtype=jnp.int32)
    hot0 = (row_ids[:, None] == place[None, :, 0]).astype(bf16)
    hot1 = (row_ids[:, None] == place[None, :, 1]).astype(bf16)
    hot = hot0 + hot1
    hot_back = (
        (row_ids[None, :] == place[:, 0:1]) | (row_ids[None, :] == place[:, 1:2])
    ).astype(bf16)

    def tagged(i):
        tag = jnp.concatenate([line_routes[:, 1 - i : 2 - i], jnp.full((ns * length, 1), i, bf16)], 1)
        return jnp.concatenate([line_g, jnp.pad(tag, ((0, 0), (0, lane - 2)))], axis=1)

    g_rows = (dot(hot0, tagged(0)) + dot(hot1, tagged(1))).astype(bf16)
    g_rows = g_rows.reshape(ne, block, width + lane)
    g_arrived = plane(g_rows)

    causal = jnp.arange(length)[:, None] >= jnp.arange(length)[None, :]
    bucket_hot = (
        jnp.arange(buckets, dtype=jnp.int32)[:, None] == bucket_ids.reshape(1, -1)
    ).astype(bf16)
    pair_bias = dot(table, bucket_hot, 0, 0).reshape(heads, length, length)
    pair_bias = jnp.where(causal[None], pair_bias, -1e30)
    attn_in, proj, probs, mixed_low, residual, ffn_in, full = local_call(
        attend_kernel,
        [
            ((length, width), bf16),
            ((length, 3 * width), bf16),
            ((heads, length, length), f32),
            ((length, width), bf16),
            ((length, width), f32),
            ((length, width), bf16),
            ((width, 4 * width), bf16),
        ],
        [place_ids, tokens, gain_one, gain_two, *pieces, pair_bias],
        scalars=1,
        flops=2 * length * width * 4 * width + 4 * heads * length * length * lane,
        moved=4 * width * 4 * width + 8 * heads * length * length,
    )

    split_e = 3 * ne // 4
    factors = plane(
        jnp.concatenate(
            [
                jnp.broadcast_to(attn_in[None], (split_e, length, width)),
                jnp.broadcast_to(mixed_low[None], (ne - split_e, length, width)),
            ],
            axis=0,
        )
    ).reshape(ne * length, width)
    line_ffn = jnp.concatenate([ffn_in] + [from_shift(ffn_in, k) for k in range(1, ns)], axis=0)
    line_ffn, factors = lax.optimization_barrier((line_ffn, factors))
    arrived = plane(dot(hot, line_ffn).astype(bf16).reshape(ne, block, width))

    wide_width = width + lane
    first_id = (me_e * exp_dev).astype(jnp.int32).reshape(1)
    send, y_send, rows, hidden, d_pre, d_y = pl.pallas_call(
        expert_kernel,
        out_shape=[
            jax.ShapeDtypeStruct((ne, block, wide_width), bf16),
            jax.ShapeDtypeStruct((ne, block, width), bf16),
            jax.ShapeDtypeStruct((exp_dev, group_rows, width), bf16),
            jax.ShapeDtypeStruct((exp_dev, group_rows, hidden_units), bf16),
            jax.ShapeDtypeStruct((exp_dev, group_rows, hidden_units), bf16),
            jax.ShapeDtypeStruct((exp_dev, group_rows, width), bf16),
        ],
        grid=(exp_dev,),
        in_specs=[
            pl.BlockSpec(memory_space=pltpu.SMEM),
            pl.BlockSpec((ne, per, width), lambda j: (0, j, 0)),
            pl.BlockSpec((ne, per, wide_width), lambda j: (0, j, 0)),
            pl.BlockSpec((1, width, hidden_units), lambda j: (j, 0, 0)),
            pl.BlockSpec((1, hidden_units, width), lambda j: (j, 0, 0)),
            pl.BlockSpec((width, experts), lambda j: (0, 0)),
        ],
        out_specs=[
            pl.BlockSpec((ne, block, wide_width), lambda j: (0, 0, 0)),
            pl.BlockSpec((ne, block, width), lambda j: (0, 0, 0)),
            pl.BlockSpec((1, group_rows, width), lambda j: (j, 0, 0)),
            pl.BlockSpec((1, group_rows, hidden_units), lambda j: (j, 0, 0)),
            pl.BlockSpec((1, group_rows, hidden_units), lambda j: (j, 0, 0)),
            pl.BlockSpec((1, group_rows, width), lambda j: (j, 0, 0)),
        ],
        compiler_params=pltpu.CompilerParams(vmem_limit_bytes=56 << 20),
        cost_estimate=pl.CostEstimate(
            flops=8 * exp_dev * group_rows * width * hidden_units,
            bytes_accessed=16 * exp_dev * group_rows * width,
            transcendentals=0,
        ),
    )(first_id, arrived, g_arrived, w_in, w_down, full_router)
    d_back = plane(send)
    grad_w_down = jnp.einsum("jrf,jrd->jfd", hidden, d_y, preferred_element_type=f32)
    grad_w_in = jnp.einsum("jrd,jrf->jdf", rows, d_pre, preferred_element_type=f32)
    d_back, y_send, grad_w_down, grad_w_in = lax.optimization_barrier(
        (d_back, y_send, grad_w_down, grad_w_in)
    )
    y_back = plane(y_send)

    own_d, *pays = local_call(
        collect_kernel,
        [((length, wide_width), f32)] + [((length, wide_width), bf16)] * (ns - 1),
        [d_back, hot_back],
        flops=2 * ns * length * total_rows * wide_width,
        moved=2 * total_rows * wide_width,
    )
    got = [to_shift(v, k + 1) for k, v in enumerate(pays)]
    columns = 4 * width // ne
    wide, d_residual, d_logits, gain_two_grad, d_scores, d_proj = local_call(
        functools.partial(backward_kernel, ns - 1),
        [
            ((ne, length, columns), bf16),
            ((length, width), f32),
            ((length, experts), bf16),
            ((1, width), f32),
            ((heads, length, length), bf16),
            ((length, 3 * width), bf16),
        ],
        [own_d, *got, ffn_in, residual, cotangent, full_router, routes, gain_two, full, proj, probs],
        views={ns + 6: ((width, width), (0, 3))},
        flops=2 * length * width * width + 10 * heads * length * length * lane,
        moved=2 * width * width + 8 * heads * length * length,
    )
    wide, y_back = lax.optimization_barrier((wide, y_back))
    wide = plane(wide)
    grad_tokens, gain_one_grad = local_call(
        tokens_kernel,
        [((length, width), f32), ((1, width), f32)],
        [d_proj, full, tokens, gain_one, d_residual],
        views={1: ((width, 3 * width), (0, 0))},
        flops=2 * length * width * 3 * width,
        moved=2 * width * 3 * width,
    )
    grad_router = dot(ffn_in, d_logits, 0, 0)
    grad_table = dot(bucket_hot, d_scores.reshape(heads, length * length), 1, 1)

    y_line = dot(hot_back, y_back.reshape(total_rows, width))
    y_got = [to_shift(y_line[k * length : (k + 1) * length].astype(bf16), k) for k in range(1, ns)]
    result = residual + y_line[:length]
    for v in y_got:
        result = result + v.astype(f32)
    result = result.astype(bf16)
    small_parts = [
        grad_router.reshape(ns, -1),
        gain_one_grad.reshape(ns, -1),
        gain_two_grad.reshape(ns, -1),
        grad_table.reshape(ns, -1),
    ]
    sizes = [v.shape[1] for v in small_parts]
    small = jnp.concatenate(small_parts, axis=1).astype(bf16)
    each = small.shape[1]
    srows = -(-each // columns)
    srows += -srows % 16
    room = srows * columns
    small = jnp.pad(small, ((0, 0), (0, room - each))).reshape(ns, srows, columns)
    product = dot(factors, wide.reshape(ne * length, columns), 0, 0).astype(bf16)
    product = jnp.concatenate([product.reshape(ns, part, columns), small], axis=1)
    product, result = lax.optimization_barrier((product, result))
    share = lax.dynamic_index_in_dim(product, me_s, 0, keepdims=False).astype(f32)
    for k in range(1, ns):
        piece = lax.dynamic_index_in_dim(product, lax.rem(me_s - k + ns, ns), 0, keepdims=False)
        share = share + to_shift(piece, k).astype(f32)
    share = share.astype(bf16)
    whole = plane(jnp.broadcast_to(share[None], (ne,) + share.shape))
    out_qkv, out_out, small = local_call(
        unpack_kernel,
        [((part, 3 * width), f32), ((part, width), f32), ((srows, columns), f32)],
        [whole],
        moved=6 * ne * (part + srows) * columns,
    )
    small = small.reshape(-1)
    smalls = []
    at = 0
    for size in sizes:
        smalls.append(small[at : at + size])
        at += size

    return (
        result,
        grad_tokens,
        out_qkv,
        out_out,
        smalls[0].reshape(part, experts),
        smalls[1],
        smalls[2],
        smalls[3].reshape(buckets // ns, heads),
        grad_w_in,
        grad_w_down,
    )


def solution(mesh):
    in_specs = (
        P(("expert", "shard"), None),
        P("shard", None),
        P("shard", None),
        P("shard", None),
        P("shard"),
        P("shard"),
        P("shard", None),
        P("expert", None, "shard"),
        P("expert", "shard", None),
        P(("expert", "shard"), None),
        P(("expert", "shard"), None),
        P(),
        P(("expert", "shard"), None),
    )
    out_specs = (
        P(("expert", "shard"), None),
        P(("expert", "shard"), None),
        P("shard", None),
        P("shard", None),
        P("shard", None),
        P("shard"),
        P("shard"),
        P("shard", None),
        P("expert", None, "shard"),
        P("expert", "shard", None),
    )
    return jax.shard_map(body, mesh=mesh, in_specs=in_specs, out_specs=out_specs, check_vma=False)
```

```python
import functools

import jax
import jax.numpy as jnp
from jax import lax
from jax.experimental import pallas as pl
from jax.experimental.pallas import tpu as pltpu
from jax.sharding import PartitionSpec as P

norm_eps = 1e-06
f32 = jnp.float32
bf16 = jnp.bfloat16
lane = 128


def inverse_rms(values):
    return lax.rsqrt(jnp.mean(values * values, axis=-1, keepdims=True) + norm_eps)


def dot(a, b, ca=1, cb=0):
    return lax.dot_general(a, b, (((ca,), (cb,)), ((), ())), preferred_element_type=f32)


def split_two(v):
    high = v.astype(bf16)
    return high, (v - high.astype(f32)).astype(bf16)


def local_call(kernel, outs, args, scalars=0, views=None, flops=0, moved=0):
    specs = [pl.BlockSpec(memory_space=pltpu.SMEM)] * scalars
    specs += [pl.BlockSpec(memory_space=pltpu.VMEM)] * (len(args) - scalars)
    for n, (shape, where) in (views or {}).items():
        specs[n] = pl.BlockSpec(shape, lambda i, where=where: where)
    return pl.pallas_call(
        kernel,
        out_shape=[jax.ShapeDtypeStruct(shape, kind) for shape, kind in outs],
        grid=(1,),
        in_specs=specs,
        out_specs=[pl.BlockSpec(memory_space=pltpu.VMEM)] * len(outs),
        compiler_params=pltpu.CompilerParams(vmem_limit_bytes=48 << 20),
        cost_estimate=pl.CostEstimate(flops=flops, bytes_accessed=moved, transcendentals=0),
    )(*args)


def join_blocks(e, s, parts, full_ref):
    count = 2 * parts[0].shape[1]
    rows, cols = parts[0].shape[2], parts[0].shape[3]
    for n, ref in enumerate(parts):
        bits = ((2, 4), (4, 2))[n // 2]
        for i in range(ref.shape[0]):
            differ = (i & 1) * bits[0] + (i >> 1) * bits[1] + n % 2
            col = pl.multiple_of(((e & 7) ^ differ) * cols, lane)
            for q in range(count // 2):
                source = lax.rem(s - (q + (n // 2) * (count // 2)) + count, count)
                row = pl.multiple_of(source * rows, 16)
                full_ref[pl.ds(row, rows), pl.ds(col, cols)] = ref[i, q]


def head_mask(shape, h, head_dim):
    return lax.broadcasted_iota(jnp.int32, shape, 1) // head_dim == h


def attend_kernel(
    ids_ref, tok_ref, gain_ref, gain_two_ref, a_ref, a_other_ref, b_ref, b_other_ref, bias_ref,
    proj_ref, probs_ref, mixed_ref, res_ref, ffn_ref, full_ref,
):
    join_blocks(ids_ref[0], ids_ref[1], (a_ref, a_other_ref, b_ref, b_other_ref), full_ref)
    length, width = tok_ref.shape
    heads = bias_ref.shape[0]
    head_dim = width // heads
    pack = lane // head_dim
    x = tok_ref[...].astype(f32)
    low = (x * inverse_rms(x) * gain_ref[...]).astype(bf16)
    step = width // 2
    for c in range(6):
        cols = slice(c * step, (c + 1) * step)
        proj_ref[:, cols] = dot(low, full_ref[:, cols]).astype(bf16)
    for g in range(heads // pack):
        q = proj_ref[:, g * lane : (g + 1) * lane]
        k = proj_ref[:, width + g * lane : width + (g + 1) * lane]
        v = proj_ref[:, 2 * width + g * lane : 2 * width + (g + 1) * lane]
        total = jnp.zeros((length, lane), f32)
        for h in range(pack):
            keep = head_mask((length, lane), h, head_dim)
            s = dot(q, jnp.where(keep, k, jnp.zeros_like(k)), 1, 1) * 0.125 + bias_ref[g * pack + h]
            e = jnp.exp(s - jnp.max(s, axis=-1, keepdims=True))
            p = e / jnp.sum(e, axis=-1, keepdims=True)
            probs_ref[g * pack + h] = p
            total = total + dot(p.astype(bf16), jnp.where(keep, v, jnp.zeros_like(v)))
        mixed_ref[:, g * lane : (g + 1) * lane] = total.astype(bf16)
    res = x + dot(mixed_ref[...], full_ref[:, 3 * width :])
    res_ref[...] = res
    ffn_ref[...] = (res * inverse_rms(res) * gain_two_ref[...]).astype(bf16)


def expert_kernel(
    ids_ref, rows_ref, g_ref, wi_ref, wd_ref, router_ref,
    send_ref, y_ref, rows_out, hidden_out, dpre_out, dy_out,
):
    j = pl.program_id(0)
    count, per, width = rows_ref.shape
    total = count * per
    experts = router_ref.shape[1]
    x = rows_ref[...].reshape(total, width)
    rows_out[0] = x
    g = g_ref[:, :, :width].reshape(total, width).astype(f32)
    tags = g_ref[:, :, width:].reshape(total, lane).astype(f32)
    other, choice = tags[:, 0:1], tags[:, 1:2]
    logits = dot(x, router_ref[...])
    ids = lax.broadcasted_iota(jnp.int32, (total, experts), 1)
    own_logit = jnp.sum(jnp.where(ids == ids_ref[0] + j, logits, 0.0), -1, keepdims=True)
    other_logit = jnp.sum(jnp.where(ids.astype(f32) == other, logits, 0.0), -1, keepdims=True)
    gate = 1.0 / (1.0 + jnp.exp(other_logit - own_logit))
    d_y = (gate * g).astype(bf16)
    dy_out[0] = d_y
    pre = dot(x, wi_ref[0])
    square = pre * pre
    tanh = jnp.tanh(0.7978845608028654 * pre * (1.0 + 0.044715 * square))
    hidden = (0.5 * pre * (1.0 + tanh)).astype(bf16)
    hidden_out[0] = hidden
    slope = 0.5 * (1.0 + tanh) + 0.5 * pre * (1.0 - tanh * tanh) * (
        0.7978845608028654 * (1.0 + 3.0 * 0.044715 * square)
    )
    d_pre = (dot(d_y, wd_ref[0], 1, 1) * slope).astype(bf16)
    dpre_out[0] = d_pre
    at = pl.multiple_of(j * per, 16)
    d_rows = dot(d_pre, wi_ref[0], 1, 1).astype(bf16)
    send_ref[:, pl.ds(at, per), :width] = d_rows.reshape(count, per, width)
    y = dot(hidden, wd_ref[0])
    y_ref[:, pl.ds(at, per), :] = (gate * y).astype(bf16).reshape(count, per, width)
    d_gate = jnp.sum(g * y, axis=-1, keepdims=True)
    high = d_gate.astype(bf16).astype(f32)
    cols = lax.broadcasted_iota(jnp.int32, (total, lane), 1).astype(f32)
    tail = jnp.where(cols == choice, high, jnp.where(cols == choice + 2.0, d_gate - high, 0.0))
    send_ref[:, pl.ds(at, per), width:] = tail.astype(bf16).reshape(count, per, lane)


def collect_kernel(back_ref, hot_ref, own_ref, *pay_refs):
    length = own_ref.shape[0]
    rows = back_ref[...].reshape(-1, back_ref.shape[2])
    for k in range(len(pay_refs) + 1):
        got = dot(hot_ref[k * length : (k + 1) * length, :], rows)
        if k == 0:
            own_ref[...] = got
        else:
            pay_refs[k - 1][...] = got.astype(bf16)


def backward_kernel(count, *refs):
    own_ref = refs[0]
    got_refs = refs[1 : 1 + count]
    (
        ffn_ref, res_ref, cot_ref, router_ref, routes_ref, gain_ref, full_ref, proj_ref, probs_ref,
        wide_ref, dres_ref, dlog_ref, gain_grad_ref, ds_ref, dproj_ref,
    ) = refs[1 + count :]
    length, width = ffn_ref.shape
    heads = probs_ref.shape[0]
    head_dim = width // heads
    pack = lane // head_dim
    experts = router_ref.shape[1]
    d = own_ref[...]
    for ref in got_refs:
        d = d + ref[...].astype(f32)
    tail = d[:, width:]
    d = d[:, :width]
    dg = [tail[:, i : i + 1] + tail[:, i + 2 : i + 3] for i in range(2)]
    logits = dot(ffn_ref[...], router_ref[...])
    e = jnp.exp(logits - jnp.max(logits, axis=-1, keepdims=True))
    router = e / jnp.sum(e, axis=-1, keepdims=True)
    ids = lax.broadcasted_iota(jnp.int32, (length, experts), 1)
    hots = [ids == routes_ref[:, i : i + 1] for i in range(2)]
    picked = [jnp.sum(jnp.where(h, router, 0.0), -1, keepdims=True) for h in hots]
    both = picked[0] + picked[1]
    mean = (dg[0] * picked[0] + dg[1] * picked[1]) / (both * both)
    d_router = sum(jnp.where(h, v / both - mean, 0.0) for h, v in zip(hots, dg))
    d_logits = router * (d_router - jnp.sum(router * d_router, -1, keepdims=True))
    d_logits = d_logits.astype(bf16)
    dlog_ref[...] = d_logits
    d_ffn = d + dot(d_logits, router_ref[...], 1, 1)
    res = res_ref[...]
    inv = inverse_rms(res)
    normed = res * inv
    gain_grad_ref[...] = jnp.sum(d_ffn * normed, axis=0, keepdims=True)
    d_norm = d_ffn * gain_ref[...]
    d_res = cot_ref[...].astype(f32) + inv * (
        d_norm - normed * jnp.mean(d_norm * normed, axis=-1, keepdims=True)
    )
    dres_ref[...] = d_res
    d_branch = d_res.astype(bf16)
    d_heads = dot(d_branch, full_ref[...], 1, 1).astype(bf16)
    for g in range(heads // pack):
        q = proj_ref[:, g * lane : (g + 1) * lane]
        k = proj_ref[:, width + g * lane : width + (g + 1) * lane]
        v = proj_ref[:, 2 * width + g * lane : 2 * width + (g + 1) * lane]
        dh = d_heads[:, g * lane : (g + 1) * lane]
        zero = jnp.zeros_like(q)
        sums = [jnp.zeros((length, lane), f32) for _ in range(3)]
        for h in range(pack):
            keep = head_mask((length, lane), h, head_dim)
            p = probs_ref[g * pack + h]
            dh_one = jnp.where(keep, dh, zero)
            d_probs = dot(dh_one, v, 1, 1)
            ds = p * (d_probs - jnp.sum(p * d_probs, axis=-1, keepdims=True))
            ds = ds.astype(bf16)
            ds_ref[g * pack + h] = ds
            sums[0] = sums[0] + dot(ds, jnp.where(keep, k, zero))
            sums[1] = sums[1] + dot(ds, jnp.where(keep, q, zero), 0, 0)
            sums[2] = sums[2] + dot(p.astype(bf16), dh_one, 0, 0)
        for i, scale in enumerate((0.125, 0.125, 1.0)):
            dproj_ref[:, i * width + g * lane : i * width + (g + 1) * lane] = (sums[i] * scale).astype(bf16)
    columns = wide_ref.shape[2]
    split = 3 * width // columns
    for b in range(wide_ref.shape[0]):
        if b < split:
            wide_ref[b] = dproj_ref[:, b * columns : (b + 1) * columns]
        else:
            wide_ref[b] = d_branch[:, (b - split) * columns : (b - split + 1) * columns]


def unpack_kernel(ids_ref, *refs):
    whole_refs, (qkv_ref, out_ref, small_ref) = refs[:-3], refs[-3:]
    part, width = out_ref.shape
    cols = small_ref.shape[1]
    split = 3 * width // cols
    pair = len(whole_refs)
    total = jnp.zeros(small_ref.shape, f32)
    for n, ref in enumerate(whole_refs):
        for i in range(ref.shape[0]):
            got = ref[i, :part, :].astype(f32)
            total = total + ref[i, part:, :].astype(f32)
            if pair * i < split:
                target, first = qkv_ref, pair * i
            else:
                target, first = out_ref, pair * i - split
            if pair == 1:
                target[:, first * cols : (first + 1) * cols] = got
            else:
                at = pl.multiple_of((first + ((ids_ref[0] & 1) ^ n)) * cols, lane)
                target[:, pl.ds(at, cols)] = got
    small_ref[...] = total


def tokens_kernel(dproj_ref, full_ref, tok_ref, gain_ref, dres_ref, out_ref, gain_grad_ref):
    d_in = dot(dproj_ref[...], full_ref[...], 1, 1)
    x = tok_ref[...].astype(f32)
    inv = inverse_rms(x)
    normed = x * inv
    gain_grad_ref[...] = jnp.sum(d_in * normed, axis=0, keepdims=True)
    d_norm = d_in * gain_ref[...]
    out_ref[...] = dres_ref[...] + inv * (
        d_norm - normed * jnp.mean(d_norm * normed, axis=-1, keepdims=True)
    )


def body(
    tokens,
    w_qkv,
    w_out,
    w_router,
    gain_attn,
    gain_ffn,
    bias_table,
    w_in,
    w_down,
    routes,
    slots,
    bucket_ids,
    cotangent,
):
    length, width = tokens.shape
    ne = lax.axis_size("expert")
    ns = lax.axis_size("shard")
    me_e = lax.axis_index("expert")
    me_s = lax.axis_index("shard")
    place_ids = jnp.stack([me_e, me_s]).astype(jnp.int32)
    exp_dev = w_in.shape[0]
    hidden_units = w_in.shape[2]
    experts = exp_dev * ne
    cap = 3 * length // experts
    per = ns * cap
    block = exp_dev * per
    total_rows = ne * block
    group_rows = ne * per
    heads = bias_table.shape[1]
    buckets = bias_table.shape[0] * ns
    part = width // ns

    def from_shift(v, k):
        return lax.ppermute(v, "shard", [(i, (i + k) % ns) for i in range(ns)])

    def to_shift(v, k):
        return lax.ppermute(v, "shard", [(i, (i - k) % ns) for i in range(ns)])

    def plane(v):
        return lax.all_to_all(v, "expert", split_axis=0, concat_axis=0, tiled=True)

    def across(v, bit):
        return lax.ppermute(v, "expert", [(i, i ^ bit) for i in range(ne)])

    cols = width // 2
    mine = me_e & 7
    weight = jnp.where(
        mine < 6,
        lax.dynamic_slice_in_dim(w_qkv, jnp.minimum(mine, 5) * cols, cols, 1),
        lax.dynamic_slice_in_dim(w_out, (jnp.maximum(mine, 6) - 6) * cols, cols, 1),
    )
    line = [weight] + [from_shift(weight, k) for k in range(1, ns)]

    plane_tokens = lax.all_gather(tokens, "expert", axis=0, tiled=True)

    smalls = (w_router, gain_attn, gain_ffn, bias_table, routes.astype(bf16), slots.astype(bf16))
    small = jnp.concatenate([v.reshape(-1) for v in smalls])
    small_rows = -(-small.size // width)
    small_rows += -small_rows % 16
    small = jnp.pad(small, (0, small_rows * width - small.size)).reshape(small_rows, width)
    packed = jnp.concatenate([cotangent, small], axis=0)
    packed, line = lax.optimization_barrier((packed, line))
    pieces = []
    for half, bits in ((line[: ns // 2], (2, 4)), (line[ns // 2 :], (4, 2))):
        held = jnp.stack(half)[None]
        for bit in bits:
            held = jnp.concatenate([held, across(held, bit)], axis=0)
        pieces += [held, across(held, 1)]
    line = [packed] + [from_shift(packed, k) for k in range(1, ns)]
    line_small = jnp.stack([v[length:].reshape(-1) for v in line])
    line_g = jnp.concatenate([v[:length] for v in line], axis=0)
    order = lax.rem(me_s - jnp.arange(ns, dtype=jnp.int32) + ns, ns)
    in_order = jnp.take(line_small, order, axis=0)

    cuts = []
    at = 0
    for v in smalls:
        cuts.append((at, at + v.size))
        at += v.size

    def cut(v, i):
        return v[:, cuts[i][0] : cuts[i][1]]

    full_router = cut(in_order, 0).reshape(width, experts)
    gain_one = cut(in_order, 1).reshape(1, width).astype(f32)
    gain_two = cut(in_order, 2).reshape(1, width).astype(f32)
    table = cut(in_order, 3).reshape(buckets, heads)
    line_routes = cut(line_small, 4).reshape(ns * length, 2)
    line_slots = cut(line_small, 5).reshape(ns * length, 2).astype(jnp.int32)
    place = (
        line_routes.astype(jnp.int32) * per + jnp.repeat(order, length)[:, None] * cap + line_slots
    )
    row_ids = jnp.arange(total_rows, dtype=jnp.int32)
    hot0 = (row_ids[:, None] == place[None, :, 0]).astype(bf16)
    hot1 = (row_ids[:, None] == place[None, :, 1]).astype(bf16)
    hot = hot0 + hot1
    hot_back = (
        (row_ids[None, :] == place[:, 0:1]) | (row_ids[None, :] == place[:, 1:2])
    ).astype(bf16)

    def tagged(i):
        tag = jnp.concatenate([line_routes[:, 1 - i : 2 - i], jnp.full((ns * length, 1), i, bf16)], 1)
        return jnp.concatenate([line_g, jnp.pad(tag, ((0, 0), (0, lane - 2)))], axis=1)

    g_rows = (dot(hot0, tagged(0)) + dot(hot1, tagged(1))).astype(bf16)
    g_rows = g_rows.reshape(ne, block, width + lane)

    causal = jnp.arange(length)[:, None] >= jnp.arange(length)[None, :]
    bucket_hot = (
        jnp.arange(buckets, dtype=jnp.int32)[:, None] == bucket_ids.reshape(1, -1)
    ).astype(bf16)
    pair_bias = dot(table, bucket_hot, 0, 0).reshape(heads, length, length)
    pair_bias = jnp.where(causal[None], pair_bias, -1e30)
    pair_bias, g_rows = lax.optimization_barrier((pair_bias, g_rows))
    g_arrived = plane(g_rows)
    proj, probs, mixed_low, residual, ffn_in, full = local_call(
        attend_kernel,
        [
            ((length, 3 * width), bf16),
            ((heads, length, length), f32),
            ((length, width), bf16),
            ((length, width), f32),
            ((length, width), bf16),
            ((width, 4 * width), bf16),
        ],
        [place_ids, tokens, gain_one, gain_two, *pieces, pair_bias],
        scalars=1,
    )

    split_e = 3 * ne // 4
    mixed_low, plane_tokens = lax.optimization_barrier((mixed_low, plane_tokens))
    plane_mixed = lax.all_gather(mixed_low, "expert", axis=0, tiled=True)
    line_ffn = jnp.concatenate([ffn_in] + [from_shift(ffn_in, k) for k in range(1, ns)], axis=0)
    line_ffn, g_arrived = lax.optimization_barrier((line_ffn, g_arrived))
    arrived = plane(dot(hot, line_ffn).astype(bf16).reshape(ne, block, width))

    wide_width = width + lane
    first_id = (me_e * exp_dev).astype(jnp.int32).reshape(1)
    send, y_send, rows, hidden, d_pre, d_y = pl.pallas_call(
        expert_kernel,
        out_shape=[
            jax.ShapeDtypeStruct((ne, block, wide_width), bf16),
            jax.ShapeDtypeStruct((ne, block, width), bf16),
            jax.ShapeDtypeStruct((exp_dev, group_rows, width), bf16),
            jax.ShapeDtypeStruct((exp_dev, group_rows, hidden_units), bf16),
            jax.ShapeDtypeStruct((exp_dev, group_rows, hidden_units), bf16),
            jax.ShapeDtypeStruct((exp_dev, group_rows, width), bf16),
        ],
        grid=(exp_dev,),
        in_specs=[
            pl.BlockSpec(memory_space=pltpu.SMEM),
            pl.BlockSpec((ne, per, width), lambda j: (0, j, 0)),
            pl.BlockSpec((ne, per, wide_width), lambda j: (0, j, 0)),
            pl.BlockSpec((1, width, hidden_units), lambda j: (j, 0, 0)),
            pl.BlockSpec((1, hidden_units, width), lambda j: (j, 0, 0)),
            pl.BlockSpec((width, experts), lambda j: (0, 0)),
        ],
        out_specs=[
            pl.BlockSpec((ne, block, wide_width), lambda j: (0, 0, 0)),
            pl.BlockSpec((ne, block, width), lambda j: (0, 0, 0)),
            pl.BlockSpec((1, group_rows, width), lambda j: (j, 0, 0)),
            pl.BlockSpec((1, group_rows, hidden_units), lambda j: (j, 0, 0)),
            pl.BlockSpec((1, group_rows, hidden_units), lambda j: (j, 0, 0)),
            pl.BlockSpec((1, group_rows, width), lambda j: (j, 0, 0)),
        ],
        compiler_params=pltpu.CompilerParams(vmem_limit_bytes=56 << 20),
        cost_estimate=pl.CostEstimate(
            flops=8 * exp_dev * group_rows * width * hidden_units,
            bytes_accessed=16 * exp_dev * group_rows * width,
            transcendentals=0,
        ),
    )(first_id, arrived, g_arrived, w_in, w_down, full_router)
    d_back = plane(send)
    grad_w_down = jnp.einsum("jrf,jrd->jfd", hidden, d_y, preferred_element_type=f32)
    grad_w_in = jnp.einsum("jrd,jrf->jdf", rows, d_pre, preferred_element_type=f32)
    d_back, grad_w_down, grad_w_in = lax.optimization_barrier((d_back, grad_w_down, grad_w_in))

    own_d, *pays = local_call(
        collect_kernel,
        [((length, wide_width), f32)] + [((length, wide_width), bf16)] * (ns - 1),
        [d_back, hot_back],
        flops=2 * ns * length * total_rows * wide_width,
        moved=2 * total_rows * wide_width,
    )
    got = [to_shift(v, k + 1) for k, v in enumerate(pays)]
    pays, y_send = lax.optimization_barrier((pays, y_send))
    y_back = plane(y_send)
    plane_float = plane_tokens.astype(f32)
    plane_attn = (plane_float * inverse_rms(plane_float) * gain_one).astype(bf16)
    factors = jnp.where(me_e < split_e, plane_attn, plane_mixed)
    got, factors = lax.optimization_barrier((got, factors))
    columns = 4 * width // ne
    wide, d_residual, d_logits, gain_two_grad, d_scores, d_proj = local_call(
        functools.partial(backward_kernel, ns - 1),
        [
            ((ne, length, columns), bf16),
            ((length, width), f32),
            ((length, experts), bf16),
            ((1, width), f32),
            ((heads, length, length), bf16),
            ((length, 3 * width), bf16),
        ],
        [own_d, *got, ffn_in, residual, cotangent, full_router, routes, gain_two, full, proj, probs],
        views={ns + 6: ((width, width), (0, 3))},
        flops=2 * length * width * width + 10 * heads * length * length * lane,
        moved=2 * width * width + 8 * heads * length * length,
    )
    wide = plane(wide)
    grad_tokens, gain_one_grad = local_call(
        tokens_kernel,
        [((length, width), f32), ((1, width), f32)],
        [d_proj, full, tokens, gain_one, d_residual],
        views={1: ((width, 3 * width), (0, 0))},
    )
    grad_router = dot(ffn_in, d_logits, 0, 0)
    grad_table = dot(bucket_hot, d_scores.reshape(heads, length * length), 1, 1)

    small_parts = [
        grad_router.reshape(ns, -1),
        gain_one_grad.reshape(ns, -1),
        gain_two_grad.reshape(ns, -1),
        grad_table.reshape(ns, -1),
    ]
    sizes = [v.shape[1] for v in small_parts]
    small = jnp.concatenate(small_parts, axis=1).astype(bf16)
    each = small.shape[1]
    srows = -(-each // columns)
    srows += -srows % 16
    room = srows * columns
    small = jnp.pad(small, ((0, 0), (0, room - each))).reshape(ns, srows, columns)
    product = dot(factors, wide.reshape(ne * length, columns), 0, 0).astype(bf16)
    product = jnp.concatenate([product.reshape(ns, part, columns), small], axis=1)
    product, y_back = lax.optimization_barrier((product, y_back))
    y_line = dot(hot_back, y_back.reshape(total_rows, width))
    y_own = residual + y_line[:length]
    y_low = y_line[length:].astype(bf16)
    share = lax.dynamic_index_in_dim(product, me_s, 0, keepdims=False).astype(f32)
    for k in range(1, ns):
        piece = lax.dynamic_index_in_dim(product, lax.rem(me_s - k + ns, ns), 0, keepdims=False)
        share = share + to_shift(piece, k).astype(f32)
    share = share.astype(bf16)
    share, y_low, y_own = lax.optimization_barrier((share, y_low, y_own))
    y_got = [to_shift(y_low[(k - 1) * length : k * length], k) for k in range(1, ns)]
    by_core = columns % lane == 0
    if by_core:
        spread = jnp.broadcast_to(share[None], (ne // 2,) + share.shape)
        same = [list(range(c, ne, 2)) for c in range(2)]
        whole = lax.all_to_all(
            spread, "expert", split_axis=0, concat_axis=0, axis_index_groups=same, tiled=True
        )
        whole = [whole, across(whole, 1)]
    else:
        whole = [plane(jnp.broadcast_to(share[None], (ne,) + share.shape))]
    out_qkv, out_out, small = local_call(
        unpack_kernel,
        [((part, 3 * width), f32), ((part, width), f32), ((srows, columns), f32)],
        [place_ids, *whole],
        scalars=1,
        moved=6 * ne * (part + srows) * columns,
    )
    small = small.reshape(-1)
    smalls = []
    at = 0
    for size in sizes:
        smalls.append(small[at : at + size])
        at += size

    for v in y_got:
        y_own = y_own + v.astype(f32)
    return (
        y_own.astype(bf16),
        grad_tokens,
        out_qkv,
        out_out,
        smalls[0].reshape(part, experts),
        smalls[1],
        smalls[2],
        smalls[3].reshape(buckets // ns, heads),
        grad_w_in,
        grad_w_down,
    )


def solution(mesh):
    in_specs = (
        P(("expert", "shard"), None),
        P("shard", None),
        P("shard", None),
        P("shard", None),
        P("shard"),
        P("shard"),
        P("shard", None),
        P("expert", None, "shard"),
        P("expert", "shard", None),
        P(("expert", "shard"), None),
        P(("expert", "shard"), None),
        P(),
        P(("expert", "shard"), None),
    )
    out_specs = (
        P(("expert", "shard"), None),
        P(("expert", "shard"), None),
        P("shard", None),
        P("shard", None),
        P("shard", None),
        P("shard"),
        P("shard"),
        P("shard", None),
        P("expert", None, "shard"),
        P("expert", "shard", None),
    )
    return jax.shard_map(body, mesh=mesh, in_specs=in_specs, out_specs=out_specs, check_vma=False)
```

```python
import functools

import jax
import jax.numpy as jnp
from jax import lax
from jax.experimental import pallas as pl
from jax.experimental.pallas import tpu as pltpu
from jax.sharding import PartitionSpec as P

norm_eps = 1e-06
f32 = jnp.float32
bf16 = jnp.bfloat16
lane = 128


def inverse_rms(values):
    return lax.rsqrt(jnp.mean(values * values, axis=-1, keepdims=True) + norm_eps)


def dot(a, b, ca=1, cb=0):
    return lax.dot_general(a, b, (((ca,), (cb,)), ((), ())), preferred_element_type=f32)


def split_two(v):
    high = v.astype(bf16)
    return high, (v - high.astype(f32)).astype(bf16)


def local_call(kernel, outs, args, scalars=0, views=None, scratch=(), flops=0, moved=0):
    def block(shape, where=None):
        where = where or (0,) * len(shape)
        return pl.BlockSpec(shape, lambda i: where)

    specs = [pl.BlockSpec(memory_space=pltpu.SMEM)] * scalars
    specs += [block(v.shape) for v in args[scalars:]]
    for n, (shape, where) in (views or {}).items():
        specs[n] = block(shape, where)
    return pl.pallas_call(
        kernel,
        out_shape=[jax.ShapeDtypeStruct(shape, kind) for shape, kind in outs],
        grid=(1,),
        in_specs=specs,
        out_specs=[block(shape) for shape, _ in outs],
        scratch_shapes=list(scratch),
        compiler_params=pltpu.CompilerParams(vmem_limit_bytes=56 << 20),
        cost_estimate=pl.CostEstimate(flops=flops, bytes_accessed=moved, transcendentals=0),
    )(*args)


def join_blocks(e, s, parts, full_ref):
    count = 2 * parts[0].shape[1]
    rows, cols = parts[0].shape[2], parts[0].shape[3]
    for n, ref in enumerate(parts):
        bits = ((2, 4), (4, 2))[n // 2]
        for i in range(ref.shape[0]):
            differ = (i & 1) * bits[0] + (i >> 1) * bits[1] + n % 2
            col = pl.multiple_of(((e & 7) ^ differ) * cols, lane)
            for q in range(count // 2):
                source = lax.rem(s - (q + (n // 2) * (count // 2)) + count, count)
                row = pl.multiple_of(source * rows, 16)
                full_ref[pl.ds(row, rows), pl.ds(col, cols)] = ref[i, q]


def head_mask(shape, h, head_dim):
    return lax.broadcasted_iota(jnp.int32, shape, 1) // head_dim == h


def attend_kernel(
    ids_ref, tok_ref, gain_ref, gain_two_ref, a_ref, a_other_ref, b_ref, b_other_ref, bias_ref,
    attn_ref, proj_ref, probs_ref, mixed_ref, res_ref, ffn_ref, full_ref,
):
    join_blocks(ids_ref[0], ids_ref[1], (a_ref, a_other_ref, b_ref, b_other_ref), full_ref)
    length, width = tok_ref.shape
    heads = bias_ref.shape[0]
    head_dim = width // heads
    pack = lane // head_dim
    x = tok_ref[...].astype(f32)
    low = (x * inverse_rms(x) * gain_ref[...]).astype(bf16)
    attn_ref[...] = low
    step = width // 2
    for c in range(6):
        cols = slice(c * step, (c + 1) * step)
        proj_ref[:, cols] = dot(low, full_ref[:, cols]).astype(bf16)
    for g in range(heads // pack):
        q = proj_ref[:, g * lane : (g + 1) * lane]
        k = proj_ref[:, width + g * lane : width + (g + 1) * lane]
        v = proj_ref[:, 2 * width + g * lane : 2 * width + (g + 1) * lane]
        total = jnp.zeros((length, lane), f32)
        for h in range(pack):
            keep = head_mask((length, lane), h, head_dim)
            s = dot(q, jnp.where(keep, k, jnp.zeros_like(k)), 1, 1) * 0.125 + bias_ref[g * pack + h]
            e = jnp.exp(s - jnp.max(s, axis=-1, keepdims=True))
            p = e / jnp.sum(e, axis=-1, keepdims=True)
            probs_ref[g * pack + h] = p
            total = total + dot(p.astype(bf16), jnp.where(keep, v, jnp.zeros_like(v)))
        mixed_ref[:, g * lane : (g + 1) * lane] = total.astype(bf16)
    res = x + dot(mixed_ref[...], full_ref[:, 3 * width :])
    res_ref[...] = res
    ffn_ref[...] = (res * inverse_rms(res) * gain_two_ref[...]).astype(bf16)


def expert_kernel(
    ids_ref, rows_ref, g_ref, wi_ref, wd_ref, router_ref,
    send_ref, y_ref, rows_out, hidden_out, dpre_out, dy_out,
):
    j = pl.program_id(0)
    count, per, width = rows_ref.shape
    total = count * per
    experts = router_ref.shape[1]
    x = rows_ref[...].reshape(total, width)
    rows_out[0] = x
    g = g_ref[:, :, :width].reshape(total, width).astype(f32)
    tags = g_ref[:, :, width:].reshape(total, lane).astype(f32)
    other, choice = tags[:, 0:1], tags[:, 1:2]
    logits = dot(x, router_ref[...])
    ids = lax.broadcasted_iota(jnp.int32, (total, experts), 1)
    own_logit = jnp.sum(jnp.where(ids == ids_ref[0] + j, logits, 0.0), -1, keepdims=True)
    other_logit = jnp.sum(jnp.where(ids.astype(f32) == other, logits, 0.0), -1, keepdims=True)
    gate = 1.0 / (1.0 + jnp.exp(other_logit - own_logit))
    d_y = (gate * g).astype(bf16)
    dy_out[0] = d_y
    pre = dot(x, wi_ref[0])
    square = pre * pre
    tanh = jnp.tanh(0.7978845608028654 * pre * (1.0 + 0.044715 * square))
    hidden = (0.5 * pre * (1.0 + tanh)).astype(bf16)
    hidden_out[0] = hidden
    slope = 0.5 * (1.0 + tanh) + 0.5 * pre * (1.0 - tanh * tanh) * (
        0.7978845608028654 * (1.0 + 3.0 * 0.044715 * square)
    )
    d_pre = (dot(d_y, wd_ref[0], 1, 1) * slope).astype(bf16)
    dpre_out[0] = d_pre
    at = pl.multiple_of(j * per, 16)
    d_rows = dot(d_pre, wi_ref[0], 1, 1).astype(bf16)
    send_ref[:, pl.ds(at, per), :width] = d_rows.reshape(count, per, width)
    y = dot(hidden, wd_ref[0])
    y_ref[:, pl.ds(at, per), :] = (gate * y).astype(bf16).reshape(count, per, width)
    d_gate = jnp.sum(g * y, axis=-1, keepdims=True)
    high = d_gate.astype(bf16).astype(f32)
    cols = lax.broadcasted_iota(jnp.int32, (total, lane), 1).astype(f32)
    tail = jnp.where(cols == choice, high, jnp.where(cols == choice + 2.0, d_gate - high, 0.0))
    send_ref[:, pl.ds(at, per), width:] = tail.astype(bf16).reshape(count, per, lane)


def collect_kernel(back_ref, hot_ref, own_ref, *pay_refs):
    length = own_ref.shape[0]
    rows = back_ref[...].reshape(-1, back_ref.shape[2])
    for k in range(len(pay_refs) + 1):
        got = dot(hot_ref[k * length : (k + 1) * length, :], rows)
        if k == 0:
            own_ref[...] = got
        else:
            pay_refs[k - 1][...] = got.astype(bf16)


def backward_kernel(count, *refs):
    own_ref = refs[0]
    got_refs = refs[1 : 1 + count]
    (
        ffn_ref, res_ref, cot_ref, router_ref, routes_ref, gain_ref, full_ref, proj_ref, probs_ref,
        wide_ref, dres_ref, dlog_ref, gain_grad_ref, ds_ref, dproj_ref,
    ) = refs[1 + count :]
    length, width = ffn_ref.shape
    heads = probs_ref.shape[0]
    head_dim = width // heads
    pack = lane // head_dim
    experts = router_ref.shape[1]
    d = own_ref[...]
    for ref in got_refs:
        d = d + ref[...].astype(f32)
    tail = d[:, width:]
    d = d[:, :width]
    dg = [tail[:, i : i + 1] + tail[:, i + 2 : i + 3] for i in range(2)]
    logits = dot(ffn_ref[...], router_ref[...])
    e = jnp.exp(logits - jnp.max(logits, axis=-1, keepdims=True))
    router = e / jnp.sum(e, axis=-1, keepdims=True)
    ids = lax.broadcasted_iota(jnp.int32, (length, experts), 1)
    hots = [ids == routes_ref[:, i : i + 1] for i in range(2)]
    picked = [jnp.sum(jnp.where(h, router, 0.0), -1, keepdims=True) for h in hots]
    both = picked[0] + picked[1]
    mean = (dg[0] * picked[0] + dg[1] * picked[1]) / (both * both)
    d_router = sum(jnp.where(h, v / both - mean, 0.0) for h, v in zip(hots, dg))
    d_logits = router * (d_router - jnp.sum(router * d_router, -1, keepdims=True))
    d_logits = d_logits.astype(bf16)
    dlog_ref[...] = d_logits
    d_ffn = d + dot(d_logits, router_ref[...], 1, 1)
    res = res_ref[...]
    inv = inverse_rms(res)
    normed = res * inv
    gain_grad_ref[...] = jnp.sum(d_ffn * normed, axis=0, keepdims=True)
    d_norm = d_ffn * gain_ref[...]
    d_res = cot_ref[...].astype(f32) + inv * (
        d_norm - normed * jnp.mean(d_norm * normed, axis=-1, keepdims=True)
    )
    dres_ref[...] = d_res
    d_branch = d_res.astype(bf16)
    d_heads = dot(d_branch, full_ref[...], 1, 1).astype(bf16)
    for g in range(heads // pack):
        q = proj_ref[:, g * lane : (g + 1) * lane]
        k = proj_ref[:, width + g * lane : width + (g + 1) * lane]
        v = proj_ref[:, 2 * width + g * lane : 2 * width + (g + 1) * lane]
        dh = d_heads[:, g * lane : (g + 1) * lane]
        zero = jnp.zeros_like(q)
        sums = [jnp.zeros((length, lane), f32) for _ in range(3)]
        for h in range(pack):
            keep = head_mask((length, lane), h, head_dim)
            p = probs_ref[g * pack + h]
            dh_one = jnp.where(keep, dh, zero)
            d_probs = dot(dh_one, v, 1, 1)
            ds = p * (d_probs - jnp.sum(p * d_probs, axis=-1, keepdims=True))
            ds = ds.astype(bf16)
            ds_ref[g * pack + h] = ds
            sums[0] = sums[0] + dot(ds, jnp.where(keep, k, zero))
            sums[1] = sums[1] + dot(ds, jnp.where(keep, q, zero), 0, 0)
            sums[2] = sums[2] + dot(p.astype(bf16), dh_one, 0, 0)
        for i, scale in enumerate((0.125, 0.125, 1.0)):
            dproj_ref[:, i * width + g * lane : i * width + (g + 1) * lane] = (sums[i] * scale).astype(bf16)
    columns = wide_ref.shape[2]
    split = 3 * width // columns
    for b in range(wide_ref.shape[0]):
        if b < split:
            wide_ref[b] = dproj_ref[:, b * columns : (b + 1) * columns]
        else:
            wide_ref[b] = d_branch[:, (b - split) * columns : (b - split + 1) * columns]


def product_kernel(ids_ref, own_ref, other_ref, wide_ref, small_ref, share_ref, *refs):
    pay_refs, order_ref, total_ref = refs[:-2], refs[-2], refs[-1]
    pairs, length, width = own_ref.shape
    e, s = ids_ref[0], ids_ref[1]
    count, part = small_ref.shape[0], width // small_ref.shape[0]
    for n in range(2):
        for i in range(pairs):
            at = (n * pairs + i) * length
            order_ref[at : at + length, :] = wide_ref[e ^ (2 * i + n)]
    half = pairs * length
    total_ref[...] = dot(own_ref[...].reshape(half, width), order_ref[:half, :], 0, 0) + dot(
        other_ref[...].reshape(half, width), order_ref[half:, :], 0, 0
    )
    for k in range(count):
        target = lax.rem(s - k + count, count)
        rows = total_ref[pl.ds(pl.multiple_of(target * part, 16), part), :]
        ref = share_ref if k == 0 else pay_refs[k - 1]
        ref[:part, :] = rows.astype(ref.dtype)
        ref[part:, :] = small_ref[target].astype(ref.dtype)


def unpack_kernel(ids_ref, *refs):
    whole_refs, (qkv_ref, out_ref, small_ref) = refs[:-3], refs[-3:]
    part, width = out_ref.shape
    cols = small_ref.shape[1]
    split = 3 * width // cols
    pair = len(whole_refs)
    total = jnp.zeros(small_ref.shape, f32)
    for n, ref in enumerate(whole_refs):
        for i in range(ref.shape[0]):
            got = ref[i, :part, :].astype(f32)
            total = total + ref[i, part:, :].astype(f32)
            if pair * i < split:
                target, first = qkv_ref, pair * i
            else:
                target, first = out_ref, pair * i - split
            if pair == 1:
                target[:, first * cols : (first + 1) * cols] = got
            else:
                at = pl.multiple_of((first + ((ids_ref[0] & 1) ^ n)) * cols, lane)
                target[:, pl.ds(at, cols)] = got
    small_ref[...] = total


def tokens_kernel(dproj_ref, full_ref, tok_ref, gain_ref, dres_ref, out_ref, gain_grad_ref):
    d_in = dot(dproj_ref[...], full_ref[...], 1, 1)
    x = tok_ref[...].astype(f32)
    inv = inverse_rms(x)
    normed = x * inv
    gain_grad_ref[...] = jnp.sum(d_in * normed, axis=0, keepdims=True)
    d_norm = d_in * gain_ref[...]
    out_ref[...] = dres_ref[...] + inv * (
        d_norm - normed * jnp.mean(d_norm * normed, axis=-1, keepdims=True)
    )


def body(
    tokens,
    w_qkv,
    w_out,
    w_router,
    gain_attn,
    gain_ffn,
    bias_table,
    w_in,
    w_down,
    routes,
    slots,
    bucket_ids,
    cotangent,
):
    length, width = tokens.shape
    ne = lax.axis_size("expert")
    ns = lax.axis_size("shard")
    me_e = lax.axis_index("expert")
    me_s = lax.axis_index("shard")
    place_ids = jnp.stack([me_e, me_s]).astype(jnp.int32)
    exp_dev = w_in.shape[0]
    hidden_units = w_in.shape[2]
    experts = exp_dev * ne
    cap = 3 * length // experts
    per = ns * cap
    block = exp_dev * per
    total_rows = ne * block
    group_rows = ne * per
    heads = bias_table.shape[1]
    buckets = bias_table.shape[0] * ns
    part = width // ns

    def from_shift(v, k):
        return lax.ppermute(v, "shard", [(i, (i + k) % ns) for i in range(ns)])

    def to_shift(v, k):
        return lax.ppermute(v, "shard", [(i, (i - k) % ns) for i in range(ns)])

    def plane(v):
        return lax.all_to_all(v, "expert", split_axis=0, concat_axis=0, tiled=True)

    def across(v, bit):
        return lax.ppermute(v, "expert", [(i, i ^ bit) for i in range(ne)])

    cols = width // 2
    mine = me_e & 7
    weight = jnp.where(
        mine < 6,
        lax.dynamic_slice_in_dim(w_qkv, jnp.minimum(mine, 5) * cols, cols, 1),
        lax.dynamic_slice_in_dim(w_out, (jnp.maximum(mine, 6) - 6) * cols, cols, 1),
    )
    line = [weight] + [from_shift(weight, k) for k in range(1, ns)]

    smalls = (w_router, gain_attn, gain_ffn, bias_table, routes.astype(bf16), slots.astype(bf16))
    small = jnp.concatenate([v.reshape(-1) for v in smalls])
    small_rows = -(-small.size // width)
    small_rows += -small_rows % 16
    small = jnp.pad(small, (0, small_rows * width - small.size)).reshape(small_rows, width)
    packed = jnp.concatenate([cotangent, small], axis=0)
    packed, line = lax.optimization_barrier((packed, line))
    halves = []
    for half, bits in ((line[: ns // 2], (2, 4)), (line[ns // 2 :], (4, 2))):
        held = jnp.stack(half)[None]
        for bit in bits:
            held = jnp.concatenate([held, across(held, bit)], axis=0)
        halves.append(held)
    line = [packed] + [from_shift(packed, k) for k in range(1, ns)]
    line_small = jnp.stack([v[length:].reshape(-1) for v in line])
    line_g = jnp.concatenate([v[:length] for v in line], axis=0)
    order = lax.rem(me_s - jnp.arange(ns, dtype=jnp.int32) + ns, ns)
    in_order = jnp.take(line_small, order, axis=0)

    cuts = []
    at = 0
    for v in smalls:
        cuts.append((at, at + v.size))
        at += v.size

    def cut(v, i):
        return v[:, cuts[i][0] : cuts[i][1]]

    full_router = cut(in_order, 0).reshape(width, experts)
    gain_one = cut(in_order, 1).reshape(1, width).astype(f32)
    gain_two = cut(in_order, 2).reshape(1, width).astype(f32)
    table = cut(in_order, 3).reshape(buckets, heads)
    line_routes = cut(line_small, 4).reshape(ns * length, 2)
    line_slots = cut(line_small, 5).reshape(ns * length, 2).astype(jnp.int32)
    place = (
        line_routes.astype(jnp.int32) * per + jnp.repeat(order, length)[:, None] * cap + line_slots
    )
    row_ids = jnp.arange(total_rows, dtype=jnp.int32)
    hot0 = (row_ids[:, None] == place[None, :, 0]).astype(bf16)
    hot1 = (row_ids[:, None] == place[None, :, 1]).astype(bf16)
    hot = hot0 + hot1
    hot_back = (
        (row_ids[None, :] == place[:, 0:1]) | (row_ids[None, :] == place[:, 1:2])
    ).astype(bf16)

    def tagged(i):
        tag = jnp.concatenate([line_routes[:, 1 - i : 2 - i], jnp.full((ns * length, 1), i, bf16)], 1)
        return jnp.concatenate([line_g, jnp.pad(tag, ((0, 0), (0, lane - 2)))], axis=1)

    g_rows = (dot(hot0, tagged(0)) + dot(hot1, tagged(1))).astype(bf16)
    g_rows = g_rows.reshape(ne, block, width + lane)

    causal = jnp.arange(length)[:, None] >= jnp.arange(length)[None, :]
    bucket_hot = (
        jnp.arange(buckets, dtype=jnp.int32)[:, None] == bucket_ids.reshape(1, -1)
    ).astype(bf16)
    pair_bias = dot(table, bucket_hot, 0, 0).reshape(heads, length, length)
    pair_bias = jnp.where(causal[None], pair_bias, -1e30)
    pair_bias, g_rows, halves = lax.optimization_barrier((pair_bias, g_rows, halves))
    g_arrived = plane(g_rows)
    pieces = [halves[0], across(halves[0], 1), halves[1], across(halves[1], 1)]
    attn_in, proj, probs, mixed_low, residual, ffn_in, full = local_call(
        attend_kernel,
        [
            ((length, width), bf16),
            ((length, 3 * width), bf16),
            ((heads, length, length), f32),
            ((length, width), bf16),
            ((length, width), f32),
            ((length, width), bf16),
            ((width, 4 * width), bf16),
        ],
        [place_ids, tokens, gain_one, gain_two, *pieces, pair_bias],
        scalars=1,
    )

    line_ffn = jnp.concatenate([ffn_in] + [from_shift(ffn_in, k) for k in range(1, ns)], axis=0)
    line_ffn, g_arrived = lax.optimization_barrier((line_ffn, g_arrived))
    arrived = plane(dot(hot, line_ffn).astype(bf16).reshape(ne, block, width))

    wide_width = width + lane
    first_id = (me_e * exp_dev).astype(jnp.int32).reshape(1)
    send, y_send, rows, hidden, d_pre, d_y = pl.pallas_call(
        expert_kernel,
        out_shape=[
            jax.ShapeDtypeStruct((ne, block, wide_width), bf16),
            jax.ShapeDtypeStruct((ne, block, width), bf16),
            jax.ShapeDtypeStruct((exp_dev, group_rows, width), bf16),
            jax.ShapeDtypeStruct((exp_dev, group_rows, hidden_units), bf16),
            jax.ShapeDtypeStruct((exp_dev, group_rows, hidden_units), bf16),
            jax.ShapeDtypeStruct((exp_dev, group_rows, width), bf16),
        ],
        grid=(exp_dev,),
        in_specs=[
            pl.BlockSpec(memory_space=pltpu.SMEM),
            pl.BlockSpec((ne, per, width), lambda j: (0, j, 0)),
            pl.BlockSpec((ne, per, wide_width), lambda j: (0, j, 0)),
            pl.BlockSpec((1, width, hidden_units), lambda j: (j, 0, 0)),
            pl.BlockSpec((1, hidden_units, width), lambda j: (j, 0, 0)),
            pl.BlockSpec((width, experts), lambda j: (0, 0)),
        ],
        out_specs=[
            pl.BlockSpec((ne, block, wide_width), lambda j: (0, 0, 0)),
            pl.BlockSpec((ne, block, width), lambda j: (0, 0, 0)),
            pl.BlockSpec((1, group_rows, width), lambda j: (j, 0, 0)),
            pl.BlockSpec((1, group_rows, hidden_units), lambda j: (j, 0, 0)),
            pl.BlockSpec((1, group_rows, hidden_units), lambda j: (j, 0, 0)),
            pl.BlockSpec((1, group_rows, width), lambda j: (j, 0, 0)),
        ],
        compiler_params=pltpu.CompilerParams(vmem_limit_bytes=56 << 20),
        cost_estimate=pl.CostEstimate(
            flops=8 * exp_dev * group_rows * width * hidden_units,
            bytes_accessed=16 * exp_dev * group_rows * width,
            transcendentals=0,
        ),
    )(first_id, arrived, g_arrived, w_in, w_down, full_router)
    d_back = plane(send)
    grad_w_down = jnp.einsum("jrf,jrd->jfd", hidden, d_y, preferred_element_type=f32)
    grad_w_in = jnp.einsum("jrd,jrf->jdf", rows, d_pre, preferred_element_type=f32)
    d_back, grad_w_down, grad_w_in = lax.optimization_barrier((d_back, grad_w_down, grad_w_in))

    own_d, *pays = local_call(
        collect_kernel,
        [((length, wide_width), f32)] + [((length, wide_width), bf16)] * (ns - 1),
        [d_back, hot_back],
        flops=2 * ns * length * total_rows * wide_width,
        moved=2 * total_rows * wide_width,
    )
    got = [to_shift(v, k + 1) for k, v in enumerate(pays)]
    pays, y_send, attn_in, mixed_low = lax.optimization_barrier((pays, y_send, attn_in, mixed_low))
    y_back = plane(y_send)
    split_e = 3 * ne // 4
    held = []
    for k in range(0, ne, 2):
        factor = jnp.where((me_e ^ k) < split_e, attn_in, mixed_low)
        held.append(across(factor, k) if k else factor)
    held = jnp.stack(held)
    held_other = across(held, 1)
    got, y_back, held, held_other = lax.optimization_barrier((got, y_back, held, held_other))
    columns = 4 * width // ne
    wide, d_residual, d_logits, gain_two_grad, d_scores, d_proj = local_call(
        functools.partial(backward_kernel, ns - 1),
        [
            ((ne, length, columns), bf16),
            ((length, width), f32),
            ((length, experts), bf16),
            ((1, width), f32),
            ((heads, length, length), bf16),
            ((length, 3 * width), bf16),
        ],
        [own_d, *got, ffn_in, residual, cotangent, full_router, routes, gain_two, full, proj, probs],
        views={ns + 6: ((width, width), (0, 3))},
        flops=2 * length * width * width + 10 * heads * length * length * lane,
        moved=2 * width * width + 8 * heads * length * length,
    )
    wide, y_back = lax.optimization_barrier((wide, y_back))
    wide = plane(wide)
    grad_tokens, gain_one_grad = local_call(
        tokens_kernel,
        [((length, width), f32), ((1, width), f32)],
        [d_proj, full, tokens, gain_one, d_residual],
        views={1: ((width, 3 * width), (0, 0))},
    )
    grad_router = dot(ffn_in, d_logits, 0, 0)
    grad_table = dot(bucket_hot, d_scores.reshape(heads, length * length), 1, 1)

    small_parts = [
        grad_router.reshape(ns, -1),
        gain_one_grad.reshape(ns, -1),
        gain_two_grad.reshape(ns, -1),
        grad_table.reshape(ns, -1),
    ]
    sizes = [v.shape[1] for v in small_parts]
    small = jnp.concatenate(small_parts, axis=1).astype(bf16)
    each = small.shape[1]
    srows = -(-each // columns)
    srows += -srows % 16
    room = srows * columns
    small = jnp.pad(small, ((0, 0), (0, room - each))).reshape(ns, srows, columns)
    y_own, *y_pays = local_call(
        collect_kernel,
        [((length, width), f32)] + [((length, width), bf16)] * (ns - 1),
        [y_back, hot_back],
    )
    y_got = [to_shift(v, k + 1) for k, v in enumerate(y_pays)]
    y_own = residual + y_own
    share, *products = local_call(
        product_kernel,
        [((part + srows, columns), f32)] + [((part + srows, columns), bf16)] * (ns - 1),
        [place_ids, held, held_other, wide, small],
        scalars=1,
        scratch=[pltpu.VMEM((ne * length, columns), bf16), pltpu.VMEM((width, columns), f32)],
        flops=2 * ne * length * width * columns,
        moved=2 * ne * length * (width + columns),
    )
    products, y_got = lax.optimization_barrier((products, y_got))
    for k, v in enumerate(products):
        share = share + to_shift(v, k + 1).astype(f32)
    share = share.astype(bf16)
    by_core = columns % lane == 0
    if by_core:
        spread = jnp.broadcast_to(share[None], (ne // 2,) + share.shape)
        same = [list(range(c, ne, 2)) for c in range(2)]
        whole = lax.all_to_all(
            spread, "expert", split_axis=0, concat_axis=0, axis_index_groups=same, tiled=True
        )
        whole = [whole, across(whole, 1)]
    else:
        whole = [plane(jnp.broadcast_to(share[None], (ne,) + share.shape))]
    out_qkv, out_out, small = local_call(
        unpack_kernel,
        [((part, 3 * width), f32), ((part, width), f32), ((srows, columns), f32)],
        [place_ids, *whole],
        scalars=1,
        moved=6 * ne * (part + srows) * columns,
    )
    small = small.reshape(-1)
    smalls = []
    at = 0
    for size in sizes:
        smalls.append(small[at : at + size])
        at += size

    for v in y_got:
        y_own = y_own + v.astype(f32)
    return (
        y_own.astype(bf16),
        grad_tokens,
        out_qkv,
        out_out,
        smalls[0].reshape(part, experts),
        smalls[1],
        smalls[2],
        smalls[3].reshape(buckets // ns, heads),
        grad_w_in,
        grad_w_down,
    )


def solution(mesh):
    in_specs = (
        P(("expert", "shard"), None),
        P("shard", None),
        P("shard", None),
        P("shard", None),
        P("shard"),
        P("shard"),
        P("shard", None),
        P("expert", None, "shard"),
        P("expert", "shard", None),
        P(("expert", "shard"), None),
        P(("expert", "shard"), None),
        P(),
        P(("expert", "shard"), None),
    )
    out_specs = (
        P(("expert", "shard"), None),
        P(("expert", "shard"), None),
        P("shard", None),
        P("shard", None),
        P("shard", None),
        P("shard"),
        P("shard"),
        P("shard", None),
        P("expert", None, "shard"),
        P("expert", "shard", None),
    )
    return jax.shard_map(body, mesh=mesh, in_specs=in_specs, out_specs=out_specs, check_vma=False)
```

```python
import functools

import jax
import jax.numpy as jnp
from jax import lax
from jax.experimental import pallas as pl
from jax.experimental.pallas import tpu as pltpu
from jax.sharding import PartitionSpec as P

norm_eps = 1e-06
f32 = jnp.float32
bf16 = jnp.bfloat16
lane = 128


def inverse_rms(values):
    return lax.rsqrt(jnp.mean(values * values, axis=-1, keepdims=True) + norm_eps)


def dot(a, b, ca=1, cb=0):
    return lax.dot_general(a, b, (((ca,), (cb,)), ((), ())), preferred_element_type=f32)


def split_two(v):
    high = v.astype(bf16)
    return high, (v - high.astype(f32)).astype(bf16)


def local_call(kernel, outs, args, scalars=0, views=None, scratch=(), flops=0, moved=0):
    def block(shape, where=None):
        where = where or (0,) * len(shape)
        return pl.BlockSpec(shape, lambda i: where)

    specs = [pl.BlockSpec(memory_space=pltpu.SMEM)] * scalars
    specs += [block(v.shape) for v in args[scalars:]]
    for n, (shape, where) in (views or {}).items():
        specs[n] = block(shape, where)
    return pl.pallas_call(
        kernel,
        out_shape=[jax.ShapeDtypeStruct(shape, kind) for shape, kind in outs],
        grid=(1,),
        in_specs=specs,
        out_specs=[block(shape) for shape, _ in outs],
        scratch_shapes=list(scratch),
        compiler_params=pltpu.CompilerParams(vmem_limit_bytes=56 << 20),
        cost_estimate=pl.CostEstimate(flops=flops, bytes_accessed=moved, transcendentals=0),
    )(*args)


def join_blocks(e, s, parts, full_ref):
    count = 2 * parts[0].shape[1]
    rows, cols = parts[0].shape[2], parts[0].shape[3]
    for n, ref in enumerate(parts):
        bits = ((2, 4), (4, 2))[n // 2]
        for i in range(ref.shape[0]):
            differ = (i & 1) * bits[0] + (i >> 1) * bits[1] + n % 2
            col = pl.multiple_of(((e & 7) ^ differ) * cols, lane)
            for q in range(count // 2):
                source = lax.rem(s - (q + (n // 2) * (count // 2)) + count, count)
                row = pl.multiple_of(source * rows, 16)
                full_ref[pl.ds(row, rows), pl.ds(col, cols)] = ref[i, q]


def head_mask(shape, h, head_dim):
    return lax.broadcasted_iota(jnp.int32, shape, 1) // head_dim == h


def prepare_kernel(row_ref, col_ref, route_ref, *refs):
    line_refs, (hot_ref, back_ref, g_ref) = refs[:-3], refs[-3:]
    total, tokens = hot_ref.shape
    width = line_refs[0].shape[1]
    length = tokens // len(line_refs)
    one, zero = jnp.ones((), f32), jnp.zeros((), f32)
    ids = lax.broadcasted_iota(jnp.int32, (total, tokens), 0)
    hots = [jnp.where(ids == row_ref[i : i + 1, :], one, zero).astype(bf16) for i in range(2)]
    hot_ref[...] = hots[0] + hots[1]
    ids = lax.broadcasted_iota(jnp.int32, (tokens, total), 1)
    found = (ids == col_ref[:, 0:1]) | (ids == col_ref[:, 1:2])
    back_ref[...] = jnp.where(found, one, zero).astype(bf16)
    rows = jnp.concatenate([ref[:length, :] for ref in line_refs], axis=0)
    shape = g_ref.shape
    g_ref[:, :, :width] = dot(hot_ref[...], rows).astype(bf16).reshape(shape[0], shape[1], width)
    cols = lax.broadcasted_iota(jnp.int32, (tokens, lane), 1)
    tags = zero
    for i in range(2):
        tag = jnp.where(cols == 0, route_ref[:, 1 - i : 2 - i].astype(f32), jnp.where(cols == 1, float(i), 0.0))
        tags = tags + dot(hots[i], tag.astype(bf16))
    g_ref[:, :, width:] = tags.astype(bf16).reshape(shape[0], shape[1], lane)


def attend_kernel(
    ids_ref, tok_ref, gain_ref, gain_two_ref, a_ref, a_other_ref, b_ref, b_other_ref, bias_ref,
    attn_ref, proj_ref, probs_ref, mixed_ref, res_ref, ffn_ref, full_ref,
):
    join_blocks(ids_ref[0], ids_ref[1], (a_ref, a_other_ref, b_ref, b_other_ref), full_ref)
    length, width = tok_ref.shape
    heads = bias_ref.shape[0]
    head_dim = width // heads
    pack = lane // head_dim
    x = tok_ref[...].astype(f32)
    low = (x * inverse_rms(x) * gain_ref[...]).astype(bf16)
    attn_ref[...] = low
    step = width // 2
    for c in range(6):
        cols = slice(c * step, (c + 1) * step)
        proj_ref[:, cols] = dot(low, full_ref[:, cols]).astype(bf16)
    for g in range(heads // pack):
        q = proj_ref[:, g * lane : (g + 1) * lane]
        k = proj_ref[:, width + g * lane : width + (g + 1) * lane]
        v = proj_ref[:, 2 * width + g * lane : 2 * width + (g + 1) * lane]
        total = jnp.zeros((length, lane), f32)
        for h in range(pack):
            keep = head_mask((length, lane), h, head_dim)
            s = dot(q, jnp.where(keep, k, jnp.zeros_like(k)), 1, 1) * 0.125 + bias_ref[g * pack + h]
            e = jnp.exp(s - jnp.max(s, axis=-1, keepdims=True))
            p = e / jnp.sum(e, axis=-1, keepdims=True)
            probs_ref[g * pack + h] = p
            total = total + dot(p.astype(bf16), jnp.where(keep, v, jnp.zeros_like(v)))
        mixed_ref[:, g * lane : (g + 1) * lane] = total.astype(bf16)
    res = x + dot(mixed_ref[...], full_ref[:, 3 * width :])
    res_ref[...] = res
    ffn_ref[...] = (res * inverse_rms(res) * gain_two_ref[...]).astype(bf16)


def expert_kernel(
    ids_ref, rows_ref, g_ref, wi_ref, wd_ref, router_ref,
    send_ref, y_ref, rows_out, hidden_out, dpre_out, dy_out,
):
    j = pl.program_id(0)
    count, per, width = rows_ref.shape
    total = count * per
    experts = router_ref.shape[1]
    x = rows_ref[...].reshape(total, width)
    rows_out[0] = x
    g = g_ref[:, :, :width].reshape(total, width).astype(f32)
    tags = g_ref[:, :, width:].reshape(total, lane).astype(f32)
    other, choice = tags[:, 0:1], tags[:, 1:2]
    logits = dot(x, router_ref[...])
    ids = lax.broadcasted_iota(jnp.int32, (total, experts), 1)
    own_logit = jnp.sum(jnp.where(ids == ids_ref[0] + j, logits, 0.0), -1, keepdims=True)
    other_logit = jnp.sum(jnp.where(ids.astype(f32) == other, logits, 0.0), -1, keepdims=True)
    gate = 1.0 / (1.0 + jnp.exp(other_logit - own_logit))
    d_y = (gate * g).astype(bf16)
    dy_out[0] = d_y
    pre = dot(x, wi_ref[0])
    square = pre * pre
    tanh = jnp.tanh(0.7978845608028654 * pre * (1.0 + 0.044715 * square))
    hidden = (0.5 * pre * (1.0 + tanh)).astype(bf16)
    hidden_out[0] = hidden
    slope = 0.5 * (1.0 + tanh) + 0.5 * pre * (1.0 - tanh * tanh) * (
        0.7978845608028654 * (1.0 + 3.0 * 0.044715 * square)
    )
    d_pre = (dot(d_y, wd_ref[0], 1, 1) * slope).astype(bf16)
    dpre_out[0] = d_pre
    at = pl.multiple_of(j * per, 16)
    d_rows = dot(d_pre, wi_ref[0], 1, 1).astype(bf16)
    send_ref[:, pl.ds(at, per), :width] = d_rows.reshape(count, per, width)
    y = dot(hidden, wd_ref[0])
    y_ref[:, pl.ds(at, per), :] = (gate * y).astype(bf16).reshape(count, per, width)
    d_gate = jnp.sum(g * y, axis=-1, keepdims=True)
    high = d_gate.astype(bf16).astype(f32)
    cols = lax.broadcasted_iota(jnp.int32, (total, lane), 1).astype(f32)
    tail = jnp.where(cols == choice, high, jnp.where(cols == choice + 2.0, d_gate - high, 0.0))
    send_ref[:, pl.ds(at, per), width:] = tail.astype(bf16).reshape(count, per, lane)


def collect_kernel(back_ref, hot_ref, own_ref, *pay_refs):
    length = own_ref.shape[0]
    rows = back_ref[...].reshape(-1, back_ref.shape[2])
    for k in range(len(pay_refs) + 1):
        got = dot(hot_ref[k * length : (k + 1) * length, :], rows)
        if k == 0:
            own_ref[...] = got
        else:
            pay_refs[k - 1][...] = got.astype(bf16)


def backward_kernel(count, *refs):
    own_ref = refs[0]
    got_refs = refs[1 : 1 + count]
    (
        ffn_ref, res_ref, cot_ref, router_ref, routes_ref, gain_ref, full_ref, proj_ref, probs_ref,
        wide_ref, dres_ref, dlog_ref, gain_grad_ref, ds_ref, dproj_ref,
    ) = refs[1 + count :]
    length, width = ffn_ref.shape
    heads = probs_ref.shape[0]
    head_dim = width // heads
    pack = lane // head_dim
    experts = router_ref.shape[1]
    d = own_ref[...]
    for ref in got_refs:
        d = d + ref[...].astype(f32)
    tail = d[:, width:]
    d = d[:, :width]
    dg = [tail[:, i : i + 1] + tail[:, i + 2 : i + 3] for i in range(2)]
    logits = dot(ffn_ref[...], router_ref[...])
    e = jnp.exp(logits - jnp.max(logits, axis=-1, keepdims=True))
    router = e / jnp.sum(e, axis=-1, keepdims=True)
    ids = lax.broadcasted_iota(jnp.int32, (length, experts), 1)
    hots = [ids == routes_ref[:, i : i + 1] for i in range(2)]
    picked = [jnp.sum(jnp.where(h, router, 0.0), -1, keepdims=True) for h in hots]
    both = picked[0] + picked[1]
    mean = (dg[0] * picked[0] + dg[1] * picked[1]) / (both * both)
    d_router = sum(jnp.where(h, v / both - mean, 0.0) for h, v in zip(hots, dg))
    d_logits = router * (d_router - jnp.sum(router * d_router, -1, keepdims=True))
    d_logits = d_logits.astype(bf16)
    dlog_ref[...] = d_logits
    d_ffn = d + dot(d_logits, router_ref[...], 1, 1)
    res = res_ref[...]
    inv = inverse_rms(res)
    normed = res * inv
    gain_grad_ref[...] = jnp.sum(d_ffn * normed, axis=0, keepdims=True)
    d_norm = d_ffn * gain_ref[...]
    d_res = cot_ref[...].astype(f32) + inv * (
        d_norm - normed * jnp.mean(d_norm * normed, axis=-1, keepdims=True)
    )
    dres_ref[...] = d_res
    d_branch = d_res.astype(bf16)
    d_heads = dot(d_branch, full_ref[...], 1, 1).astype(bf16)
    for g in range(heads // pack):
        q = proj_ref[:, g * lane : (g + 1) * lane]
        k = proj_ref[:, width + g * lane : width + (g + 1) * lane]
        v = proj_ref[:, 2 * width + g * lane : 2 * width + (g + 1) * lane]
        dh = d_heads[:, g * lane : (g + 1) * lane]
        zero = jnp.zeros_like(q)
        sums = [jnp.zeros((length, lane), f32) for _ in range(3)]
        for h in range(pack):
            keep = head_mask((length, lane), h, head_dim)
            p = probs_ref[g * pack + h]
            dh_one = jnp.where(keep, dh, zero)
            d_probs = dot(dh_one, v, 1, 1)
            ds = p * (d_probs - jnp.sum(p * d_probs, axis=-1, keepdims=True))
            ds = ds.astype(bf16)
            ds_ref[g * pack + h] = ds
            sums[0] = sums[0] + dot(ds, jnp.where(keep, k, zero))
            sums[1] = sums[1] + dot(ds, jnp.where(keep, q, zero), 0, 0)
            sums[2] = sums[2] + dot(p.astype(bf16), dh_one, 0, 0)
        for i, scale in enumerate((0.125, 0.125, 1.0)):
            dproj_ref[:, i * width + g * lane : i * width + (g + 1) * lane] = (sums[i] * scale).astype(bf16)
    columns = wide_ref.shape[2]
    split = 3 * width // columns
    for b in range(wide_ref.shape[0]):
        if b < split:
            wide_ref[b] = dproj_ref[:, b * columns : (b + 1) * columns]
        else:
            wide_ref[b] = d_branch[:, (b - split) * columns : (b - split + 1) * columns]


def product_kernel(ids_ref, own_ref, other_ref, wide_ref, small_ref, share_ref, *refs):
    pay_refs, order_ref, total_ref = refs[:-2], refs[-2], refs[-1]
    pairs, length, width = own_ref.shape
    e, s = ids_ref[0], ids_ref[1]
    count, part = small_ref.shape[0], width // small_ref.shape[0]
    for n in range(2):
        for i in range(pairs):
            at = (n * pairs + i) * length
            order_ref[at : at + length, :] = wide_ref[2 * i + ((e & 1) ^ n)]
    half = pairs * length
    total_ref[...] = dot(own_ref[...].reshape(half, width), order_ref[:half, :], 0, 0) + dot(
        other_ref[...].reshape(half, width), order_ref[half:, :], 0, 0
    )
    for k in range(count):
        target = lax.rem(s - k + count, count)
        rows = total_ref[pl.ds(pl.multiple_of(target * part, 16), part), :]
        ref = share_ref if k == 0 else pay_refs[k - 1]
        ref[:part, :] = rows.astype(ref.dtype)
        ref[part:, :] = small_ref[target].astype(ref.dtype)


def unpack_kernel(ids_ref, *refs):
    whole_refs, (qkv_ref, out_ref, small_ref) = refs[:-3], refs[-3:]
    part, width = out_ref.shape
    cols = small_ref.shape[1]
    split = 3 * width // cols
    pair = len(whole_refs)
    total = jnp.zeros(small_ref.shape, f32)
    for n, ref in enumerate(whole_refs):
        for i in range(ref.shape[0]):
            got = ref[i, :part, :].astype(f32)
            total = total + ref[i, part:, :].astype(f32)
            if pair * i < split:
                target, first = qkv_ref, pair * i
            else:
                target, first = out_ref, pair * i - split
            if pair == 1:
                target[:, first * cols : (first + 1) * cols] = got
            else:
                at = pl.multiple_of((first + ((ids_ref[0] & 1) ^ n)) * cols, lane)
                target[:, pl.ds(at, cols)] = got
    small_ref[...] = total


def tokens_kernel(dproj_ref, full_ref, tok_ref, gain_ref, dres_ref, out_ref, gain_grad_ref):
    d_in = dot(dproj_ref[...], full_ref[...], 1, 1)
    x = tok_ref[...].astype(f32)
    inv = inverse_rms(x)
    normed = x * inv
    gain_grad_ref[...] = jnp.sum(d_in * normed, axis=0, keepdims=True)
    d_norm = d_in * gain_ref[...]
    out_ref[...] = dres_ref[...] + inv * (
        d_norm - normed * jnp.mean(d_norm * normed, axis=-1, keepdims=True)
    )


def body(
    tokens,
    w_qkv,
    w_out,
    w_router,
    gain_attn,
    gain_ffn,
    bias_table,
    w_in,
    w_down,
    routes,
    slots,
    bucket_ids,
    cotangent,
):
    length, width = tokens.shape
    ne = lax.axis_size("expert")
    ns = lax.axis_size("shard")
    me_e = lax.axis_index("expert")
    me_s = lax.axis_index("shard")
    place_ids = jnp.stack([me_e, me_s]).astype(jnp.int32)
    exp_dev = w_in.shape[0]
    hidden_units = w_in.shape[2]
    experts = exp_dev * ne
    cap = 3 * length // experts
    per = ns * cap
    block = exp_dev * per
    total_rows = ne * block
    group_rows = ne * per
    heads = bias_table.shape[1]
    buckets = bias_table.shape[0] * ns
    part = width // ns

    def from_shift(v, k):
        return lax.ppermute(v, "shard", [(i, (i + k) % ns) for i in range(ns)])

    def to_shift(v, k):
        return lax.ppermute(v, "shard", [(i, (i - k) % ns) for i in range(ns)])

    def plane(v):
        return lax.all_to_all(v, "expert", split_axis=0, concat_axis=0, tiled=True)

    def across(v, bit):
        return lax.ppermute(v, "expert", [(i, i ^ bit) for i in range(ne)])

    cols = width // 2
    mine = me_e & 7
    weight = jnp.where(
        mine < 6,
        lax.dynamic_slice_in_dim(w_qkv, jnp.minimum(mine, 5) * cols, cols, 1),
        lax.dynamic_slice_in_dim(w_out, (jnp.maximum(mine, 6) - 6) * cols, cols, 1),
    )
    line = [weight] + [from_shift(weight, k) for k in range(1, ns)]

    smalls = (w_router, gain_attn, gain_ffn, bias_table, routes.astype(bf16), slots.astype(bf16))
    small = jnp.concatenate([v.reshape(-1) for v in smalls])
    small_rows = -(-small.size // width)
    small_rows += -small_rows % 16
    small = jnp.pad(small, (0, small_rows * width - small.size)).reshape(small_rows, width)
    packed = jnp.concatenate([cotangent, small], axis=0)
    packed, line = lax.optimization_barrier((packed, line))
    halves = []
    for half, bits in ((line[: ns // 2], (2, 4)), (line[ns // 2 :], (4, 2))):
        held = jnp.stack(half)[None]
        for bit in bits:
            held = jnp.concatenate([held, across(held, bit)], axis=0)
        halves.append(held)
    line = [packed] + [from_shift(packed, k) for k in range(1, ns)]
    line_small = jnp.stack([v[length:].reshape(-1) for v in line])
    order = lax.rem(me_s - jnp.arange(ns, dtype=jnp.int32) + ns, ns)
    in_order = jnp.take(line_small, order, axis=0)

    cuts = []
    at = 0
    for v in smalls:
        cuts.append((at, at + v.size))
        at += v.size

    def cut(v, i):
        return v[:, cuts[i][0] : cuts[i][1]]

    full_router = cut(in_order, 0).reshape(width, experts)
    gain_one = cut(in_order, 1).reshape(1, width).astype(f32)
    gain_two = cut(in_order, 2).reshape(1, width).astype(f32)
    table = cut(in_order, 3).reshape(buckets, heads)
    line_routes = cut(line_small, 4).reshape(ns * length, 2)
    line_slots = cut(line_small, 5).reshape(ns * length, 2).astype(jnp.int32)
    place = (
        line_routes.astype(jnp.int32) * per + jnp.repeat(order, length)[:, None] * cap + line_slots
    )
    causal = jnp.arange(length)[:, None] >= jnp.arange(length)[None, :]
    bucket_hot = (
        jnp.arange(buckets, dtype=jnp.int32)[:, None] == bucket_ids.reshape(1, -1)
    ).astype(bf16)
    pair_bias = dot(table, bucket_hot, 0, 0).reshape(heads, length, length)
    pair_bias = jnp.where(causal[None], pair_bias, -1e30)
    line, pair_bias = lax.optimization_barrier((line, pair_bias))
    hot, hot_back, g_rows = local_call(
        prepare_kernel,
        [((total_rows, ns * length), bf16), ((ns * length, total_rows), bf16), ((ne, block, width + lane), bf16)],
        [place.T, place, line_routes, *line],
    )
    pair_bias, g_rows, halves = lax.optimization_barrier((pair_bias, g_rows, halves))
    g_arrived = plane(g_rows)
    pieces = [halves[0], across(halves[0], 1), halves[1], across(halves[1], 1)]
    attn_in, proj, probs, mixed_low, residual, ffn_in, full = local_call(
        attend_kernel,
        [
            ((length, width), bf16),
            ((length, 3 * width), bf16),
            ((heads, length, length), f32),
            ((length, width), bf16),
            ((length, width), f32),
            ((length, width), bf16),
            ((width, 4 * width), bf16),
        ],
        [place_ids, tokens, gain_one, gain_two, *pieces, pair_bias],
        scalars=1,
    )

    line_ffn = jnp.concatenate([ffn_in] + [from_shift(ffn_in, k) for k in range(1, ns)], axis=0)
    line_ffn, g_arrived = lax.optimization_barrier((line_ffn, g_arrived))
    arrived = plane(dot(hot, line_ffn).astype(bf16).reshape(ne, block, width))

    split_e = 3 * ne // 4
    same = [list(range(c, ne, 2)) for c in range(2)]
    factors = jnp.stack([attn_in] * (split_e // 2) + [mixed_low] * ((ne - split_e) // 2))
    arrived, factors = lax.optimization_barrier((arrived, factors))
    held = lax.all_to_all(
        factors, "expert", split_axis=0, concat_axis=0, axis_index_groups=same, tiled=True
    )

    wide_width = width + lane
    first_id = (me_e * exp_dev).astype(jnp.int32).reshape(1)
    send, y_send, rows, hidden, d_pre, d_y = pl.pallas_call(
        expert_kernel,
        out_shape=[
            jax.ShapeDtypeStruct((ne, block, wide_width), bf16),
            jax.ShapeDtypeStruct((ne, block, width), bf16),
            jax.ShapeDtypeStruct((exp_dev, group_rows, width), bf16),
            jax.ShapeDtypeStruct((exp_dev, group_rows, hidden_units), bf16),
            jax.ShapeDtypeStruct((exp_dev, group_rows, hidden_units), bf16),
            jax.ShapeDtypeStruct((exp_dev, group_rows, width), bf16),
        ],
        grid=(exp_dev,),
        in_specs=[
            pl.BlockSpec(memory_space=pltpu.SMEM),
            pl.BlockSpec((ne, per, width), lambda j: (0, j, 0)),
            pl.BlockSpec((ne, per, wide_width), lambda j: (0, j, 0)),
            pl.BlockSpec((1, width, hidden_units), lambda j: (j, 0, 0)),
            pl.BlockSpec((1, hidden_units, width), lambda j: (j, 0, 0)),
            pl.BlockSpec((width, experts), lambda j: (0, 0)),
        ],
        out_specs=[
            pl.BlockSpec((ne, block, wide_width), lambda j: (0, 0, 0)),
            pl.BlockSpec((ne, block, width), lambda j: (0, 0, 0)),
            pl.BlockSpec((1, group_rows, width), lambda j: (j, 0, 0)),
            pl.BlockSpec((1, group_rows, hidden_units), lambda j: (j, 0, 0)),
            pl.BlockSpec((1, group_rows, hidden_units), lambda j: (j, 0, 0)),
            pl.BlockSpec((1, group_rows, width), lambda j: (j, 0, 0)),
        ],
        compiler_params=pltpu.CompilerParams(vmem_limit_bytes=56 << 20),
        cost_estimate=pl.CostEstimate(
            flops=8 * exp_dev * group_rows * width * hidden_units,
            bytes_accessed=16 * exp_dev * group_rows * width,
            transcendentals=0,
        ),
    )(first_id, arrived, g_arrived, w_in, w_down, full_router)
    send, held = lax.optimization_barrier((send, held))
    held_other = across(held, 1)
    d_back = plane(send)
    grad_w_down = jnp.einsum("jrf,jrd->jfd", hidden, d_y, preferred_element_type=f32)
    grad_w_in = jnp.einsum("jrd,jrf->jdf", rows, d_pre, preferred_element_type=f32)
    d_back, grad_w_down, grad_w_in = lax.optimization_barrier((d_back, grad_w_down, grad_w_in))

    own_d, *pays = local_call(
        collect_kernel,
        [((length, wide_width), f32)] + [((length, wide_width), bf16)] * (ns - 1),
        [d_back, hot_back],
        flops=2 * ns * length * total_rows * wide_width,
        moved=2 * total_rows * wide_width,
    )
    got = [to_shift(v, k + 1) for k, v in enumerate(pays)]
    pays, y_send = lax.optimization_barrier((pays, y_send))
    y_back = plane(y_send)
    columns = 4 * width // ne
    wide, d_residual, d_logits, gain_two_grad, d_scores, d_proj = local_call(
        functools.partial(backward_kernel, ns - 1),
        [
            ((ne, length, columns), bf16),
            ((length, width), f32),
            ((length, experts), bf16),
            ((1, width), f32),
            ((heads, length, length), bf16),
            ((length, 3 * width), bf16),
        ],
        [own_d, *got, ffn_in, residual, cotangent, full_router, routes, gain_two, full, proj, probs],
        views={ns + 6: ((width, width), (0, 3))},
        flops=2 * length * width * width + 10 * heads * length * length * lane,
        moved=2 * width * width + 8 * heads * length * length,
    )
    wide, y_back = lax.optimization_barrier((wide, y_back))
    wide = plane(wide)
    grad_table = dot(bucket_hot, d_scores.reshape(heads, length * length), 1, 1)
    d_proj, grad_table = lax.optimization_barrier((d_proj, grad_table))
    grad_tokens, gain_one_grad = local_call(
        tokens_kernel,
        [((length, width), f32), ((1, width), f32)],
        [d_proj, full, tokens, gain_one, d_residual],
        views={1: ((width, 3 * width), (0, 0))},
    )
    grad_router = dot(ffn_in, d_logits, 0, 0)

    small_parts = [
        grad_router.reshape(ns, -1),
        gain_one_grad.reshape(ns, -1),
        gain_two_grad.reshape(ns, -1),
        grad_table.reshape(ns, -1),
    ]
    sizes = [v.shape[1] for v in small_parts]
    small = jnp.concatenate(small_parts, axis=1).astype(bf16)
    each = small.shape[1]
    srows = -(-each // columns)
    srows += -srows % 16
    room = srows * columns
    small = jnp.pad(small, ((0, 0), (0, room - each))).reshape(ns, srows, columns)
    share, *products = local_call(
        product_kernel,
        [((part + srows, columns), f32)] + [((part + srows, columns), bf16)] * (ns - 1),
        [place_ids, held, held_other, wide, small],
        scalars=1,
        scratch=[pltpu.VMEM((ne * length, columns), bf16), pltpu.VMEM((width, columns), f32)],
        flops=2 * ne * length * width * columns,
        moved=2 * ne * length * (width + columns),
    )
    products, y_back = lax.optimization_barrier((products, y_back))
    y_own, *y_pays = local_call(
        collect_kernel,
        [((length, width), f32)] + [((length, width), bf16)] * (ns - 1),
        [y_back, hot_back],
    )
    y_own = residual + y_own
    for k, v in enumerate(products):
        share = share + to_shift(v, k + 1).astype(f32)
    share, y_pays = lax.optimization_barrier((share.astype(bf16), y_pays))
    y_got = [to_shift(v, k + 1) for k, v in enumerate(y_pays)]
    by_core = columns % lane == 0
    if by_core:
        spread = jnp.broadcast_to(share[None], (ne // 2,) + share.shape)
        whole = lax.all_to_all(
            spread, "expert", split_axis=0, concat_axis=0, axis_index_groups=same, tiled=True
        )
        whole, y_got = lax.optimization_barrier((whole, y_got))
        whole = [whole, across(whole, 1)]
    else:
        whole = [plane(jnp.broadcast_to(share[None], (ne,) + share.shape))]
    out_qkv, out_out, small = local_call(
        unpack_kernel,
        [((part, 3 * width), f32), ((part, width), f32), ((srows, columns), f32)],
        [place_ids, *whole],
        scalars=1,
        moved=6 * ne * (part + srows) * columns,
    )
    small = small.reshape(-1)
    smalls = []
    at = 0
    for size in sizes:
        smalls.append(small[at : at + size])
        at += size

    for v in y_got:
        y_own = y_own + v.astype(f32)
    return (
        y_own.astype(bf16),
        grad_tokens,
        out_qkv,
        out_out,
        smalls[0].reshape(part, experts),
        smalls[1],
        smalls[2],
        smalls[3].reshape(buckets // ns, heads),
        grad_w_in,
        grad_w_down,
    )


def solution(mesh):
    in_specs = (
        P(("expert", "shard"), None),
        P("shard", None),
        P("shard", None),
        P("shard", None),
        P("shard"),
        P("shard"),
        P("shard", None),
        P("expert", None, "shard"),
        P("expert", "shard", None),
        P(("expert", "shard"), None),
        P(("expert", "shard"), None),
        P(),
        P(("expert", "shard"), None),
    )
    out_specs = (
        P(("expert", "shard"), None),
        P(("expert", "shard"), None),
        P("shard", None),
        P("shard", None),
        P("shard", None),
        P("shard"),
        P("shard"),
        P("shard", None),
        P("expert", None, "shard"),
        P("expert", "shard", None),
    )
    return jax.shard_map(body, mesh=mesh, in_specs=in_specs, out_specs=out_specs, check_vma=False)
```

```python
import functools

import jax
import jax.numpy as jnp
from jax import lax
from jax.experimental import pallas as pl
from jax.experimental.pallas import tpu as pltpu
from jax.sharding import PartitionSpec as P

norm_eps = 1e-06
f32 = jnp.float32
bf16 = jnp.bfloat16
lane = 128


def inverse_rms(values):
    return lax.rsqrt(jnp.mean(values * values, axis=-1, keepdims=True) + norm_eps)


def dot(a, b, ca=1, cb=0):
    return lax.dot_general(a, b, (((ca,), (cb,)), ((), ())), preferred_element_type=f32)


def split_two(v):
    high = v.astype(bf16)
    return high, (v - high.astype(f32)).astype(bf16)


def local_call(kernel, outs, args, scalars=0, views=None, scratch=(), direct=False, flops=0, moved=0):
    def block(shape, where=None):
        where = where or (0,) * len(shape)
        return pl.BlockSpec(shape, lambda i: where)

    specs = [pl.BlockSpec(memory_space=pltpu.SMEM)] * scalars
    specs += [pl.BlockSpec(memory_space=pltpu.VMEM) if direct else block(v.shape) for v in args[scalars:]]
    for n, (shape, where) in (views or {}).items():
        specs[n] = block(shape, where)
    return pl.pallas_call(
        kernel,
        out_shape=[jax.ShapeDtypeStruct(shape, kind) for shape, kind in outs],
        grid=(1,),
        in_specs=specs,
        out_specs=[block(shape) for shape, _ in outs],
        scratch_shapes=list(scratch),
        compiler_params=pltpu.CompilerParams(vmem_limit_bytes=56 << 20),
        cost_estimate=pl.CostEstimate(flops=flops, bytes_accessed=moved, transcendentals=0),
    )(*args)


def join_blocks(e, s, parts, full_ref):
    count = 2 * parts[0].shape[1]
    rows, cols = parts[0].shape[2], parts[0].shape[3]
    for n, ref in enumerate(parts):
        bits = ((2, 4), (4, 2))[n // 4]
        for i in range(ref.shape[0]):
            differ = i * bits[0] + (n // 2 % 2) * bits[1] + n % 2
            col = pl.multiple_of(((e & 7) ^ differ) * cols, lane)
            for q in range(count // 2):
                source = lax.rem(s - (q + (n // 4) * (count // 2)) + count, count)
                row = pl.multiple_of(source * rows, 16)
                full_ref[pl.ds(row, rows), pl.ds(col, cols)] = ref[i, q]


def head_mask(shape, h, head_dim):
    return lax.broadcasted_iota(jnp.int32, shape, 1) // head_dim == h


def tables_kernel(row_ref, col_ref, route_ref, hot_ref, back_ref, tag_ref):
    total, tokens = hot_ref.shape
    one, zero = jnp.ones((), f32), jnp.zeros((), f32)
    ids = lax.broadcasted_iota(jnp.int32, (total, tokens), 0)
    hots = [jnp.where(ids == row_ref[i : i + 1, :], one, zero).astype(bf16) for i in range(2)]
    hot_ref[...] = hots[0] + hots[1]
    ids = lax.broadcasted_iota(jnp.int32, (tokens, total), 1)
    found = (ids == col_ref[:, 0:1]) | (ids == col_ref[:, 1:2])
    back_ref[...] = jnp.where(found, one, zero).astype(bf16)
    cols = lax.broadcasted_iota(jnp.int32, (tokens, lane), 1)
    tags = zero
    for i in range(2):
        tag = jnp.where(cols == 0, route_ref[:, 1 - i : 2 - i].astype(f32), jnp.where(cols == 1, float(i), 0.0))
        tags = tags + dot(hots[i], tag.astype(bf16))
    tag_ref[...] = tags.astype(bf16)


def spread_kernel(hot_ref, *refs):
    out_ref = refs[-1]
    count, block, wide = out_ref.shape
    width = refs[0].shape[1]
    line_refs = refs[:-1] if wide == width else refs[:-2]
    rows = jnp.concatenate([ref[...] for ref in line_refs], axis=0)
    out_ref[:, :, :width] = dot(hot_ref[...], rows).astype(bf16).reshape(count, block, width)
    if wide > width:
        out_ref[:, :, width:] = refs[-2][...].reshape(count, block, lane)


def attend_kernel(
    ids_ref, tok_ref, gain_ref, gain_two_ref, bias_ref, *refs,
):
    attn_ref, proj_ref, probs_ref, mixed_ref, res_ref, ffn_ref, full_ref = refs[-7:]
    join_blocks(ids_ref[0], ids_ref[1], refs[:-7], full_ref)
    length, width = tok_ref.shape
    heads = bias_ref.shape[0]
    head_dim = width // heads
    pack = lane // head_dim
    x = tok_ref[...].astype(f32)
    low = (x * inverse_rms(x) * gain_ref[...]).astype(bf16)
    attn_ref[...] = low
    step = width // 2
    for c in range(6):
        cols = slice(c * step, (c + 1) * step)
        proj_ref[:, cols] = dot(low, full_ref[:, cols]).astype(bf16)
    for g in range(heads // pack):
        q = proj_ref[:, g * lane : (g + 1) * lane]
        k = proj_ref[:, width + g * lane : width + (g + 1) * lane]
        v = proj_ref[:, 2 * width + g * lane : 2 * width + (g + 1) * lane]
        total = jnp.zeros((length, lane), f32)
        for h in range(pack):
            keep = head_mask((length, lane), h, head_dim)
            s = dot(q, jnp.where(keep, k, jnp.zeros_like(k)), 1, 1) * 0.125 + bias_ref[g * pack + h]
            e = jnp.exp(s - jnp.max(s, axis=-1, keepdims=True))
            p = e / jnp.sum(e, axis=-1, keepdims=True)
            probs_ref[g * pack + h] = p
            total = total + dot(p.astype(bf16), jnp.where(keep, v, jnp.zeros_like(v)))
        mixed_ref[:, g * lane : (g + 1) * lane] = total.astype(bf16)
    res = x + dot(mixed_ref[...], full_ref[:, 3 * width :])
    res_ref[...] = res
    ffn_ref[...] = (res * inverse_rms(res) * gain_two_ref[...]).astype(bf16)


def expert_kernel(
    ids_ref, rows_ref, g_ref, wi_ref, wd_ref, router_ref,
    send_ref, y_ref, rows_out, hidden_out, dpre_out, dy_out,
):
    j = pl.program_id(0)
    count, per, width = rows_ref.shape
    total = count * per
    experts = router_ref.shape[1]
    x = rows_ref[...].reshape(total, width)
    rows_out[0] = x
    g = g_ref[:, :, :width].reshape(total, width).astype(f32)
    tags = g_ref[:, :, width:].reshape(total, lane).astype(f32)
    other, choice = tags[:, 0:1], tags[:, 1:2]
    logits = dot(x, router_ref[...])
    ids = lax.broadcasted_iota(jnp.int32, (total, experts), 1)
    own_logit = jnp.sum(jnp.where(ids == ids_ref[0] + j, logits, 0.0), -1, keepdims=True)
    other_logit = jnp.sum(jnp.where(ids.astype(f32) == other, logits, 0.0), -1, keepdims=True)
    gate = 1.0 / (1.0 + jnp.exp(other_logit - own_logit))
    d_y = (gate * g).astype(bf16)
    dy_out[0] = d_y
    pre = dot(x, wi_ref[0])
    square = pre * pre
    root = 0.7978845608028654
    gate_in = 0.5 + 0.5 * jnp.tanh(pre * (root + root * 0.044715 * square))
    hidden = (pre * gate_in).astype(bf16)
    hidden_out[0] = hidden
    slope = gate_in + gate_in * (1.0 - gate_in) * (
        pre * (2.0 * root + 6.0 * root * 0.044715 * square)
    )
    d_pre = (dot(d_y, wd_ref[0], 1, 1) * slope).astype(bf16)
    dpre_out[0] = d_pre
    at = pl.multiple_of(j * per, 16)
    d_rows = dot(d_pre, wi_ref[0], 1, 1).astype(bf16)
    send_ref[:, pl.ds(at, per), :width] = d_rows.reshape(count, per, width)
    y = dot(hidden, wd_ref[0])
    y_ref[:, pl.ds(at, per), :] = (gate * y).astype(bf16).reshape(count, per, width)
    d_gate = jnp.sum(g * y, axis=-1, keepdims=True)
    high = d_gate.astype(bf16).astype(f32)
    cols = lax.broadcasted_iota(jnp.int32, (total, lane), 1).astype(f32)
    tail = jnp.where(cols == choice, high, jnp.where(cols == choice + 2.0, d_gate - high, 0.0))
    send_ref[:, pl.ds(at, per), width:] = tail.astype(bf16).reshape(count, per, lane)


def collect_kernel(back_ref, hot_ref, own_ref, *pay_refs):
    length = own_ref.shape[0]
    rows = back_ref[...].reshape(-1, back_ref.shape[2])
    for k in range(len(pay_refs) + 1):
        got = dot(hot_ref[k * length : (k + 1) * length, :], rows)
        if k == 0:
            own_ref[...] = got
        else:
            pay_refs[k - 1][...] = got.astype(bf16)


def backward_kernel(count, *refs):
    own_ref = refs[0]
    got_refs = refs[1 : 1 + count]
    (
        ffn_ref, res_ref, cot_ref, router_ref, routes_ref, gain_ref, full_ref, proj_ref, probs_ref,
        wide_ref, dres_ref, dlog_ref, gain_grad_ref, ds_ref, dproj_ref,
    ) = refs[1 + count :]
    length, width = ffn_ref.shape
    heads = probs_ref.shape[0]
    head_dim = width // heads
    pack = lane // head_dim
    experts = router_ref.shape[1]
    d = own_ref[...]
    for ref in got_refs:
        d = d + ref[...].astype(f32)
    tail = d[:, width:]
    d = d[:, :width]
    dg = [tail[:, i : i + 1] + tail[:, i + 2 : i + 3] for i in range(2)]
    logits = dot(ffn_ref[...], router_ref[...])
    e = jnp.exp(logits - jnp.max(logits, axis=-1, keepdims=True))
    router = e / jnp.sum(e, axis=-1, keepdims=True)
    ids = lax.broadcasted_iota(jnp.int32, (length, experts), 1)
    hots = [ids == routes_ref[:, i : i + 1] for i in range(2)]
    picked = [jnp.sum(jnp.where(h, router, 0.0), -1, keepdims=True) for h in hots]
    both = picked[0] + picked[1]
    mean = (dg[0] * picked[0] + dg[1] * picked[1]) / (both * both)
    d_router = sum(jnp.where(h, v / both - mean, 0.0) for h, v in zip(hots, dg))
    d_logits = router * (d_router - jnp.sum(router * d_router, -1, keepdims=True))
    d_logits = d_logits.astype(bf16)
    dlog_ref[...] = d_logits
    d_ffn = d + dot(d_logits, router_ref[...], 1, 1)
    res = res_ref[...]
    inv = inverse_rms(res)
    normed = res * inv
    gain_grad_ref[...] = jnp.sum(d_ffn * normed, axis=0, keepdims=True)
    d_norm = d_ffn * gain_ref[...]
    d_res = cot_ref[...].astype(f32) + inv * (
        d_norm - normed * jnp.mean(d_norm * normed, axis=-1, keepdims=True)
    )
    dres_ref[...] = d_res
    d_branch = d_res.astype(bf16)
    d_heads = dot(d_branch, full_ref[...], 1, 1).astype(bf16)
    for g in range(heads // pack):
        q = proj_ref[:, g * lane : (g + 1) * lane]
        k = proj_ref[:, width + g * lane : width + (g + 1) * lane]
        v = proj_ref[:, 2 * width + g * lane : 2 * width + (g + 1) * lane]
        dh = d_heads[:, g * lane : (g + 1) * lane]
        zero = jnp.zeros_like(q)
        sums = [jnp.zeros((length, lane), f32) for _ in range(3)]
        for h in range(pack):
            keep = head_mask((length, lane), h, head_dim)
            p = probs_ref[g * pack + h]
            dh_one = jnp.where(keep, dh, zero)
            d_probs = dot(dh_one, v, 1, 1)
            ds = p * (d_probs - jnp.sum(p * d_probs, axis=-1, keepdims=True))
            ds = ds.astype(bf16)
            ds_ref[g * pack + h] = ds.astype(f32)
            sums[0] = sums[0] + dot(ds, jnp.where(keep, k, zero))
            sums[1] = sums[1] + dot(ds, jnp.where(keep, q, zero), 0, 0)
            sums[2] = sums[2] + dot(p.astype(bf16), dh_one, 0, 0)
        for i, scale in enumerate((0.125, 0.125, 1.0)):
            dproj_ref[:, i * width + g * lane : i * width + (g + 1) * lane] = (sums[i] * scale).astype(bf16)
    columns = wide_ref.shape[2]
    split = 3 * width // columns
    for b in range(wide_ref.shape[0]):
        if b < split:
            wide_ref[b] = dproj_ref[:, b * columns : (b + 1) * columns]
        else:
            wide_ref[b] = d_branch[:, (b - split) * columns : (b - split + 1) * columns]


def product_kernel(ids_ref, own_ref, other_ref, wide_ref, small_ref, share_ref, *refs):
    pay_refs, order_ref, total_ref = refs[:-2], refs[-2], refs[-1]
    pairs, length, width = own_ref.shape
    e, s = ids_ref[0], ids_ref[1]
    count, part = small_ref.shape[0], width // small_ref.shape[0]
    for n in range(2):
        for i in range(pairs):
            at = (n * pairs + i) * length
            order_ref[at : at + length, :] = wide_ref[2 * i + ((e & 1) ^ n)]
    half = pairs * length
    total_ref[...] = dot(own_ref[...].reshape(half, width), order_ref[:half, :], 0, 0) + dot(
        other_ref[...].reshape(half, width), order_ref[half:, :], 0, 0
    )
    for k in range(count):
        target = lax.rem(s - k + count, count)
        rows = total_ref[pl.ds(pl.multiple_of(target * part, 16), part), :]
        ref = share_ref if k == 0 else pay_refs[k - 1]
        ref[:part, :] = rows.astype(ref.dtype)
        ref[part:, :] = small_ref[target].astype(ref.dtype)


def unpack_kernel(ids_ref, *refs):
    whole_refs, (qkv_ref, out_ref, small_ref) = refs[:-3], refs[-3:]
    part, width = out_ref.shape
    cols = small_ref.shape[1]
    split = 3 * width // cols
    pair = len(whole_refs)
    total = jnp.zeros(small_ref.shape, f32)
    for n, ref in enumerate(whole_refs):
        for i in range(ref.shape[0]):
            got = ref[i, :part, :].astype(f32)
            total = total + ref[i, part:, :].astype(f32)
            if pair * i < split:
                target, first = qkv_ref, pair * i
            else:
                target, first = out_ref, pair * i - split
            if pair == 1:
                target[:, first * cols : (first + 1) * cols] = got
            else:
                at = pl.multiple_of((first + ((ids_ref[0] & 1) ^ n)) * cols, lane)
                target[:, pl.ds(at, cols)] = got
    small_ref[...] = total


def tokens_kernel(
    dproj_ref, full_ref, tok_ref, gain_ref, dres_ref, ds_ref, ids_ref, out_ref, gain_grad_ref, table_ref
):
    ids = ids_ref[...]
    for b in range(table_ref.shape[0]):
        found = ids == b
        for h in range(table_ref.shape[1]):
            table_ref[b, h : h + 1, :] = jnp.sum(jnp.where(found, ds_ref[h], 0.0), axis=0, keepdims=True)
    d_in = dot(dproj_ref[...], full_ref[...], 1, 1)
    x = tok_ref[...].astype(f32)
    inv = inverse_rms(x)
    normed = x * inv
    gain_grad_ref[...] = jnp.sum(d_in * normed, axis=0, keepdims=True)
    d_norm = d_in * gain_ref[...]
    out_ref[...] = dres_ref[...] + inv * (
        d_norm - normed * jnp.mean(d_norm * normed, axis=-1, keepdims=True)
    )


def body(
    tokens,
    w_qkv,
    w_out,
    w_router,
    gain_attn,
    gain_ffn,
    bias_table,
    w_in,
    w_down,
    routes,
    slots,
    bucket_ids,
    cotangent,
):
    length, width = tokens.shape
    ne = lax.axis_size("expert")
    ns = lax.axis_size("shard")
    me_e = lax.axis_index("expert")
    me_s = lax.axis_index("shard")
    place_ids = jnp.stack([me_e, me_s]).astype(jnp.int32)
    exp_dev = w_in.shape[0]
    hidden_units = w_in.shape[2]
    experts = exp_dev * ne
    cap = 3 * length // experts
    per = ns * cap
    block = exp_dev * per
    total_rows = ne * block
    group_rows = ne * per
    heads = bias_table.shape[1]
    buckets = bias_table.shape[0] * ns
    part = width // ns

    def from_shift(v, k):
        return lax.ppermute(v, "shard", [(i, (i + k) % ns) for i in range(ns)])

    def to_shift(v, k):
        return lax.ppermute(v, "shard", [(i, (i - k) % ns) for i in range(ns)])

    def plane(v):
        return lax.all_to_all(v, "expert", split_axis=0, concat_axis=0, tiled=True)

    def across(v, bit):
        return lax.ppermute(v, "expert", [(i, i ^ bit) for i in range(ne)])

    cols = width // 2
    mine = me_e & 7
    weight = jnp.where(
        mine < 6,
        lax.dynamic_slice_in_dim(w_qkv, jnp.minimum(mine, 5) * cols, cols, 1),
        lax.dynamic_slice_in_dim(w_out, (jnp.maximum(mine, 6) - 6) * cols, cols, 1),
    )
    smalls = (w_router, gain_attn, gain_ffn, bias_table, routes.astype(bf16), slots.astype(bf16))
    small = jnp.concatenate([v.reshape(-1) for v in smalls])
    small_rows = -(-small.size // cols)
    small_rows += -small_rows % 16
    small = jnp.pad(small, (0, small_rows * cols - small.size)).reshape(small_rows, cols)
    weight = jnp.concatenate([weight, small], axis=0)
    line = [weight] + [from_shift(weight, k) for k in range(1, ns)]
    cotangent, line = lax.optimization_barrier((cotangent, line))
    pieces = []
    for half, bits in ((line[: ns // 2], (2, 4)), (line[ns // 2 :], (4, 2))):
        held = jnp.stack([v[:part] for v in half])[None]
        held = jnp.concatenate([held, across(held, bits[0])], axis=0)
        pieces.append((held, across(held, 1), across(held, bits[1])))

    line_small = jnp.stack([v[part:].reshape(-1) for v in line])
    line_g = [cotangent] + [from_shift(cotangent, k) for k in range(1, ns)]
    order = lax.rem(me_s - jnp.arange(ns, dtype=jnp.int32) + ns, ns)
    in_order = jnp.take(line_small, order, axis=0)

    cuts = []
    at = 0
    for v in smalls:
        cuts.append((at, at + v.size))
        at += v.size

    def cut(v, i):
        return v[:, cuts[i][0] : cuts[i][1]]

    full_router = cut(in_order, 0).reshape(width, experts)
    gain_one = cut(in_order, 1).reshape(1, width).astype(f32)
    gain_two = cut(in_order, 2).reshape(1, width).astype(f32)
    table = cut(in_order, 3).reshape(buckets, heads)
    line_routes = cut(line_small, 4).reshape(ns * length, 2)
    line_slots = cut(line_small, 5).reshape(ns * length, 2).astype(jnp.int32)
    place = (
        line_routes.astype(jnp.int32) * per + jnp.repeat(order, length)[:, None] * cap + line_slots
    )
    causal = jnp.arange(length)[:, None] >= jnp.arange(length)[None, :]
    bucket_hot = (
        jnp.arange(buckets, dtype=jnp.int32)[:, None] == bucket_ids.reshape(1, -1)
    ).astype(bf16)
    pair_bias = dot(table, bucket_hot, 0, 0).reshape(heads, length, length)
    pair_bias = jnp.where(causal[None], pair_bias, -1e30)
    hot, hot_back, tags = local_call(
        tables_kernel,
        [((total_rows, ns * length), bf16), ((ns * length, total_rows), bf16), ((total_rows, lane), bf16)],
        [place.T, place, line_routes],
    )
    (g_rows,) = local_call(
        spread_kernel,
        [((ne, block, width + lane), bf16)],
        [hot, *line_g, tags],
    )
    last = [p[2] for p in pieces]
    pair_bias, g_rows, last, gain_one, gain_two, place_ids = lax.optimization_barrier(
        (pair_bias, g_rows, last, gain_one, gain_two, place_ids)
    )
    g_arrived = plane(g_rows)
    pieces = [v for p, q in zip(pieces, last) for v in (p[0], p[1], q, across(q, 1))]
    attn_in, proj, probs, mixed_low, residual, ffn_in, full = local_call(
        attend_kernel,
        [
            ((length, width), bf16),
            ((length, 3 * width), bf16),
            ((heads, length, length), f32),
            ((length, width), bf16),
            ((length, width), f32),
            ((length, width), bf16),
            ((width, 4 * width), bf16),
        ],
        [place_ids, tokens, gain_one, gain_two, pair_bias, *pieces],
        scalars=1,
        direct=True,
    )

    line_ffn = [ffn_in] + [from_shift(ffn_in, k) for k in range(1, ns)]
    line_ffn, g_arrived = lax.optimization_barrier((line_ffn, g_arrived))
    (sent,) = local_call(spread_kernel, [((ne, block, width), bf16)], [hot, *line_ffn], direct=True)
    arrived = plane(sent)
    split_e = 3 * ne // 4
    same = [list(range(c, ne, 2)) for c in range(2)]
    factors = jnp.stack([attn_in] * (split_e // 2) + [mixed_low] * ((ne - split_e) // 2))
    arrived, factors = lax.optimization_barrier((arrived, factors))
    held = lax.all_to_all(
        factors, "expert", split_axis=0, concat_axis=0, axis_index_groups=same, tiled=True
    )

    wide_width = width + lane
    first_id = (me_e * exp_dev).astype(jnp.int32).reshape(1)
    send, y_send, rows, hidden, d_pre, d_y = pl.pallas_call(
        expert_kernel,
        out_shape=[
            jax.ShapeDtypeStruct((ne, block, wide_width), bf16),
            jax.ShapeDtypeStruct((ne, block, width), bf16),
            jax.ShapeDtypeStruct((exp_dev, group_rows, width), bf16),
            jax.ShapeDtypeStruct((exp_dev, group_rows, hidden_units), bf16),
            jax.ShapeDtypeStruct((exp_dev, group_rows, hidden_units), bf16),
            jax.ShapeDtypeStruct((exp_dev, group_rows, width), bf16),
        ],
        grid=(exp_dev,),
        in_specs=[
            pl.BlockSpec(memory_space=pltpu.SMEM),
            pl.BlockSpec((ne, per, width), lambda j: (0, j, 0)),
            pl.BlockSpec((ne, per, wide_width), lambda j: (0, j, 0)),
            pl.BlockSpec((1, width, hidden_units), lambda j: (j, 0, 0)),
            pl.BlockSpec((1, hidden_units, width), lambda j: (j, 0, 0)),
            pl.BlockSpec((width, experts), lambda j: (0, 0)),
        ],
        out_specs=[
            pl.BlockSpec((ne, block, wide_width), lambda j: (0, 0, 0)),
            pl.BlockSpec((ne, block, width), lambda j: (0, 0, 0)),
            pl.BlockSpec((1, group_rows, width), lambda j: (j, 0, 0)),
            pl.BlockSpec((1, group_rows, hidden_units), lambda j: (j, 0, 0)),
            pl.BlockSpec((1, group_rows, hidden_units), lambda j: (j, 0, 0)),
            pl.BlockSpec((1, group_rows, width), lambda j: (j, 0, 0)),
        ],
        compiler_params=pltpu.CompilerParams(vmem_limit_bytes=56 << 20),
        cost_estimate=pl.CostEstimate(
            flops=8 * exp_dev * group_rows * width * hidden_units,
            bytes_accessed=16 * exp_dev * group_rows * width,
            transcendentals=0,
        ),
    )(first_id, arrived, g_arrived, w_in, w_down, full_router)
    send, held = lax.optimization_barrier((send, held))
    held_other = across(held, 1)
    d_back = plane(send)
    grad_w_down = jnp.einsum("jrf,jrd->jfd", hidden, d_y, preferred_element_type=f32)
    grad_w_in = jnp.einsum("jrd,jrf->jdf", rows, d_pre, preferred_element_type=f32)
    d_back, grad_w_down, grad_w_in = lax.optimization_barrier((d_back, grad_w_down, grad_w_in))

    own_d, *pays = local_call(
        collect_kernel,
        [((length, wide_width), f32)] + [((length, wide_width), bf16)] * (ns - 1),
        [d_back, hot_back],
        direct=True,
        flops=2 * ns * length * total_rows * wide_width,
        moved=2 * total_rows * wide_width,
    )
    got = [to_shift(v, k + 1) for k, v in enumerate(pays)]
    pays, y_send = lax.optimization_barrier((pays, y_send))
    y_back = plane(y_send)
    columns = 4 * width // ne
    wide, d_residual, d_logits, gain_two_grad, d_scores, d_proj = local_call(
        functools.partial(backward_kernel, ns - 1),
        [
            ((ne, length, columns), bf16),
            ((length, width), f32),
            ((length, experts), bf16),
            ((1, width), f32),
            ((heads, length, length), f32),
            ((length, 3 * width), bf16),
        ],
        [own_d, *got, ffn_in, residual, cotangent, full_router, routes, gain_two, full, proj, probs],
        views={ns + 6: ((width, width), (0, 3))},
        flops=2 * length * width * width + 10 * heads * length * length * lane,
        moved=2 * width * width + 8 * heads * length * length,
    )
    wide, y_back = lax.optimization_barrier((wide, y_back))
    wide = plane(wide)
    grad_tokens, gain_one_grad, grad_table = local_call(
        tokens_kernel,
        [((length, width), f32), ((1, width), f32), ((buckets, heads, lane), f32)],
        [d_proj, full, tokens, gain_one, d_residual, d_scores, bucket_ids],
        views={1: ((width, 3 * width), (0, 0))},
    )
    grad_router = dot(ffn_in, d_logits, 0, 0)

    small_parts = [
        grad_router.reshape(ns, -1),
        gain_one_grad.reshape(ns, -1),
        gain_two_grad.reshape(ns, -1),
        jnp.sum(grad_table, axis=-1).reshape(ns, -1),
    ]
    sizes = [v.shape[1] for v in small_parts]
    small = jnp.concatenate(small_parts, axis=1).astype(bf16)
    each = small.shape[1]
    srows = -(-each // columns)
    srows += -srows % 16
    room = srows * columns
    small = jnp.pad(small, ((0, 0), (0, room - each))).reshape(ns, srows, columns)
    share, *products = local_call(
        product_kernel,
        [((part + srows, columns), f32)] + [((part + srows, columns), bf16)] * (ns - 1),
        [place_ids, held, held_other, wide, small],
        scalars=1,
        direct=True,
        scratch=[pltpu.VMEM((ne * length, columns), bf16), pltpu.VMEM((width, columns), f32)],
        flops=2 * ne * length * width * columns,
        moved=2 * ne * length * (width + columns),
    )
    products, y_back = lax.optimization_barrier((products, y_back))
    y_own, *y_pays = local_call(
        collect_kernel,
        [((length, width), f32)] + [((length, width), bf16)] * (ns - 1),
        [y_back, hot_back],
        direct=True,
    )
    y_own = residual + y_own
    for k, v in enumerate(products):
        share = share + to_shift(v, k + 1).astype(f32)
    share, y_pays = lax.optimization_barrier((share.astype(bf16), y_pays))
    y_got = [to_shift(v, k + 1) for k, v in enumerate(y_pays)]
    by_core = columns % lane == 0
    if by_core:
        spread = jnp.broadcast_to(share[None], (ne // 2,) + share.shape)
        whole = lax.all_to_all(
            spread, "expert", split_axis=0, concat_axis=0, axis_index_groups=same, tiled=True
        )
        whole, y_got[1] = lax.optimization_barrier((whole, y_got[1]))
        whole = [whole, across(whole, 1)]
    else:
        whole = [plane(jnp.broadcast_to(share[None], (ne,) + share.shape))]
    out_qkv, out_out, small = local_call(
        unpack_kernel,
        [((part, 3 * width), f32), ((part, width), f32), ((srows, columns), f32)],
        [place_ids, *whole],
        scalars=1,
        direct=True,
    )
    y_own, small = lax.optimization_barrier((y_own, small.reshape(-1)))
    smalls = []
    at = 0
    for size in sizes:
        smalls.append(small[at : at + size])
        at += size

    for v in y_got:
        y_own = y_own + v.astype(f32)
    return (
        y_own.astype(bf16),
        grad_tokens,
        out_qkv,
        out_out,
        smalls[0].reshape(part, experts),
        smalls[1],
        smalls[2],
        smalls[3].reshape(buckets // ns, heads),
        grad_w_in,
        grad_w_down,
    )


def solution(mesh):
    in_specs = (
        P(("expert", "shard"), None),
        P("shard", None),
        P("shard", None),
        P("shard", None),
        P("shard"),
        P("shard"),
        P("shard", None),
        P("expert", None, "shard"),
        P("expert", "shard", None),
        P(("expert", "shard"), None),
        P(("expert", "shard"), None),
        P(),
        P(("expert", "shard"), None),
    )
    out_specs = (
        P(("expert", "shard"), None),
        P(("expert", "shard"), None),
        P("shard", None),
        P("shard", None),
        P("shard", None),
        P("shard"),
        P("shard"),
        P("shard", None),
        P("expert", None, "shard"),
        P("expert", "shard", None),
    )
    return jax.shard_map(body, mesh=mesh, in_specs=in_specs, out_specs=out_specs, check_vma=False)
```

```python
import functools
import math

import jax
import jax.numpy as jnp
from jax import lax
from jax.experimental import pallas as pl
from jax.experimental.pallas import tpu as pltpu
from jax.sharding import PartitionSpec as P

norm_eps = 1e-06
f32 = jnp.float32
bf16 = jnp.bfloat16
lane = 128


def inverse_rms(values):
    return lax.rsqrt(jnp.mean(values * values, axis=-1, keepdims=True) + norm_eps)


def dot(a, b, ca=1, cb=0):
    return lax.dot_general(a, b, (((ca,), (cb,)), ((), ())), preferred_element_type=f32)


def split_two(v):
    high = v.astype(bf16)
    return high, (v - high.astype(f32)).astype(bf16)


def local_call(kernel, outs, args, scalars=0, views=None, scratch=(), direct=False, flops=0, moved=0):
    def block(shape, where=None):
        where = where or (0,) * len(shape)
        return pl.BlockSpec(shape, lambda i: where)

    specs = [pl.BlockSpec(memory_space=pltpu.SMEM)] * scalars
    specs += [pl.BlockSpec(memory_space=pltpu.VMEM) if direct else block(v.shape) for v in args[scalars:]]
    for n, (shape, where) in (views or {}).items():
        specs[n] = block(shape, where)
    return pl.pallas_call(
        kernel,
        out_shape=[jax.ShapeDtypeStruct(shape, kind) for shape, kind in outs],
        grid=(1,),
        in_specs=specs,
        out_specs=[block(shape) for shape, _ in outs],
        scratch_shapes=list(scratch),
        compiler_params=pltpu.CompilerParams(vmem_limit_bytes=56 << 20),
        cost_estimate=pl.CostEstimate(flops=flops, bytes_accessed=moved, transcendentals=0),
    )(*args)


def join_blocks(e, s, parts, full_ref):
    count = 2 * parts[0].shape[1]
    rows, cols = parts[0].shape[2], parts[0].shape[3]
    for n, ref in enumerate(parts):
        bits = ((2, 4), (4, 2))[n // 4]
        for i in range(ref.shape[0]):
            differ = i * bits[0] + (n // 2 % 2) * bits[1] + n % 2
            col = pl.multiple_of(((e & 7) ^ differ) * cols, lane)
            for q in range(count // 2):
                source = lax.rem(s - (q + (n // 4) * (count // 2)) + count, count)
                row = pl.multiple_of(source * rows, 16)
                full_ref[pl.ds(row, rows), pl.ds(col, cols)] = ref[i, q]


def head_mask(shape, h, head_dim):
    return lax.broadcasted_iota(jnp.int32, shape, 1) // head_dim == h


def tables_kernel(row_ref, col_ref, route_ref, hot_ref, back_ref, tag_ref):
    total, tokens = hot_ref.shape
    one, zero = jnp.ones((), f32), jnp.zeros((), f32)
    ids = lax.broadcasted_iota(jnp.int32, (total, tokens), 0)
    hots = [jnp.where(ids == row_ref[i : i + 1, :], one, zero).astype(bf16) for i in range(2)]
    hot_ref[...] = hots[0] + hots[1]
    ids = lax.broadcasted_iota(jnp.int32, (tokens, total), 1)
    found = (ids == col_ref[:, 0:1]) | (ids == col_ref[:, 1:2])
    back_ref[...] = jnp.where(found, one, zero).astype(bf16)
    cols = lax.broadcasted_iota(jnp.int32, (tokens, lane), 1)
    tags = zero
    for i in range(2):
        tag = jnp.where(cols == 0, route_ref[:, 1 - i : 2 - i].astype(f32), jnp.where(cols == 1, float(i), 0.0))
        tags = tags + dot(hots[i], tag.astype(bf16))
    tag_ref[...] = tags.astype(bf16)


def spread_kernel(hot_ref, *refs):
    out_ref, rows_ref = refs[-2:]
    count, block, wide = out_ref.shape
    length, width = refs[0].shape
    line_refs = refs[: rows_ref.shape[0] // length]

    @pl.when(pl.program_id(0) == 0)
    def _():
        for k, ref in enumerate(line_refs):
            rows_ref[k * length : (k + 1) * length, :] = ref[...]

    out_ref[:, :, :width] = dot(hot_ref[...], rows_ref[...]).astype(bf16).reshape(count, block, width)
    if wide > width:
        out_ref[:, :, width:] = refs[-3][...].reshape(count, block, lane)


def spread(hot, line, shape, tags=None):
    length, width = line[0].shape
    count, block, wide = shape
    rows = 2 * block
    specs = [pl.BlockSpec((rows, hot.shape[1]), lambda i: (i, 0))]
    specs += [pl.BlockSpec((length, width), lambda i: (0, 0))] * len(line)
    args = [hot, *line]
    if tags is not None:
        specs.append(pl.BlockSpec((rows, lane), lambda i: (i, 0)))
        args.append(tags)
    return pl.pallas_call(
        spread_kernel,
        out_shape=jax.ShapeDtypeStruct(shape, bf16),
        grid=(count // 2,),
        in_specs=specs,
        out_specs=pl.BlockSpec((2, block, wide), lambda i: (i, 0, 0)),
        scratch_shapes=[pltpu.VMEM((len(line) * length, width), bf16)],
        compiler_params=pltpu.CompilerParams(vmem_limit_bytes=32 << 20),
        cost_estimate=pl.CostEstimate(flops=0, bytes_accessed=0, transcendentals=0),
    )(*args)


def attend_kernel(
    ids_ref, tok_ref, gain_ref, gain_two_ref, bias_ref, *refs,
):
    attn_ref, proj_ref, probs_ref, mixed_ref, res_ref, ffn_ref, full_ref = refs[-7:]
    join_blocks(ids_ref[0], ids_ref[1], refs[:-7], full_ref)
    length, width = tok_ref.shape
    heads = bias_ref.shape[0]
    head_dim = width // heads
    pack = lane // head_dim
    x = tok_ref[...].astype(f32)
    low = (x * inverse_rms(x) * gain_ref[...]).astype(bf16)
    attn_ref[...] = low
    step = width // 2
    for c in range(6):
        cols = slice(c * step, (c + 1) * step)
        proj_ref[:, cols] = dot(low, full_ref[:, cols]).astype(bf16)
    for g in range(heads // pack):
        q = proj_ref[:, g * lane : (g + 1) * lane]
        k = proj_ref[:, width + g * lane : width + (g + 1) * lane]
        v = proj_ref[:, 2 * width + g * lane : 2 * width + (g + 1) * lane]
        total = jnp.zeros((length, lane), f32)
        for h in range(pack):
            keep = head_mask((length, lane), h, head_dim)
            s = dot(q, jnp.where(keep, k, jnp.zeros_like(k)), 1, 1) * 0.125 + bias_ref[g * pack + h]
            e = jnp.exp(s - jnp.max(s, axis=-1, keepdims=True))
            p = e / jnp.sum(e, axis=-1, keepdims=True)
            probs_ref[g * pack + h] = p
            total = total + dot(p.astype(bf16), jnp.where(keep, v, jnp.zeros_like(v)))
        mixed_ref[:, g * lane : (g + 1) * lane] = total.astype(bf16)
    res = x + dot(mixed_ref[...], full_ref[:, 3 * width :])
    res_ref[...] = res
    ffn_ref[...] = (res * inverse_rms(res) * gain_two_ref[...]).astype(bf16)


def expert_kernel(
    ids_ref, rows_ref, g_ref, wi_ref, wd_ref, router_ref,
    send_ref, y_ref, rows_out, hidden_out, dpre_out, dy_out,
):
    j = pl.program_id(0)
    count, per, width = rows_ref.shape
    total = count * per
    experts = router_ref.shape[1]
    x = rows_ref[...].reshape(total, width)
    rows_out[0] = x
    g = g_ref[:, :, :width].reshape(total, width).astype(f32)
    tags = g_ref[:, :, width:].reshape(total, lane).astype(f32)
    other, choice = tags[:, 0:1], tags[:, 1:2]
    logits = dot(x, router_ref[...])
    ids = lax.broadcasted_iota(jnp.int32, (total, experts), 1)
    own_logit = jnp.sum(jnp.where(ids == ids_ref[0] + j, logits, 0.0), -1, keepdims=True)
    other_logit = jnp.sum(jnp.where(ids.astype(f32) == other, logits, 0.0), -1, keepdims=True)
    gate = 1.0 / (1.0 + jnp.exp(other_logit - own_logit))
    d_y = (gate * g).astype(bf16)
    dy_out[0] = d_y
    pre = dot(x, wi_ref[0])
    square = pre * pre
    root = 0.7978845608028654
    gate_in = 0.5 + 0.5 * jnp.tanh(pre * (root + root * 0.044715 * square))
    hidden = (pre * gate_in).astype(bf16)
    hidden_out[0] = hidden
    slope = gate_in + gate_in * (1.0 - gate_in) * (
        pre * (2.0 * root + 6.0 * root * 0.044715 * square)
    )
    d_pre = (dot(d_y, wd_ref[0], 1, 1) * slope).astype(bf16)
    dpre_out[0] = d_pre
    at = pl.multiple_of(j * per, 16)
    d_rows = dot(d_pre, wi_ref[0], 1, 1).astype(bf16)
    send_ref[:, pl.ds(at, per), :width] = d_rows.reshape(count, per, width)
    y = dot(hidden, wd_ref[0])
    y_ref[:, pl.ds(at, per), :] = (gate * y).astype(bf16).reshape(count, per, width)
    d_gate = jnp.sum(g * y, axis=-1, keepdims=True)
    high = d_gate.astype(bf16).astype(f32)
    cols = lax.broadcasted_iota(jnp.int32, (total, lane), 1).astype(f32)
    tail = jnp.where(cols == choice, high, jnp.where(cols == choice + 2.0, d_gate - high, 0.0))
    send_ref[:, pl.ds(at, per), width:] = tail.astype(bf16).reshape(count, per, lane)


def collect_kernel(back_ref, hot_ref, own_ref, *refs):
    pay_refs, total_ref = refs[:-1], refs[-1]
    length = own_ref.shape[0]
    step = pl.program_id(0)
    got = dot(hot_ref[...], back_ref[...].reshape(-1, back_ref.shape[2]))

    @pl.when(step == 0)
    def _():
        total_ref[...] = got

    @pl.when(step > 0)
    def _():
        total_ref[...] += got

    @pl.when(step == pl.num_programs(0) - 1)
    def _():
        own_ref[...] = total_ref[:length, :]
        for k, ref in enumerate(pay_refs):
            ref[...] = total_ref[(k + 1) * length : (k + 2) * length, :].astype(bf16)


def collect(back, hot_back, length, flops=0):
    count, block, wide = back.shape
    step = math.lcm(block, lane) // block
    line = hot_back.shape[0] // length
    kinds = [f32] + [bf16] * (line - 1)
    return pl.pallas_call(
        collect_kernel,
        out_shape=[jax.ShapeDtypeStruct((length, wide), kind) for kind in kinds],
        grid=(count // step,),
        in_specs=[
            pl.BlockSpec((step, block, wide), lambda i: (i, 0, 0)),
            pl.BlockSpec((line * length, step * block), lambda i: (0, i)),
        ],
        out_specs=[pl.BlockSpec((length, wide), lambda i: (0, 0)) for _ in kinds],
        scratch_shapes=[pltpu.VMEM((line * length, wide), f32)],
        compiler_params=pltpu.CompilerParams(vmem_limit_bytes=32 << 20),
        cost_estimate=pl.CostEstimate(flops=flops, bytes_accessed=0, transcendentals=0),
    )(back, hot_back)


def backward_kernel(count, *refs):
    own_ref = refs[0]
    got_refs = refs[1 : 1 + count]
    (
        ffn_ref, res_ref, cot_ref, router_ref, routes_ref, gain_ref, full_ref, proj_ref, probs_ref,
        wide_ref, dres_ref, dlog_ref, gain_grad_ref, ds_ref, dproj_ref,
    ) = refs[1 + count :]
    length, width = ffn_ref.shape
    heads = probs_ref.shape[0]
    head_dim = width // heads
    pack = lane // head_dim
    experts = router_ref.shape[1]
    d = own_ref[...]
    for ref in got_refs:
        d = d + ref[...].astype(f32)
    tail = d[:, width:]
    d = d[:, :width]
    dg = [tail[:, i : i + 1] + tail[:, i + 2 : i + 3] for i in range(2)]
    logits = dot(ffn_ref[...], router_ref[...])
    e = jnp.exp(logits - jnp.max(logits, axis=-1, keepdims=True))
    router = e / jnp.sum(e, axis=-1, keepdims=True)
    ids = lax.broadcasted_iota(jnp.int32, (length, experts), 1)
    hots = [ids == routes_ref[:, i : i + 1] for i in range(2)]
    picked = [jnp.sum(jnp.where(h, router, 0.0), -1, keepdims=True) for h in hots]
    both = picked[0] + picked[1]
    mean = (dg[0] * picked[0] + dg[1] * picked[1]) / (both * both)
    d_router = sum(jnp.where(h, v / both - mean, 0.0) for h, v in zip(hots, dg))
    d_logits = router * (d_router - jnp.sum(router * d_router, -1, keepdims=True))
    d_logits = d_logits.astype(bf16)
    dlog_ref[...] = d_logits
    d_ffn = d + dot(d_logits, router_ref[...], 1, 1)
    res = res_ref[...]
    inv = inverse_rms(res)
    normed = res * inv
    gain_grad_ref[...] = jnp.sum(d_ffn * normed, axis=0, keepdims=True)
    d_norm = d_ffn * gain_ref[...]
    d_res = cot_ref[...].astype(f32) + inv * (
        d_norm - normed * jnp.mean(d_norm * normed, axis=-1, keepdims=True)
    )
    dres_ref[...] = d_res
    d_branch = d_res.astype(bf16)
    d_heads = dot(d_branch, full_ref[...], 1, 1).astype(bf16)
    for g in range(heads // pack):
        q = proj_ref[:, g * lane : (g + 1) * lane]
        k = proj_ref[:, width + g * lane : width + (g + 1) * lane]
        v = proj_ref[:, 2 * width + g * lane : 2 * width + (g + 1) * lane]
        dh = d_heads[:, g * lane : (g + 1) * lane]
        zero = jnp.zeros_like(q)
        sums = [jnp.zeros((length, lane), f32) for _ in range(3)]
        for h in range(pack):
            keep = head_mask((length, lane), h, head_dim)
            p = probs_ref[g * pack + h]
            dh_one = jnp.where(keep, dh, zero)
            d_probs = dot(dh_one, v, 1, 1)
            ds = p * (d_probs - jnp.sum(p * d_probs, axis=-1, keepdims=True))
            ds = ds.astype(bf16)
            ds_ref[g * pack + h] = ds.astype(f32)
            sums[0] = sums[0] + dot(ds, jnp.where(keep, k, zero))
            sums[1] = sums[1] + dot(ds, jnp.where(keep, q, zero), 0, 0)
            sums[2] = sums[2] + dot(p.astype(bf16), dh_one, 0, 0)
        for i, scale in enumerate((0.125, 0.125, 1.0)):
            dproj_ref[:, i * width + g * lane : i * width + (g + 1) * lane] = (sums[i] * scale).astype(bf16)
    columns = wide_ref.shape[2]
    split = 3 * width // columns
    for b in range(wide_ref.shape[0]):
        if b < split:
            wide_ref[b] = dproj_ref[:, b * columns : (b + 1) * columns]
        else:
            wide_ref[b] = d_branch[:, (b - split) * columns : (b - split + 1) * columns]


def product_kernel(ids_ref, own_ref, other_ref, wide_ref, small_ref, share_ref, *refs):
    pay_refs, order_ref, total_ref = refs[:-2], refs[-2], refs[-1]
    pairs, length, width = own_ref.shape
    e, s = ids_ref[0], ids_ref[1]
    count, part = small_ref.shape[0], width // small_ref.shape[0]
    for n in range(2):
        for i in range(pairs):
            at = (n * pairs + i) * length
            order_ref[at : at + length, :] = wide_ref[2 * i + ((e & 1) ^ n)]
    half = pairs * length
    total_ref[...] = dot(own_ref[...].reshape(half, width), order_ref[:half, :], 0, 0) + dot(
        other_ref[...].reshape(half, width), order_ref[half:, :], 0, 0
    )
    for k in range(count):
        target = lax.rem(s - k + count, count)
        rows = total_ref[pl.ds(pl.multiple_of(target * part, 16), part), :]
        ref = share_ref if k == 0 else pay_refs[k - 1]
        ref[:part, :] = rows.astype(ref.dtype)
        ref[part:, :] = small_ref[target].astype(ref.dtype)


def unpack_kernel(ids_ref, *refs):
    whole_refs, (qkv_ref, out_ref, small_ref) = refs[:-3], refs[-3:]
    part, width = out_ref.shape
    cols = small_ref.shape[1]
    split = 3 * width // cols
    pair = len(whole_refs)
    total = jnp.zeros(small_ref.shape, f32)
    for n, ref in enumerate(whole_refs):
        for i in range(ref.shape[0]):
            got = ref[i, :part, :].astype(f32)
            total = total + ref[i, part:, :].astype(f32)
            if pair * i < split:
                target, first = qkv_ref, pair * i
            else:
                target, first = out_ref, pair * i - split
            if pair == 1:
                target[:, first * cols : (first + 1) * cols] = got
            else:
                at = pl.multiple_of((first + ((ids_ref[0] & 1) ^ n)) * cols, lane)
                target[:, pl.ds(at, cols)] = got
    small_ref[...] = total


def tokens_kernel(
    dproj_ref, full_ref, tok_ref, gain_ref, dres_ref, ds_ref, ids_ref, out_ref, gain_grad_ref, table_ref
):
    ids = ids_ref[...]
    for b in range(table_ref.shape[0]):
        found = ids == b
        for h in range(table_ref.shape[1]):
            table_ref[b, h : h + 1, :] = jnp.sum(jnp.where(found, ds_ref[h], 0.0), axis=0, keepdims=True)
    d_in = dot(dproj_ref[...], full_ref[...], 1, 1)
    x = tok_ref[...].astype(f32)
    inv = inverse_rms(x)
    normed = x * inv
    gain_grad_ref[...] = jnp.sum(d_in * normed, axis=0, keepdims=True)
    d_norm = d_in * gain_ref[...]
    out_ref[...] = dres_ref[...] + inv * (
        d_norm - normed * jnp.mean(d_norm * normed, axis=-1, keepdims=True)
    )


def body(
    tokens,
    w_qkv,
    w_out,
    w_router,
    gain_attn,
    gain_ffn,
    bias_table,
    w_in,
    w_down,
    routes,
    slots,
    bucket_ids,
    cotangent,
):
    length, width = tokens.shape
    ne = lax.axis_size("expert")
    ns = lax.axis_size("shard")
    me_e = lax.axis_index("expert")
    me_s = lax.axis_index("shard")
    place_ids = jnp.stack([me_e, me_s]).astype(jnp.int32)
    exp_dev = w_in.shape[0]
    hidden_units = w_in.shape[2]
    experts = exp_dev * ne
    cap = 3 * length // experts
    per = ns * cap
    block = exp_dev * per
    total_rows = ne * block
    group_rows = ne * per
    heads = bias_table.shape[1]
    buckets = bias_table.shape[0] * ns
    part = width // ns

    def from_shift(v, k):
        return lax.ppermute(v, "shard", [(i, (i + k) % ns) for i in range(ns)])

    def to_shift(v, k):
        return lax.ppermute(v, "shard", [(i, (i - k) % ns) for i in range(ns)])

    def plane(v):
        return lax.all_to_all(v, "expert", split_axis=0, concat_axis=0, tiled=True)

    def across(v, bit):
        return lax.ppermute(v, "expert", [(i, i ^ bit) for i in range(ne)])

    cols = width // 2
    mine = me_e & 7
    weight = jnp.where(
        mine < 6,
        lax.dynamic_slice_in_dim(w_qkv, jnp.minimum(mine, 5) * cols, cols, 1),
        lax.dynamic_slice_in_dim(w_out, (jnp.maximum(mine, 6) - 6) * cols, cols, 1),
    )
    line = [weight] + [from_shift(weight, k) for k in range(1, ns)]

    smalls = (w_router, gain_attn, gain_ffn, bias_table, routes.astype(bf16), slots.astype(bf16))
    small = jnp.concatenate([v.reshape(-1) for v in smalls])
    small_rows = -(-small.size // lane)
    small_rows += -small_rows % 16
    small = jnp.pad(small, (0, small_rows * lane - small.size)).reshape(1, small_rows, lane)
    in_order = lax.all_to_all(
        jnp.broadcast_to(small, (ns, small_rows, lane)), "shard", split_axis=0, concat_axis=0, tiled=True
    ).reshape(ns, small_rows * lane)
    cotangent, line = lax.optimization_barrier((cotangent, line))
    pieces = []
    for half, bits in ((line[: ns // 2], (2, 4)), (line[ns // 2 :], (4, 2))):
        held = jnp.stack(half)[None]
        held = jnp.concatenate([held, across(held, bits[0])], axis=0)
        pieces.append((held, across(held, 1), across(held, bits[1])))

    line_g = [cotangent] + [from_shift(cotangent, k) for k in range(1, ns)]
    order = lax.rem(me_s - jnp.arange(ns, dtype=jnp.int32) + ns, ns)
    line_small = jnp.take(in_order, order, axis=0)

    cuts = []
    at = 0
    for v in smalls:
        cuts.append((at, at + v.size))
        at += v.size

    def cut(v, i):
        return v[:, cuts[i][0] : cuts[i][1]]

    full_router = cut(in_order, 0).reshape(width, experts)
    gain_one = cut(in_order, 1).reshape(1, width).astype(f32)
    gain_two = cut(in_order, 2).reshape(1, width).astype(f32)
    table = cut(in_order, 3).reshape(buckets, heads)
    line_g, table, gain_one, gain_two = lax.optimization_barrier((line_g, table, gain_one, gain_two))
    line_routes = cut(line_small, 4).reshape(ns * length, 2)
    line_slots = cut(line_small, 5).reshape(ns * length, 2).astype(jnp.int32)
    place = (
        line_routes.astype(jnp.int32) * per + jnp.repeat(order, length)[:, None] * cap + line_slots
    )
    causal = jnp.arange(length)[:, None] >= jnp.arange(length)[None, :]
    bucket_hot = (
        jnp.arange(buckets, dtype=jnp.int32)[:, None] == bucket_ids.reshape(1, -1)
    ).astype(bf16)
    pair_bias = dot(table, bucket_hot, 0, 0).reshape(heads, length, length)
    pair_bias = jnp.where(causal[None], pair_bias, -1e30)
    hot, hot_back, tags = local_call(
        tables_kernel,
        [((total_rows, ns * length), bf16), ((ns * length, total_rows), bf16), ((total_rows, lane), bf16)],
        [place.T, place, line_routes],
    )
    g_rows = spread(hot, line_g, (ne, block, width + lane), tags)
    last = [p[2] for p in pieces]
    pair_bias, g_rows, last, gain_one, gain_two, place_ids = lax.optimization_barrier(
        (pair_bias, g_rows, last, gain_one, gain_two, place_ids)
    )
    g_arrived = plane(g_rows)
    pieces = [v for p, q in zip(pieces, last) for v in (p[0], p[1], q, across(q, 1))]
    attn_in, proj, probs, mixed_low, residual, ffn_in, full = local_call(
        attend_kernel,
        [
            ((length, width), bf16),
            ((length, 3 * width), bf16),
            ((heads, length, length), f32),
            ((length, width), bf16),
            ((length, width), f32),
            ((length, width), bf16),
            ((width, 4 * width), bf16),
        ],
        [place_ids, tokens, gain_one, gain_two, pair_bias, *pieces],
        scalars=1,
    )

    line_ffn = [ffn_in] + [from_shift(ffn_in, k) for k in range(1, ns)]
    line_ffn, g_arrived = lax.optimization_barrier((line_ffn, g_arrived))
    sent = spread(hot, line_ffn, (ne, block, width))
    arrived = plane(sent)
    split_e = 3 * ne // 4
    same = [list(range(c, ne, 2)) for c in range(2)]
    factors = jnp.stack([attn_in] * (split_e // 2) + [mixed_low] * ((ne - split_e) // 2))
    arrived, factors = lax.optimization_barrier((arrived, factors))
    held = lax.all_to_all(
        factors, "expert", split_axis=0, concat_axis=0, axis_index_groups=same, tiled=True
    )

    wide_width = width + lane
    first_id = (me_e * exp_dev).astype(jnp.int32).reshape(1)
    send, y_send, rows, hidden, d_pre, d_y = pl.pallas_call(
        expert_kernel,
        out_shape=[
            jax.ShapeDtypeStruct((ne, block, wide_width), bf16),
            jax.ShapeDtypeStruct((ne, block, width), bf16),
            jax.ShapeDtypeStruct((exp_dev, group_rows, width), bf16),
            jax.ShapeDtypeStruct((exp_dev, group_rows, hidden_units), bf16),
            jax.ShapeDtypeStruct((exp_dev, group_rows, hidden_units), bf16),
            jax.ShapeDtypeStruct((exp_dev, group_rows, width), bf16),
        ],
        grid=(exp_dev,),
        in_specs=[
            pl.BlockSpec(memory_space=pltpu.SMEM),
            pl.BlockSpec((ne, per, width), lambda j: (0, j, 0)),
            pl.BlockSpec((ne, per, wide_width), lambda j: (0, j, 0)),
            pl.BlockSpec((1, width, hidden_units), lambda j: (j, 0, 0)),
            pl.BlockSpec((1, hidden_units, width), lambda j: (j, 0, 0)),
            pl.BlockSpec((width, experts), lambda j: (0, 0)),
        ],
        out_specs=[
            pl.BlockSpec((ne, block, wide_width), lambda j: (0, 0, 0)),
            pl.BlockSpec((ne, block, width), lambda j: (0, 0, 0)),
            pl.BlockSpec((1, group_rows, width), lambda j: (j, 0, 0)),
            pl.BlockSpec((1, group_rows, hidden_units), lambda j: (j, 0, 0)),
            pl.BlockSpec((1, group_rows, hidden_units), lambda j: (j, 0, 0)),
            pl.BlockSpec((1, group_rows, width), lambda j: (j, 0, 0)),
        ],
        compiler_params=pltpu.CompilerParams(vmem_limit_bytes=56 << 20),
        cost_estimate=pl.CostEstimate(
            flops=8 * exp_dev * group_rows * width * hidden_units,
            bytes_accessed=16 * exp_dev * group_rows * width,
            transcendentals=0,
        ),
    )(first_id, arrived, g_arrived, w_in, w_down, full_router)
    send, held = lax.optimization_barrier((send, held))
    held_other = across(held, 1)
    d_back = plane(send)
    grad_w_down = jnp.einsum("jrf,jrd->jfd", hidden, d_y, preferred_element_type=f32)
    grad_w_in = jnp.einsum("jrd,jrf->jdf", rows, d_pre, preferred_element_type=f32)
    d_back, grad_w_down, grad_w_in = lax.optimization_barrier((d_back, grad_w_down, grad_w_in))

    own_d, *pays = collect(d_back, hot_back, length, 2 * ns * length * total_rows * wide_width)
    got = [to_shift(v, k + 1) for k, v in enumerate(pays)]
    pays, y_send = lax.optimization_barrier((pays, y_send))
    y_back = plane(y_send)
    columns = 4 * width // ne
    wide, d_residual, d_logits, gain_two_grad, d_scores, d_proj = local_call(
        functools.partial(backward_kernel, ns - 1),
        [
            ((ne, length, columns), bf16),
            ((length, width), f32),
            ((length, experts), bf16),
            ((1, width), f32),
            ((heads, length, length), f32),
            ((length, 3 * width), bf16),
        ],
        [own_d, *got, ffn_in, residual, cotangent, full_router, routes, gain_two, full, proj, probs],
        views={ns + 6: ((width, width), (0, 3))},
        flops=2 * length * width * width + 10 * heads * length * length * lane,
        moved=2 * width * width + 8 * heads * length * length,
    )
    wide, y_back = lax.optimization_barrier((wide, y_back))
    wide = plane(wide)
    grad_tokens, gain_one_grad, grad_table = local_call(
        tokens_kernel,
        [((length, width), f32), ((1, width), f32), ((buckets, heads, lane), f32)],
        [d_proj, full, tokens, gain_one, d_residual, d_scores, bucket_ids],
        views={1: ((width, 3 * width), (0, 0))},
    )
    grad_router = dot(ffn_in, d_logits, 0, 0)

    small_parts = [
        grad_router.reshape(ns, -1),
        gain_one_grad.reshape(ns, -1),
        gain_two_grad.reshape(ns, -1),
        jnp.sum(grad_table, axis=-1).reshape(ns, -1),
    ]
    sizes = [v.shape[1] for v in small_parts]
    small = jnp.concatenate(small_parts, axis=1).astype(bf16)
    each = small.shape[1]
    srows = -(-each // columns)
    srows += -srows % 16
    room = srows * columns
    small = jnp.pad(small, ((0, 0), (0, room - each))).reshape(ns, srows, columns)
    share, *products = local_call(
        product_kernel,
        [((part + srows, columns), f32)] + [((part + srows, columns), bf16)] * (ns - 1),
        [place_ids, held, held_other, wide, small],
        scalars=1,
        scratch=[pltpu.VMEM((ne * length, columns), bf16), pltpu.VMEM((width, columns), f32)],
        flops=2 * ne * length * width * columns,
        moved=2 * ne * length * (width + columns),
    )
    products, y_back = lax.optimization_barrier((products, y_back))
    y_own, *y_pays = collect(y_back, hot_back, length)
    y_own = residual + y_own
    for k, v in enumerate(products):
        share = share + to_shift(v, k + 1).astype(f32)
    share, y_pays = lax.optimization_barrier((share.astype(bf16), y_pays))
    y_got = [to_shift(v, k + 1) for k, v in enumerate(y_pays)]
    by_core = columns % lane == 0
    if by_core:
        copies = jnp.broadcast_to(share[None], (ne // 2,) + share.shape)
        whole = lax.all_to_all(
            copies, "expert", split_axis=0, concat_axis=0, axis_index_groups=same, tiled=True
        )
        whole, y_got[1] = lax.optimization_barrier((whole, y_got[1]))
        whole = [whole, across(whole, 1)]
    else:
        whole = [plane(jnp.broadcast_to(share[None], (ne,) + share.shape))]
    out_qkv, out_out, small = local_call(
        unpack_kernel,
        [((part, 3 * width), f32), ((part, width), f32), ((srows, columns), f32)],
        [place_ids, *whole],
        scalars=1,
    )
    y_own, small = lax.optimization_barrier((y_own, small.reshape(-1)))
    smalls = []
    at = 0
    for size in sizes:
        smalls.append(small[at : at + size])
        at += size

    for v in y_got:
        y_own = y_own + v.astype(f32)
    return (
        y_own.astype(bf16),
        grad_tokens,
        out_qkv,
        out_out,
        smalls[0].reshape(part, experts),
        smalls[1],
        smalls[2],
        smalls[3].reshape(buckets // ns, heads),
        grad_w_in,
        grad_w_down,
    )


def solution(mesh):
    in_specs = (
        P(("expert", "shard"), None),
        P("shard", None),
        P("shard", None),
        P("shard", None),
        P("shard"),
        P("shard"),
        P("shard", None),
        P("expert", None, "shard"),
        P("expert", "shard", None),
        P(("expert", "shard"), None),
        P(("expert", "shard"), None),
        P(),
        P(("expert", "shard"), None),
    )
    out_specs = (
        P(("expert", "shard"), None),
        P(("expert", "shard"), None),
        P("shard", None),
        P("shard", None),
        P("shard", None),
        P("shard"),
        P("shard"),
        P("shard", None),
        P("expert", None, "shard"),
        P("expert", "shard", None),
    )
    return jax.shard_map(body, mesh=mesh, in_specs=in_specs, out_specs=out_specs, check_vma=False)
```

```python
import functools
import math

import jax
import jax.numpy as jnp
from jax import lax
from jax.experimental import pallas as pl
from jax.experimental.pallas import tpu as pltpu
from jax.sharding import PartitionSpec as P

norm_eps = 1e-06
f32 = jnp.float32
bf16 = jnp.bfloat16
lane = 128


def inverse_rms(values):
    return lax.rsqrt(jnp.mean(values * values, axis=-1, keepdims=True) + norm_eps)


def dot(a, b, ca=1, cb=0):
    return lax.dot_general(a, b, (((ca,), (cb,)), ((), ())), preferred_element_type=f32)


def split_two(v):
    high = v.astype(bf16)
    return high, (v - high.astype(f32)).astype(bf16)


def local_call(kernel, outs, args, scalars=0, views=None, scratch=(), direct=False, flops=0, moved=0):
    def block(shape, where=None):
        where = where or (0,) * len(shape)
        return pl.BlockSpec(shape, lambda i: where)

    specs = [pl.BlockSpec(memory_space=pltpu.SMEM)] * scalars
    specs += [pl.BlockSpec(memory_space=pltpu.VMEM) if direct else block(v.shape) for v in args[scalars:]]
    for n, (shape, where) in (views or {}).items():
        specs[n] = block(shape, where)
    return pl.pallas_call(
        kernel,
        out_shape=[jax.ShapeDtypeStruct(shape, kind) for shape, kind in outs],
        grid=(1,),
        in_specs=specs,
        out_specs=[block(shape) for shape, _ in outs],
        scratch_shapes=list(scratch),
        compiler_params=pltpu.CompilerParams(vmem_limit_bytes=56 << 20),
        cost_estimate=pl.CostEstimate(flops=flops, bytes_accessed=moved, transcendentals=0),
    )(*args)


def join_blocks(e, s, parts, full_ref):
    count = 2 * parts[0].shape[1]
    rows, cols = parts[0].shape[2], parts[0].shape[3]
    for n, ref in enumerate(parts):
        bits = ((2, 4), (4, 2))[n // 4]
        for i in range(ref.shape[0]):
            differ = i * bits[0] + (n // 2 % 2) * bits[1] + n % 2
            col = pl.multiple_of(((e & 7) ^ differ) * cols, lane)
            for q in range(count // 2):
                source = lax.rem(s - (q + (n // 4) * (count // 2)) + count, count)
                row = pl.multiple_of(source * rows, 16)
                full_ref[pl.ds(row, rows), pl.ds(col, cols)] = ref[i, q]


def head_mask(shape, h, head_dim):
    return lax.broadcasted_iota(jnp.int32, shape, 1) // head_dim == h


def tables_kernel(row_ref, col_ref, route_ref, hot_ref, back_ref, tag_ref):
    total, tokens = hot_ref.shape
    one, zero = jnp.ones((), f32), jnp.zeros((), f32)
    ids = lax.broadcasted_iota(jnp.int32, (total, tokens), 0)
    hots = [jnp.where(ids == row_ref[i : i + 1, :], one, zero).astype(bf16) for i in range(2)]
    hot_ref[...] = hots[0] + hots[1]
    ids = lax.broadcasted_iota(jnp.int32, (tokens, total), 1)
    found = (ids == col_ref[:, 0:1]) | (ids == col_ref[:, 1:2])
    back_ref[...] = jnp.where(found, one, zero).astype(bf16)
    cols = lax.broadcasted_iota(jnp.int32, (tokens, lane), 1)
    tags = zero
    for i in range(2):
        tag = jnp.where(cols == 0, route_ref[:, 1 - i : 2 - i].astype(f32), jnp.where(cols == 1, float(i), 0.0))
        tags = tags + dot(hots[i], tag.astype(bf16))
    tag_ref[...] = tags.astype(bf16)


def spread_kernel(hot_ref, *refs):
    out_ref, rows_ref = refs[-2:]
    count, block, wide = out_ref.shape
    length, width = refs[0].shape
    line_refs = refs[: rows_ref.shape[0] // length]

    @pl.when(pl.program_id(0) == 0)
    def _():
        for k, ref in enumerate(line_refs):
            rows_ref[k * length : (k + 1) * length, :] = ref[...]

    out_ref[:, :, :width] = dot(hot_ref[...], rows_ref[...]).astype(bf16).reshape(count, block, width)
    if wide > width:
        out_ref[:, :, width:] = refs[-3][...].reshape(count, block, lane)


def spread(hot, line, shape, tags=None):
    length, width = line[0].shape
    count, block, wide = shape
    rows = 2 * block
    specs = [pl.BlockSpec((rows, hot.shape[1]), lambda i: (i, 0))]
    specs += [pl.BlockSpec((length, width), lambda i: (0, 0))] * len(line)
    args = [hot, *line]
    if tags is not None:
        specs.append(pl.BlockSpec((rows, lane), lambda i: (i, 0)))
        args.append(tags)
    return pl.pallas_call(
        spread_kernel,
        out_shape=jax.ShapeDtypeStruct(shape, bf16),
        grid=(count // 2,),
        in_specs=specs,
        out_specs=pl.BlockSpec((2, block, wide), lambda i: (i, 0, 0)),
        scratch_shapes=[pltpu.VMEM((len(line) * length, width), bf16)],
        compiler_params=pltpu.CompilerParams(vmem_limit_bytes=32 << 20),
        cost_estimate=pl.CostEstimate(flops=0, bytes_accessed=0, transcendentals=0),
    )(*args)


def attend_kernel(
    ids_ref, tok_ref, gain_ref, gain_two_ref, bias_ref, *refs,
):
    attn_ref, proj_ref, probs_ref, mixed_ref, res_ref, ffn_ref, full_ref = refs[-7:]
    join_blocks(ids_ref[0], ids_ref[1], refs[:-7], full_ref)
    length, width = tok_ref.shape
    heads = bias_ref.shape[0]
    head_dim = width // heads
    pack = lane // head_dim
    x = tok_ref[...].astype(f32)
    low = (x * inverse_rms(x) * gain_ref[...]).astype(bf16)
    attn_ref[...] = low
    step = width // 2
    for c in range(6):
        cols = slice(c * step, (c + 1) * step)
        proj_ref[:, cols] = dot(low, full_ref[:, cols]).astype(bf16)
    for g in range(heads // pack):
        q = proj_ref[:, g * lane : (g + 1) * lane]
        k = proj_ref[:, width + g * lane : width + (g + 1) * lane]
        v = proj_ref[:, 2 * width + g * lane : 2 * width + (g + 1) * lane]
        total = jnp.zeros((length, lane), f32)
        for h in range(pack):
            keep = head_mask((length, lane), h, head_dim)
            s = dot(q, jnp.where(keep, k, jnp.zeros_like(k)), 1, 1) * 0.125 + bias_ref[g * pack + h]
            e = jnp.exp(s - jnp.max(s, axis=-1, keepdims=True))
            p = e / jnp.sum(e, axis=-1, keepdims=True)
            probs_ref[g * pack + h] = p
            total = total + dot(p.astype(bf16), jnp.where(keep, v, jnp.zeros_like(v)))
        mixed_ref[:, g * lane : (g + 1) * lane] = total.astype(bf16)
    res = x + dot(mixed_ref[...], full_ref[:, 3 * width :])
    res_ref[...] = res
    ffn_ref[...] = (res * inverse_rms(res) * gain_two_ref[...]).astype(bf16)


def expert_kernel(
    ids_ref, rows_ref, g_ref, wi_ref, wd_ref, router_ref,
    send_ref, y_ref, rows_out, hidden_out, dpre_out, dy_out,
):
    j = pl.program_id(0)
    count, per, width = rows_ref.shape
    total = count * per
    experts = router_ref.shape[1]
    x = rows_ref[...].reshape(total, width)
    rows_out[0] = x
    g = g_ref[:, :, :width].reshape(total, width).astype(f32)
    tags = g_ref[:, :, width:].reshape(total, lane).astype(f32)
    other, choice = tags[:, 0:1], tags[:, 1:2]
    logits = dot(x, router_ref[...])
    ids = lax.broadcasted_iota(jnp.int32, (total, experts), 1)
    own_logit = jnp.sum(jnp.where(ids == ids_ref[0] + j, logits, 0.0), -1, keepdims=True)
    other_logit = jnp.sum(jnp.where(ids.astype(f32) == other, logits, 0.0), -1, keepdims=True)
    gate = 1.0 / (1.0 + jnp.exp(other_logit - own_logit))
    d_y = (gate * g).astype(bf16)
    dy_out[0] = d_y
    pre = dot(x, wi_ref[0])
    square = pre * pre
    root = 0.7978845608028654
    gate_in = 0.5 + 0.5 * jnp.tanh(pre * (root + root * 0.044715 * square))
    hidden = (pre * gate_in).astype(bf16)
    hidden_out[0] = hidden
    slope = gate_in + gate_in * (1.0 - gate_in) * (
        pre * (2.0 * root + 6.0 * root * 0.044715 * square)
    )
    d_pre = (dot(d_y, wd_ref[0], 1, 1) * slope).astype(bf16)
    dpre_out[0] = d_pre
    d_rows = dot(d_pre, wi_ref[0], 1, 1).astype(bf16)
    send_ref[:, :, :width] = d_rows.reshape(count, per, width)
    y = dot(hidden, wd_ref[0])
    y_ref[...] = (gate * y).astype(bf16).reshape(count, per, width)
    d_gate = jnp.sum(g * y, axis=-1, keepdims=True)
    high = d_gate.astype(bf16).astype(f32)
    cols = lax.broadcasted_iota(jnp.int32, (total, lane), 1).astype(f32)
    tail = jnp.where(cols == choice, high, jnp.where(cols == choice + 2.0, d_gate - high, 0.0))
    send_ref[:, :, width:] = tail.astype(bf16).reshape(count, per, lane)


def collect_kernel(back_ref, hot_ref, own_ref, *refs):
    pay_refs, total_ref = refs[:-1], refs[-1]
    length = own_ref.shape[0]
    step = pl.program_id(0)
    got = dot(hot_ref[...], back_ref[...].reshape(-1, back_ref.shape[2]))

    @pl.when(step == 0)
    def _():
        total_ref[...] = got

    @pl.when(step > 0)
    def _():
        total_ref[...] += got

    @pl.when(step == pl.num_programs(0) - 1)
    def _():
        own_ref[...] = total_ref[:length, :]
        for k, ref in enumerate(pay_refs):
            ref[...] = total_ref[(k + 1) * length : (k + 2) * length, :].astype(bf16)


def collect(back, hot_back, length, flops=0):
    count, block, wide = back.shape
    step = math.lcm(block, lane) // block
    line = hot_back.shape[0] // length
    kinds = [f32] + [bf16] * (line - 1)
    return pl.pallas_call(
        collect_kernel,
        out_shape=[jax.ShapeDtypeStruct((length, wide), kind) for kind in kinds],
        grid=(count // step,),
        in_specs=[
            pl.BlockSpec((step, block, wide), lambda i: (i, 0, 0)),
            pl.BlockSpec((line * length, step * block), lambda i: (0, i)),
        ],
        out_specs=[pl.BlockSpec((length, wide), lambda i: (0, 0)) for _ in kinds],
        scratch_shapes=[pltpu.VMEM((line * length, wide), f32)],
        compiler_params=pltpu.CompilerParams(vmem_limit_bytes=32 << 20),
        cost_estimate=pl.CostEstimate(flops=flops, bytes_accessed=0, transcendentals=0),
    )(back, hot_back)


def backward_kernel(count, *refs):
    own_ref = refs[0]
    got_refs = refs[1 : 1 + count]
    (
        ffn_ref, res_ref, cot_ref, router_ref, routes_ref, gain_ref, full_ref, proj_ref, probs_ref,
        wide_ref, dres_ref, dlog_ref, gain_grad_ref, ds_ref, dproj_ref,
    ) = refs[1 + count :]
    length, width = ffn_ref.shape
    heads = probs_ref.shape[0]
    head_dim = width // heads
    pack = lane // head_dim
    experts = router_ref.shape[1]
    d = own_ref[...]
    for ref in got_refs:
        d = d + ref[...].astype(f32)
    tail = d[:, width:]
    d = d[:, :width]
    dg = [tail[:, i : i + 1] + tail[:, i + 2 : i + 3] for i in range(2)]
    logits = dot(ffn_ref[...], router_ref[...])
    e = jnp.exp(logits - jnp.max(logits, axis=-1, keepdims=True))
    router = e / jnp.sum(e, axis=-1, keepdims=True)
    ids = lax.broadcasted_iota(jnp.int32, (length, experts), 1)
    hots = [ids == routes_ref[:, i : i + 1] for i in range(2)]
    picked = [jnp.sum(jnp.where(h, router, 0.0), -1, keepdims=True) for h in hots]
    both = picked[0] + picked[1]
    mean = (dg[0] * picked[0] + dg[1] * picked[1]) / (both * both)
    d_router = sum(jnp.where(h, v / both - mean, 0.0) for h, v in zip(hots, dg))
    d_logits = router * (d_router - jnp.sum(router * d_router, -1, keepdims=True))
    d_logits = d_logits.astype(bf16)
    dlog_ref[...] = d_logits
    d_ffn = d + dot(d_logits, router_ref[...], 1, 1)
    res = res_ref[...]
    inv = inverse_rms(res)
    normed = res * inv
    gain_grad_ref[...] = jnp.sum(d_ffn * normed, axis=0, keepdims=True)
    d_norm = d_ffn * gain_ref[...]
    d_res = cot_ref[...].astype(f32) + inv * (
        d_norm - normed * jnp.mean(d_norm * normed, axis=-1, keepdims=True)
    )
    dres_ref[...] = d_res
    d_branch = d_res.astype(bf16)
    d_heads = dot(d_branch, full_ref[...], 1, 1).astype(bf16)
    for g in range(heads // pack):
        q = proj_ref[:, g * lane : (g + 1) * lane]
        k = proj_ref[:, width + g * lane : width + (g + 1) * lane]
        v = proj_ref[:, 2 * width + g * lane : 2 * width + (g + 1) * lane]
        dh = d_heads[:, g * lane : (g + 1) * lane]
        zero = jnp.zeros_like(q)
        sums = [jnp.zeros((length, lane), f32) for _ in range(3)]
        for h in range(pack):
            keep = head_mask((length, lane), h, head_dim)
            p = probs_ref[g * pack + h]
            dh_one = jnp.where(keep, dh, zero)
            d_probs = dot(dh_one, v, 1, 1)
            ds = p * (d_probs - jnp.sum(p * d_probs, axis=-1, keepdims=True))
            ds = ds.astype(bf16)
            ds_ref[g * pack + h] = ds.astype(f32)
            sums[0] = sums[0] + dot(ds, jnp.where(keep, k, zero))
            sums[1] = sums[1] + dot(ds, jnp.where(keep, q, zero), 0, 0)
            sums[2] = sums[2] + dot(p.astype(bf16), dh_one, 0, 0)
        for i, scale in enumerate((0.125, 0.125, 1.0)):
            dproj_ref[:, i * width + g * lane : i * width + (g + 1) * lane] = (sums[i] * scale).astype(bf16)
    columns = wide_ref.shape[2]
    split = 3 * width // columns
    for b in range(wide_ref.shape[0]):
        if b < split:
            wide_ref[b] = dproj_ref[:, b * columns : (b + 1) * columns]
        else:
            wide_ref[b] = d_branch[:, (b - split) * columns : (b - split + 1) * columns]


def product_kernel(ids_ref, own_ref, other_ref, wide_ref, small_ref, share_ref, *refs):
    pay_refs, order_ref, total_ref = refs[:-2], refs[-2], refs[-1]
    pairs, length, width = own_ref.shape
    e, s = ids_ref[0], ids_ref[1]
    count, part = small_ref.shape[0], width // small_ref.shape[0]
    for n in range(2):
        for i in range(pairs):
            at = (n * pairs + i) * length
            order_ref[at : at + length, :] = wide_ref[2 * i + ((e & 1) ^ n)]
    half = pairs * length
    total_ref[...] = dot(own_ref[...].reshape(half, width), order_ref[:half, :], 0, 0) + dot(
        other_ref[...].reshape(half, width), order_ref[half:, :], 0, 0
    )
    for k in range(count):
        target = lax.rem(s - k + count, count)
        rows = total_ref[pl.ds(pl.multiple_of(target * part, 16), part), :]
        ref = share_ref if k == 0 else pay_refs[k - 1]
        ref[:part, :] = rows.astype(ref.dtype)
        ref[part:, :] = small_ref[target].astype(ref.dtype)


def unpack_kernel(ids_ref, *refs):
    whole_refs, (qkv_ref, out_ref, small_ref) = refs[:-3], refs[-3:]
    part, width = out_ref.shape
    cols = small_ref.shape[1]
    split = 3 * width // cols
    pair = len(whole_refs)
    total = jnp.zeros(small_ref.shape, f32)
    for n, ref in enumerate(whole_refs):
        for i in range(ref.shape[0]):
            got = ref[i, :part, :].astype(f32)
            total = total + ref[i, part:, :].astype(f32)
            if pair * i < split:
                target, first = qkv_ref, pair * i
            else:
                target, first = out_ref, pair * i - split
            if pair == 1:
                target[:, first * cols : (first + 1) * cols] = got
            else:
                at = pl.multiple_of((first + ((ids_ref[0] & 1) ^ n)) * cols, lane)
                target[:, pl.ds(at, cols)] = got
    small_ref[...] = total


def tokens_kernel(
    dproj_ref, full_ref, tok_ref, gain_ref, dres_ref, ds_ref, ids_ref, out_ref, gain_grad_ref, table_ref
):
    ids = ids_ref[...]
    for b in range(table_ref.shape[0]):
        found = ids == b
        for h in range(table_ref.shape[1]):
            table_ref[b, h : h + 1, :] = jnp.sum(jnp.where(found, ds_ref[h], 0.0), axis=0, keepdims=True)
    d_in = dot(dproj_ref[...], full_ref[...], 1, 1)
    x = tok_ref[...].astype(f32)
    inv = inverse_rms(x)
    normed = x * inv
    gain_grad_ref[...] = jnp.sum(d_in * normed, axis=0, keepdims=True)
    d_norm = d_in * gain_ref[...]
    out_ref[...] = dres_ref[...] + inv * (
        d_norm - normed * jnp.mean(d_norm * normed, axis=-1, keepdims=True)
    )


def body(
    tokens,
    w_qkv,
    w_out,
    w_router,
    gain_attn,
    gain_ffn,
    bias_table,
    w_in,
    w_down,
    routes,
    slots,
    bucket_ids,
    cotangent,
):
    length, width = tokens.shape
    ne = lax.axis_size("expert")
    ns = lax.axis_size("shard")
    me_e = lax.axis_index("expert")
    me_s = lax.axis_index("shard")
    place_ids = jnp.stack([me_e, me_s]).astype(jnp.int32)
    exp_dev = w_in.shape[0]
    hidden_units = w_in.shape[2]
    experts = exp_dev * ne
    cap = 3 * length // experts
    per = ns * cap
    block = exp_dev * per
    total_rows = ne * block
    group_rows = ne * per
    heads = bias_table.shape[1]
    buckets = bias_table.shape[0] * ns
    part = width // ns

    def from_shift(v, k):
        return lax.ppermute(v, "shard", [(i, (i + k) % ns) for i in range(ns)])

    def to_shift(v, k):
        return lax.ppermute(v, "shard", [(i, (i - k) % ns) for i in range(ns)])

    def plane(v):
        return lax.all_to_all(v, "expert", split_axis=0, concat_axis=0, tiled=True)

    def across(v, bit):
        return lax.ppermute(v, "expert", [(i, i ^ bit) for i in range(ne)])

    cols = width // 2
    mine = me_e & 7
    weight = jnp.where(
        mine < 6,
        lax.dynamic_slice_in_dim(w_qkv, jnp.minimum(mine, 5) * cols, cols, 1),
        lax.dynamic_slice_in_dim(w_out, (jnp.maximum(mine, 6) - 6) * cols, cols, 1),
    )
    line = [weight] + [from_shift(weight, k) for k in range(1, ns)]

    smalls = (w_router, gain_attn, gain_ffn, bias_table, routes.astype(bf16), slots.astype(bf16))
    small = jnp.concatenate([v.reshape(-1) for v in smalls])
    small_rows = -(-small.size // lane)
    small_rows += -small_rows % 16
    small = jnp.pad(small, (0, small_rows * lane - small.size)).reshape(1, small_rows, lane)
    in_order = lax.all_to_all(
        jnp.broadcast_to(small, (ns, small_rows, lane)), "shard", split_axis=0, concat_axis=0, tiled=True
    ).reshape(ns, small_rows * lane)
    cotangent, line = lax.optimization_barrier((cotangent, line))
    halves = []
    for half, bit in ((line[: ns // 2], 2), (line[ns // 2 :], 4)):
        held = jnp.stack(half)[None]
        halves.append(jnp.concatenate([held, across(held, bit)], axis=0))
    halves, in_order = lax.optimization_barrier((halves, in_order))
    pieces = [(v, across(v, bit)) for v, bit in zip(halves, (4, 2))]

    line_g = [cotangent] + [from_shift(cotangent, k) for k in range(1, ns)]
    order = lax.rem(me_s - jnp.arange(ns, dtype=jnp.int32) + ns, ns)
    line_small = jnp.take(in_order, order, axis=0)

    cuts = []
    at = 0
    for v in smalls:
        cuts.append((at, at + v.size))
        at += v.size

    def cut(v, i):
        return v[:, cuts[i][0] : cuts[i][1]]

    full_router = cut(in_order, 0).reshape(width, experts)
    gain_one = cut(in_order, 1).reshape(1, width).astype(f32)
    gain_two = cut(in_order, 2).reshape(1, width).astype(f32)
    table = cut(in_order, 3).reshape(buckets, heads)
    line_g, table, gain_one, gain_two = lax.optimization_barrier((line_g, table, gain_one, gain_two))
    line_routes = cut(line_small, 4).reshape(ns * length, 2)
    line_slots = cut(line_small, 5).reshape(ns * length, 2).astype(jnp.int32)
    place = (
        line_routes.astype(jnp.int32) * per + jnp.repeat(order, length)[:, None] * cap + line_slots
    )
    causal = jnp.arange(length)[:, None] >= jnp.arange(length)[None, :]
    bucket_hot = (
        jnp.arange(buckets, dtype=jnp.int32)[:, None] == bucket_ids.reshape(1, -1)
    ).astype(bf16)
    pair_bias = dot(table, bucket_hot, 0, 0).reshape(heads, length, length)
    pair_bias = jnp.where(causal[None], pair_bias, -1e30)
    hot, hot_back, tags = local_call(
        tables_kernel,
        [((total_rows, ns * length), bf16), ((ns * length, total_rows), bf16), ((total_rows, lane), bf16)],
        [place.T, place, line_routes],
    )
    g_rows = spread(hot, line_g, (ne, block, width + lane), tags)
    last = [p[1] for p in pieces]
    pair_bias, g_rows, last, gain_one, gain_two, place_ids = lax.optimization_barrier(
        (pair_bias, g_rows, last, gain_one, gain_two, place_ids)
    )
    g_arrived = plane(g_rows)
    pieces = [v for p, q in zip(pieces, last) for v in (p[0], across(p[0], 1), q, across(q, 1))]
    attn_in, proj, probs, mixed_low, residual, ffn_in, full = local_call(
        attend_kernel,
        [
            ((length, width), bf16),
            ((length, 3 * width), bf16),
            ((heads, length, length), f32),
            ((length, width), bf16),
            ((length, width), f32),
            ((length, width), bf16),
            ((width, 4 * width), bf16),
        ],
        [place_ids, tokens, gain_one, gain_two, pair_bias, *pieces],
        scalars=1,
    )

    line_ffn = [ffn_in] + [from_shift(ffn_in, k) for k in range(1, ns)]
    line_ffn, g_arrived = lax.optimization_barrier((line_ffn, g_arrived))
    sent = spread(hot, line_ffn, (ne, block, width))
    arrived = plane(sent)
    split_e = 3 * ne // 4
    same = [list(range(c, ne, 2)) for c in range(2)]
    factors = jnp.stack([attn_in] * (split_e // 2) + [mixed_low] * ((ne - split_e) // 2))
    arrived, factors = lax.optimization_barrier((arrived, factors))
    held = lax.all_to_all(
        factors, "expert", split_axis=0, concat_axis=0, axis_index_groups=same, tiled=True
    )

    wide_width = width + lane
    first_id = (me_e * exp_dev).astype(jnp.int32).reshape(1)
    send, y_send, rows, hidden, d_pre, d_y = pl.pallas_call(
        expert_kernel,
        out_shape=[
            jax.ShapeDtypeStruct((ne, block, wide_width), bf16),
            jax.ShapeDtypeStruct((ne, block, width), bf16),
            jax.ShapeDtypeStruct((exp_dev, group_rows, width), bf16),
            jax.ShapeDtypeStruct((exp_dev, group_rows, hidden_units), bf16),
            jax.ShapeDtypeStruct((exp_dev, group_rows, hidden_units), bf16),
            jax.ShapeDtypeStruct((exp_dev, group_rows, width), bf16),
        ],
        grid=(exp_dev, 2),
        in_specs=[
            pl.BlockSpec(memory_space=pltpu.SMEM),
            pl.BlockSpec((ne // 2, per, width), lambda j, h: (h, j, 0)),
            pl.BlockSpec((ne // 2, per, wide_width), lambda j, h: (h, j, 0)),
            pl.BlockSpec((1, width, hidden_units), lambda j, h: (j, 0, 0)),
            pl.BlockSpec((1, hidden_units, width), lambda j, h: (j, 0, 0)),
            pl.BlockSpec((width, experts), lambda j, h: (0, 0)),
        ],
        out_specs=[
            pl.BlockSpec((ne // 2, per, wide_width), lambda j, h: (h, j, 0)),
            pl.BlockSpec((ne // 2, per, width), lambda j, h: (h, j, 0)),
            pl.BlockSpec((1, group_rows // 2, width), lambda j, h: (j, h, 0)),
            pl.BlockSpec((1, group_rows // 2, hidden_units), lambda j, h: (j, h, 0)),
            pl.BlockSpec((1, group_rows // 2, hidden_units), lambda j, h: (j, h, 0)),
            pl.BlockSpec((1, group_rows // 2, width), lambda j, h: (j, h, 0)),
        ],
        compiler_params=pltpu.CompilerParams(vmem_limit_bytes=56 << 20),
        cost_estimate=pl.CostEstimate(
            flops=8 * exp_dev * group_rows * width * hidden_units,
            bytes_accessed=16 * exp_dev * group_rows * width,
            transcendentals=0,
        ),
    )(first_id, arrived, g_arrived, w_in, w_down, full_router)
    send, held = lax.optimization_barrier((send, held))
    held_other = across(held, 1)
    d_back = plane(send)
    grad_w_down = jnp.einsum("jrf,jrd->jfd", hidden, d_y, preferred_element_type=f32)
    grad_w_in = jnp.einsum("jrd,jrf->jdf", rows, d_pre, preferred_element_type=f32)
    d_back, grad_w_down, grad_w_in = lax.optimization_barrier((d_back, grad_w_down, grad_w_in))

    own_d, *pays = collect(d_back, hot_back, length, 2 * ns * length * total_rows * wide_width)
    got = [to_shift(v, k + 1) for k, v in enumerate(pays)]
    pays, y_send = lax.optimization_barrier((pays, y_send))
    y_back = plane(y_send)
    columns = 4 * width // ne
    wide, d_residual, d_logits, gain_two_grad, d_scores, d_proj = local_call(
        functools.partial(backward_kernel, ns - 1),
        [
            ((ne, length, columns), bf16),
            ((length, width), f32),
            ((length, experts), bf16),
            ((1, width), f32),
            ((heads, length, length), f32),
            ((length, 3 * width), bf16),
        ],
        [own_d, *got, ffn_in, residual, cotangent, full_router, routes, gain_two, full, proj, probs],
        views={ns + 6: ((width, width), (0, 3))},
        flops=2 * length * width * width + 10 * heads * length * length * lane,
        moved=2 * width * width + 8 * heads * length * length,
    )
    wide, y_back = lax.optimization_barrier((wide, y_back))
    wide = plane(wide)
    grad_tokens, gain_one_grad, grad_table = local_call(
        tokens_kernel,
        [((length, width), f32), ((1, width), f32), ((buckets, heads, lane), f32)],
        [d_proj, full, tokens, gain_one, d_residual, d_scores, bucket_ids],
        views={1: ((width, 3 * width), (0, 0))},
    )
    grad_router = dot(ffn_in, d_logits, 0, 0)

    small_parts = [
        grad_router.reshape(ns, -1),
        gain_one_grad.reshape(ns, -1),
        gain_two_grad.reshape(ns, -1),
        jnp.sum(grad_table, axis=-1).reshape(ns, -1),
    ]
    sizes = [v.shape[1] for v in small_parts]
    small = jnp.concatenate(small_parts, axis=1).astype(bf16)
    each = small.shape[1]
    srows = -(-each // columns)
    srows += -srows % 16
    room = srows * columns
    small = jnp.pad(small, ((0, 0), (0, room - each))).reshape(ns, srows, columns)
    share, *products = local_call(
        product_kernel,
        [((part + srows, columns), f32)] + [((part + srows, columns), bf16)] * (ns - 1),
        [place_ids, held, held_other, wide, small],
        scalars=1,
        scratch=[pltpu.VMEM((ne * length, columns), bf16), pltpu.VMEM((width, columns), f32)],
        flops=2 * ne * length * width * columns,
        moved=2 * ne * length * (width + columns),
    )
    products, y_back = lax.optimization_barrier((products, y_back))
    y_own, *y_pays = collect(y_back, hot_back, length)
    y_own = residual + y_own
    for k, v in enumerate(products):
        share = share + to_shift(v, k + 1).astype(f32)
    share, y_pays = lax.optimization_barrier((share.astype(bf16), y_pays))
    y_got = [to_shift(v, k + 1) for k, v in enumerate(y_pays)]
    by_core = columns % lane == 0
    if by_core:
        copies = jnp.broadcast_to(share[None], (ne // 2,) + share.shape)
        whole = lax.all_to_all(
            copies, "expert", split_axis=0, concat_axis=0, axis_index_groups=same, tiled=True
        )
        whole, y_got[1] = lax.optimization_barrier((whole, y_got[1]))
        whole = [whole, across(whole, 1)]
    else:
        whole = [plane(jnp.broadcast_to(share[None], (ne,) + share.shape))]
    out_qkv, out_out, small = local_call(
        unpack_kernel,
        [((part, 3 * width), f32), ((part, width), f32), ((srows, columns), f32)],
        [place_ids, *whole],
        scalars=1,
    )
    y_own, small = lax.optimization_barrier((y_own, small.reshape(-1)))
    smalls = []
    at = 0
    for size in sizes:
        smalls.append(small[at : at + size])
        at += size

    for v in y_got:
        y_own = y_own + v.astype(f32)
    return (
        y_own.astype(bf16),
        grad_tokens,
        out_qkv,
        out_out,
        smalls[0].reshape(part, experts),
        smalls[1],
        smalls[2],
        smalls[3].reshape(buckets // ns, heads),
        grad_w_in,
        grad_w_down,
    )


def solution(mesh):
    in_specs = (
        P(("expert", "shard"), None),
        P("shard", None),
        P("shard", None),
        P("shard", None),
        P("shard"),
        P("shard"),
        P("shard", None),
        P("expert", None, "shard"),
        P("expert", "shard", None),
        P(("expert", "shard"), None),
        P(("expert", "shard"), None),
        P(),
        P(("expert", "shard"), None),
    )
    out_specs = (
        P(("expert", "shard"), None),
        P(("expert", "shard"), None),
        P("shard", None),
        P("shard", None),
        P("shard", None),
        P("shard"),
        P("shard"),
        P("shard", None),
        P("expert", None, "shard"),
        P("expert", "shard", None),
    )
    return jax.shard_map(body, mesh=mesh, in_specs=in_specs, out_specs=out_specs, check_vma=False)
```

```python
import functools
import math

import jax
import jax.numpy as jnp
from jax import lax
from jax.experimental import pallas as pl
from jax.experimental.pallas import tpu as pltpu
from jax.sharding import PartitionSpec as P

norm_eps = 1e-06
f32 = jnp.float32
bf16 = jnp.bfloat16
lane = 128


def inverse_rms(values):
    return lax.rsqrt(jnp.mean(values * values, axis=-1, keepdims=True) + norm_eps)


def dot(a, b, ca=1, cb=0):
    return lax.dot_general(a, b, (((ca,), (cb,)), ((), ())), preferred_element_type=f32)


def split_two(v):
    high = v.astype(bf16)
    return high, (v - high.astype(f32)).astype(bf16)


def local_call(kernel, outs, args, scalars=0, views=None, scratch=(), direct=False, room=56, flops=0, moved=0):
    def block(shape, where=None):
        where = where or (0,) * len(shape)
        return pl.BlockSpec(shape, lambda i: where)

    specs = [pl.BlockSpec(memory_space=pltpu.SMEM)] * scalars
    specs += [pl.BlockSpec(memory_space=pltpu.VMEM) if direct else block(v.shape) for v in args[scalars:]]
    for n, (shape, where) in (views or {}).items():
        specs[n] = block(shape, where)
    return pl.pallas_call(
        kernel,
        out_shape=[jax.ShapeDtypeStruct(shape, kind) for shape, kind in outs],
        grid=(1,),
        in_specs=specs,
        out_specs=[block(shape) for shape, _ in outs],
        scratch_shapes=list(scratch),
        compiler_params=pltpu.CompilerParams(vmem_limit_bytes=room << 20),
        cost_estimate=pl.CostEstimate(flops=flops, bytes_accessed=moved, transcendentals=0),
    )(*args)


def join_blocks(e, s, parts, full_ref):
    count = 2 * parts[0].shape[1]
    rows, cols = parts[0].shape[2], parts[0].shape[3]
    for n, ref in enumerate(parts):
        bits = ((2, 4), (4, 2))[n // 4]
        for i in range(ref.shape[0]):
            differ = i * bits[0] + (n // 2 % 2) * bits[1] + n % 2
            col = pl.multiple_of(((e & 7) ^ differ) * cols, lane)
            for q in range(count // 2):
                source = lax.rem(s - (q + (n // 4) * (count // 2)) + count, count)
                row = pl.multiple_of(source * rows, 16)
                full_ref[pl.ds(row, rows), pl.ds(col, cols)] = ref[i, q]


def head_mask(shape, h, head_dim):
    return lax.broadcasted_iota(jnp.int32, shape, 1) // head_dim == h


def tables_kernel(row_ref, col_ref, route_ref, hot_ref, back_ref, tag_ref):
    total, tokens = hot_ref.shape
    one, zero = jnp.ones((), f32), jnp.zeros((), f32)
    ids = lax.broadcasted_iota(jnp.int32, (total, tokens), 0)
    hots = [jnp.where(ids == row_ref[i : i + 1, :], one, zero).astype(bf16) for i in range(2)]
    hot_ref[...] = hots[0] + hots[1]
    ids = lax.broadcasted_iota(jnp.int32, (tokens, total), 1)
    found = (ids == col_ref[:, 0:1]) | (ids == col_ref[:, 1:2])
    back_ref[...] = jnp.where(found, one, zero).astype(bf16)
    cols = lax.broadcasted_iota(jnp.int32, (tokens, lane), 1)
    tags = zero
    for i in range(2):
        tag = jnp.where(cols == 0, route_ref[:, 1 - i : 2 - i].astype(f32), jnp.where(cols == 1, float(i), 0.0))
        tags = tags + dot(hots[i], tag.astype(bf16))
    tag_ref[...] = tags.astype(bf16)


def spread_kernel(hot_ref, *refs):
    out_ref, rows_ref = refs[-2:]
    count, block, wide = out_ref.shape
    length, width = refs[0].shape
    line_refs = refs[: rows_ref.shape[0] // length]

    @pl.when(pl.program_id(0) == 0)
    def _():
        for k, ref in enumerate(line_refs):
            rows_ref[k * length : (k + 1) * length, :] = ref[...]

    out_ref[:, :, :width] = dot(hot_ref[...], rows_ref[...]).astype(bf16).reshape(count, block, width)
    if wide > width:
        out_ref[:, :, width:] = refs[-3][...].reshape(count, block, lane)


def spread(hot, line, shape, tags=None):
    length, width = line[0].shape
    count, block, wide = shape
    rows = 2 * block
    specs = [pl.BlockSpec((rows, hot.shape[1]), lambda i: (i, 0))]
    specs += [pl.BlockSpec((length, width), lambda i: (0, 0))] * len(line)
    args = [hot, *line]
    if tags is not None:
        specs.append(pl.BlockSpec((rows, lane), lambda i: (i, 0)))
        args.append(tags)
    return pl.pallas_call(
        spread_kernel,
        out_shape=jax.ShapeDtypeStruct(shape, bf16),
        grid=(count // 2,),
        in_specs=specs,
        out_specs=pl.BlockSpec((2, block, wide), lambda i: (i, 0, 0)),
        scratch_shapes=[pltpu.VMEM((len(line) * length, width), bf16)],
        compiler_params=pltpu.CompilerParams(vmem_limit_bytes=32 << 20),
        cost_estimate=pl.CostEstimate(flops=0, bytes_accessed=0, transcendentals=0),
    )(*args)


def attend_kernel(
    ids_ref, tok_ref, gain_ref, gain_two_ref, bias_ref, *refs,
):
    attn_ref, proj_ref, probs_ref, mixed_ref, res_ref, ffn_ref, full_ref = refs[-7:]
    join_blocks(ids_ref[0], ids_ref[1], refs[:-7], full_ref)
    length, width = tok_ref.shape
    heads = bias_ref.shape[0]
    head_dim = width // heads
    pack = lane // head_dim
    x = tok_ref[...].astype(f32)
    low = (x * inverse_rms(x) * gain_ref[...]).astype(bf16)
    attn_ref[...] = low
    step = width // 2
    for c in range(6):
        cols = slice(c * step, (c + 1) * step)
        proj_ref[:, cols] = dot(low, full_ref[:, cols]).astype(bf16)
    for g in range(heads // pack):
        q = proj_ref[:, g * lane : (g + 1) * lane]
        k = proj_ref[:, width + g * lane : width + (g + 1) * lane]
        v = proj_ref[:, 2 * width + g * lane : 2 * width + (g + 1) * lane]
        total = jnp.zeros((length, lane), f32)
        for h in range(pack):
            keep = head_mask((length, lane), h, head_dim)
            s = dot(q, jnp.where(keep, k, jnp.zeros_like(k)), 1, 1) * 0.125 + bias_ref[g * pack + h]
            e = jnp.exp(s - jnp.max(s, axis=-1, keepdims=True))
            p = e / jnp.sum(e, axis=-1, keepdims=True)
            probs_ref[g * pack + h] = p
            total = total + dot(p.astype(bf16), jnp.where(keep, v, jnp.zeros_like(v)))
        mixed_ref[:, g * lane : (g + 1) * lane] = total.astype(bf16)
    res = x + dot(mixed_ref[...], full_ref[:, 3 * width :])
    res_ref[...] = res
    ffn_ref[...] = (res * inverse_rms(res) * gain_two_ref[...]).astype(bf16)


def expert_kernel(
    ids_ref, rows_ref, g_ref, wi_ref, wd_ref, router_ref,
    send_ref, y_ref, rows_out, hidden_out, dpre_out, dy_out,
):
    j = pl.program_id(0)
    count, per, width = rows_ref.shape
    total = count * per
    experts = router_ref.shape[1]
    x = rows_ref[...].reshape(total, width)
    rows_out[0] = x
    g = g_ref[:, :, :width].reshape(total, width).astype(f32)
    tags = g_ref[:, :, width:].reshape(total, lane).astype(f32)
    other, choice = tags[:, 0:1], tags[:, 1:2]
    logits = dot(x, router_ref[...])
    ids = lax.broadcasted_iota(jnp.int32, (total, experts), 1)
    own_logit = jnp.sum(jnp.where(ids == ids_ref[0] + j, logits, 0.0), -1, keepdims=True)
    other_logit = jnp.sum(jnp.where(ids.astype(f32) == other, logits, 0.0), -1, keepdims=True)
    gate = 1.0 / (1.0 + jnp.exp(other_logit - own_logit))
    d_y = (gate * g).astype(bf16)
    dy_out[0] = d_y
    pre = dot(x, wi_ref[0])
    square = pre * pre
    root = 0.7978845608028654
    gate_in = 0.5 + 0.5 * jnp.tanh(pre * (root + root * 0.044715 * square))
    hidden = (pre * gate_in).astype(bf16)
    hidden_out[0] = hidden
    slope = gate_in + gate_in * (1.0 - gate_in) * (
        pre * (2.0 * root + 6.0 * root * 0.044715 * square)
    )
    d_pre = (dot(d_y, wd_ref[0], 1, 1) * slope).astype(bf16)
    dpre_out[0] = d_pre
    d_rows = dot(d_pre, wi_ref[0], 1, 1).astype(bf16)
    send_ref[:, :, :width] = d_rows.reshape(count, per, width)
    y = dot(hidden, wd_ref[0])
    y_ref[...] = (gate * y).astype(bf16).reshape(count, per, width)
    d_gate = jnp.sum(g * y, axis=-1, keepdims=True)
    high = d_gate.astype(bf16).astype(f32)
    cols = lax.broadcasted_iota(jnp.int32, (total, lane), 1).astype(f32)
    tail = jnp.where(cols == choice, high, jnp.where(cols == choice + 2.0, d_gate - high, 0.0))
    send_ref[:, :, width:] = tail.astype(bf16).reshape(count, per, lane)


def collect_kernel(back_ref, hot_ref, own_ref, *refs):
    pay_refs, total_ref = refs[:-1], refs[-1]
    length = own_ref.shape[0]
    step = pl.program_id(0)
    got = dot(hot_ref[...], back_ref[...].reshape(-1, back_ref.shape[2]))

    @pl.when(step == 0)
    def _():
        total_ref[...] = got

    @pl.when(step > 0)
    def _():
        total_ref[...] += got

    @pl.when(step == pl.num_programs(0) - 1)
    def _():
        own_ref[...] = total_ref[:length, :]
        for k, ref in enumerate(pay_refs):
            ref[...] = total_ref[(k + 1) * length : (k + 2) * length, :].astype(bf16)


def collect(back, hot_back, length, flops=0):
    count, block, wide = back.shape
    step = math.lcm(block, lane) // block
    line = hot_back.shape[0] // length
    kinds = [f32] + [bf16] * (line - 1)
    return pl.pallas_call(
        collect_kernel,
        out_shape=[jax.ShapeDtypeStruct((length, wide), kind) for kind in kinds],
        grid=(count // step,),
        in_specs=[
            pl.BlockSpec((step, block, wide), lambda i: (i, 0, 0)),
            pl.BlockSpec((line * length, step * block), lambda i: (0, i)),
        ],
        out_specs=[pl.BlockSpec((length, wide), lambda i: (0, 0)) for _ in kinds],
        scratch_shapes=[pltpu.VMEM((line * length, wide), f32)],
        compiler_params=pltpu.CompilerParams(vmem_limit_bytes=32 << 20),
        cost_estimate=pl.CostEstimate(flops=flops, bytes_accessed=0, transcendentals=0),
    )(back, hot_back)


def backward_kernel(count, *refs):
    own_ref = refs[0]
    got_refs = refs[1 : 1 + count]
    (
        ffn_ref, res_ref, cot_ref, router_ref, routes_ref, gain_ref, full_ref, proj_ref, probs_ref,
        wide_ref, dres_ref, dlog_ref, gain_grad_ref, ds_ref, dproj_ref,
    ) = refs[1 + count :]
    length, width = ffn_ref.shape
    heads = probs_ref.shape[0]
    head_dim = width // heads
    pack = lane // head_dim
    experts = router_ref.shape[1]
    d = own_ref[...]
    for ref in got_refs:
        d = d + ref[...].astype(f32)
    tail = d[:, width:]
    d = d[:, :width]
    dg = [tail[:, i : i + 1] + tail[:, i + 2 : i + 3] for i in range(2)]
    logits = dot(ffn_ref[...], router_ref[...])
    e = jnp.exp(logits - jnp.max(logits, axis=-1, keepdims=True))
    router = e / jnp.sum(e, axis=-1, keepdims=True)
    ids = lax.broadcasted_iota(jnp.int32, (length, experts), 1)
    hots = [ids == routes_ref[:, i : i + 1] for i in range(2)]
    picked = [jnp.sum(jnp.where(h, router, 0.0), -1, keepdims=True) for h in hots]
    both = picked[0] + picked[1]
    mean = (dg[0] * picked[0] + dg[1] * picked[1]) / (both * both)
    d_router = sum(jnp.where(h, v / both - mean, 0.0) for h, v in zip(hots, dg))
    d_logits = router * (d_router - jnp.sum(router * d_router, -1, keepdims=True))
    d_logits = d_logits.astype(bf16)
    dlog_ref[...] = d_logits
    d_ffn = d + dot(d_logits, router_ref[...], 1, 1)
    res = res_ref[...]
    inv = inverse_rms(res)
    normed = res * inv
    gain_grad_ref[...] = jnp.sum(d_ffn * normed, axis=0, keepdims=True)
    d_norm = d_ffn * gain_ref[...]
    d_res = cot_ref[...].astype(f32) + inv * (
        d_norm - normed * jnp.mean(d_norm * normed, axis=-1, keepdims=True)
    )
    dres_ref[...] = d_res
    d_branch = d_res.astype(bf16)
    d_heads = dot(d_branch, full_ref[...], 1, 1).astype(bf16)
    for g in range(heads // pack):
        q = proj_ref[:, g * lane : (g + 1) * lane]
        k = proj_ref[:, width + g * lane : width + (g + 1) * lane]
        v = proj_ref[:, 2 * width + g * lane : 2 * width + (g + 1) * lane]
        dh = d_heads[:, g * lane : (g + 1) * lane]
        zero = jnp.zeros_like(q)
        sums = [jnp.zeros((length, lane), f32) for _ in range(3)]
        for h in range(pack):
            keep = head_mask((length, lane), h, head_dim)
            p = probs_ref[g * pack + h]
            dh_one = jnp.where(keep, dh, zero)
            d_probs = dot(dh_one, v, 1, 1)
            ds = p * (d_probs - jnp.sum(p * d_probs, axis=-1, keepdims=True))
            ds = ds.astype(bf16)
            ds_ref[g * pack + h] = ds.astype(f32)
            sums[0] = sums[0] + dot(ds, jnp.where(keep, k, zero))
            sums[1] = sums[1] + dot(ds, jnp.where(keep, q, zero), 0, 0)
            sums[2] = sums[2] + dot(p.astype(bf16), dh_one, 0, 0)
        for i, scale in enumerate((0.125, 0.125, 1.0)):
            dproj_ref[:, i * width + g * lane : i * width + (g + 1) * lane] = (sums[i] * scale).astype(bf16)
    columns = wide_ref.shape[2]
    split = 3 * width // columns
    for b in range(wide_ref.shape[0]):
        if b < split:
            wide_ref[b] = dproj_ref[:, b * columns : (b + 1) * columns]
        else:
            wide_ref[b] = d_branch[:, (b - split) * columns : (b - split + 1) * columns]


def product_kernel(ids_ref, own_ref, other_ref, wide_ref, small_ref, share_ref, *refs):
    pay_refs, order_ref, total_ref = refs[:-2], refs[-2], refs[-1]
    pairs, length, width = own_ref.shape
    e, s = ids_ref[0], ids_ref[1]
    count, part = small_ref.shape[0], width // small_ref.shape[0]
    for n in range(2):
        for i in range(pairs):
            at = (n * pairs + i) * length
            order_ref[at : at + length, :] = wide_ref[2 * i + ((e & 1) ^ n)]
    half = pairs * length
    total_ref[...] = dot(own_ref[...].reshape(half, width), order_ref[:half, :], 0, 0) + dot(
        other_ref[...].reshape(half, width), order_ref[half:, :], 0, 0
    )
    for k in range(count):
        target = lax.rem(s - k + count, count)
        rows = total_ref[pl.ds(pl.multiple_of(target * part, 16), part), :]
        ref = share_ref if k == 0 else pay_refs[k - 1]
        ref[:part, :] = rows.astype(ref.dtype)
        ref[part:, :] = small_ref[target].astype(ref.dtype)


def unpack_kernel(ids_ref, *refs):
    whole_refs, (qkv_ref, out_ref, small_ref) = refs[:-3], refs[-3:]
    part, width = out_ref.shape
    cols = small_ref.shape[1]
    split = 3 * width // cols
    pair = len(whole_refs)
    total = jnp.zeros(small_ref.shape, f32)
    for n, ref in enumerate(whole_refs):
        for i in range(ref.shape[0]):
            got = ref[i, :part, :].astype(f32)
            total = total + ref[i, part:, :].astype(f32)
            if pair * i < split:
                target, first = qkv_ref, pair * i
            else:
                target, first = out_ref, pair * i - split
            if pair == 1:
                target[:, first * cols : (first + 1) * cols] = got
            else:
                at = pl.multiple_of((first + ((ids_ref[0] & 1) ^ n)) * cols, lane)
                target[:, pl.ds(at, cols)] = got
    small_ref[...] = total


def tokens_kernel(
    dproj_ref, full_ref, tok_ref, gain_ref, dres_ref, ds_ref, ids_ref, out_ref, gain_grad_ref, table_ref
):
    ids = ids_ref[...]
    for b in range(table_ref.shape[0]):
        found = ids == b
        for h in range(table_ref.shape[1]):
            table_ref[b, h : h + 1, :] = jnp.sum(jnp.where(found, ds_ref[h], 0.0), axis=0, keepdims=True)
    d_in = dot(dproj_ref[...], full_ref[...], 1, 1)
    x = tok_ref[...].astype(f32)
    inv = inverse_rms(x)
    normed = x * inv
    gain_grad_ref[...] = jnp.sum(d_in * normed, axis=0, keepdims=True)
    d_norm = d_in * gain_ref[...]
    out_ref[...] = dres_ref[...] + inv * (
        d_norm - normed * jnp.mean(d_norm * normed, axis=-1, keepdims=True)
    )


def body(
    tokens,
    w_qkv,
    w_out,
    w_router,
    gain_attn,
    gain_ffn,
    bias_table,
    w_in,
    w_down,
    routes,
    slots,
    bucket_ids,
    cotangent,
):
    length, width = tokens.shape
    ne = lax.axis_size("expert")
    ns = lax.axis_size("shard")
    me_e = lax.axis_index("expert")
    me_s = lax.axis_index("shard")
    place_ids = jnp.stack([me_e, me_s]).astype(jnp.int32)
    exp_dev = w_in.shape[0]
    hidden_units = w_in.shape[2]
    experts = exp_dev * ne
    cap = 3 * length // experts
    per = ns * cap
    block = exp_dev * per
    total_rows = ne * block
    group_rows = ne * per
    heads = bias_table.shape[1]
    buckets = bias_table.shape[0] * ns
    part = width // ns

    def from_shift(v, k):
        return lax.ppermute(v, "shard", [(i, (i + k) % ns) for i in range(ns)])

    def to_shift(v, k):
        return lax.ppermute(v, "shard", [(i, (i - k) % ns) for i in range(ns)])

    def plane(v):
        return lax.all_to_all(v, "expert", split_axis=0, concat_axis=0, tiled=True)

    def across(v, bit):
        return lax.ppermute(v, "expert", [(i, i ^ bit) for i in range(ne)])

    cols = width // 2
    mine = me_e & 7
    weight = jnp.where(
        mine < 6,
        lax.dynamic_slice_in_dim(w_qkv, jnp.minimum(mine, 5) * cols, cols, 1),
        lax.dynamic_slice_in_dim(w_out, (jnp.maximum(mine, 6) - 6) * cols, cols, 1),
    )
    line = [weight] + [from_shift(weight, k) for k in range(1, ns)]

    smalls = (w_router, gain_attn, gain_ffn, bias_table, routes.astype(bf16), slots.astype(bf16))
    small = jnp.concatenate([v.reshape(-1) for v in smalls])
    small_rows = -(-small.size // lane)
    small_rows += -small_rows % 16
    small = jnp.pad(small, (0, small_rows * lane - small.size)).reshape(1, small_rows, lane)
    in_order = lax.all_to_all(
        jnp.broadcast_to(small, (ns, small_rows, lane)), "shard", split_axis=0, concat_axis=0, tiled=True
    ).reshape(ns, small_rows * lane)
    cotangent, line = lax.optimization_barrier((cotangent, line))
    halves = []
    for half, bit in ((line[: ns // 2], 2), (line[ns // 2 :], 4)):
        held = jnp.stack(half)[None]
        halves.append(jnp.concatenate([held, across(held, bit)], axis=0))
    halves, in_order = lax.optimization_barrier((halves, in_order))
    pieces = [(v, across(v, bit)) for v, bit in zip(halves, (4, 2))]

    line_g = [cotangent] + [from_shift(cotangent, k) for k in range(1, ns)]
    order = lax.rem(me_s - jnp.arange(ns, dtype=jnp.int32) + ns, ns)
    line_small = jnp.take(in_order, order, axis=0)

    cuts = []
    at = 0
    for v in smalls:
        cuts.append((at, at + v.size))
        at += v.size

    def cut(v, i):
        return v[:, cuts[i][0] : cuts[i][1]]

    full_router = cut(in_order, 0).reshape(width, experts)
    gain_one = cut(in_order, 1).reshape(1, width).astype(f32)
    gain_two = cut(in_order, 2).reshape(1, width).astype(f32)
    table = cut(in_order, 3).reshape(buckets, heads)
    line_g, table, gain_one, gain_two = lax.optimization_barrier((line_g, table, gain_one, gain_two))
    line_routes = cut(line_small, 4).reshape(ns * length, 2)
    line_slots = cut(line_small, 5).reshape(ns * length, 2).astype(jnp.int32)
    place = (
        line_routes.astype(jnp.int32) * per + jnp.repeat(order, length)[:, None] * cap + line_slots
    )
    causal = jnp.arange(length)[:, None] >= jnp.arange(length)[None, :]
    bucket_hot = (
        jnp.arange(buckets, dtype=jnp.int32)[:, None] == bucket_ids.reshape(1, -1)
    ).astype(bf16)
    pair_bias = dot(table, bucket_hot, 0, 0).reshape(heads, length, length)
    pair_bias = jnp.where(causal[None], pair_bias, -1e30)
    hot, hot_back, tags = local_call(
        tables_kernel,
        [((total_rows, ns * length), bf16), ((ns * length, total_rows), bf16), ((total_rows, lane), bf16)],
        [place.T, place, line_routes],
    )
    g_rows = spread(hot, line_g, (ne, block, width + lane), tags)
    last = [p[1] for p in pieces]
    first = [p[0] for p in pieces]
    pair_bias, g_rows, last, first, gain_one, gain_two, place_ids = lax.optimization_barrier(
        (pair_bias, g_rows, last, first, gain_one, gain_two, place_ids)
    )
    first = [across(v, 1) for v in first]
    first, g_rows = lax.optimization_barrier((first, g_rows))
    g_arrived = plane(g_rows)
    pieces = [v for p, q, r in zip(pieces, last, first) for v in (p[0], r, q, across(q, 1))]
    attn_in, proj, probs, mixed_low, residual, ffn_in, full = local_call(
        attend_kernel,
        [
            ((length, width), bf16),
            ((length, 3 * width), bf16),
            ((heads, length, length), f32),
            ((length, width), bf16),
            ((length, width), f32),
            ((length, width), bf16),
            ((width, 4 * width), bf16),
        ],
        [place_ids, tokens, gain_one, gain_two, pair_bias, *pieces],
        scalars=1,
    )

    line_ffn = [ffn_in] + [from_shift(ffn_in, k) for k in range(1, ns)]
    line_ffn, g_arrived = lax.optimization_barrier((line_ffn, g_arrived))
    sent = spread(hot, line_ffn, (ne, block, width))
    arrived = plane(sent)
    split_e = 3 * ne // 4
    same = [list(range(c, ne, 2)) for c in range(2)]
    factors = jnp.stack([attn_in] * (split_e // 2) + [mixed_low] * ((ne - split_e) // 2))
    arrived, factors = lax.optimization_barrier((arrived, factors))
    held = lax.all_to_all(
        factors, "expert", split_axis=0, concat_axis=0, axis_index_groups=same, tiled=True
    )

    wide_width = width + lane
    first_id = (me_e * exp_dev).astype(jnp.int32).reshape(1)
    send, y_send, rows, hidden, d_pre, d_y = pl.pallas_call(
        expert_kernel,
        out_shape=[
            jax.ShapeDtypeStruct((ne, block, wide_width), bf16),
            jax.ShapeDtypeStruct((ne, block, width), bf16),
            jax.ShapeDtypeStruct((exp_dev, group_rows, width), bf16),
            jax.ShapeDtypeStruct((exp_dev, group_rows, hidden_units), bf16),
            jax.ShapeDtypeStruct((exp_dev, group_rows, hidden_units), bf16),
            jax.ShapeDtypeStruct((exp_dev, group_rows, width), bf16),
        ],
        grid=(exp_dev, 2),
        in_specs=[
            pl.BlockSpec(memory_space=pltpu.SMEM),
            pl.BlockSpec((ne // 2, per, width), lambda j, h: (h, j, 0)),
            pl.BlockSpec((ne // 2, per, wide_width), lambda j, h: (h, j, 0)),
            pl.BlockSpec((1, width, hidden_units), lambda j, h: (j, 0, 0)),
            pl.BlockSpec((1, hidden_units, width), lambda j, h: (j, 0, 0)),
            pl.BlockSpec((width, experts), lambda j, h: (0, 0)),
        ],
        out_specs=[
            pl.BlockSpec((ne // 2, per, wide_width), lambda j, h: (h, j, 0)),
            pl.BlockSpec((ne // 2, per, width), lambda j, h: (h, j, 0)),
            pl.BlockSpec((1, group_rows // 2, width), lambda j, h: (j, h, 0)),
            pl.BlockSpec((1, group_rows // 2, hidden_units), lambda j, h: (j, h, 0)),
            pl.BlockSpec((1, group_rows // 2, hidden_units), lambda j, h: (j, h, 0)),
            pl.BlockSpec((1, group_rows // 2, width), lambda j, h: (j, h, 0)),
        ],
        compiler_params=pltpu.CompilerParams(vmem_limit_bytes=56 << 20),
        cost_estimate=pl.CostEstimate(
            flops=8 * exp_dev * group_rows * width * hidden_units,
            bytes_accessed=16 * exp_dev * group_rows * width,
            transcendentals=0,
        ),
    )(first_id, arrived, g_arrived, w_in, w_down, full_router)
    send, held = lax.optimization_barrier((send, held))
    held_other = across(held, 1)
    d_back = plane(send)
    grad_w_down = jnp.einsum("jrf,jrd->jfd", hidden, d_y, preferred_element_type=f32)
    grad_w_in = jnp.einsum("jrd,jrf->jdf", rows, d_pre, preferred_element_type=f32)
    d_back, grad_w_down, grad_w_in = lax.optimization_barrier((d_back, grad_w_down, grad_w_in))

    own_d, *pays = collect(d_back, hot_back, length, 2 * ns * length * total_rows * wide_width)
    got = [to_shift(v, k + 1) for k, v in enumerate(pays)]
    pays, y_send = lax.optimization_barrier((pays, y_send))
    y_back = plane(y_send)
    columns = 4 * width // ne
    wide, d_residual, d_logits, gain_two_grad, d_scores, d_proj = local_call(
        functools.partial(backward_kernel, ns - 1),
        [
            ((ne, length, columns), bf16),
            ((length, width), f32),
            ((length, experts), bf16),
            ((1, width), f32),
            ((heads, length, length), f32),
            ((length, 3 * width), bf16),
        ],
        [own_d, *got, ffn_in, residual, cotangent, full_router, routes, gain_two, full, proj, probs],
        views={ns + 6: ((width, width), (0, 3))},
        flops=2 * length * width * width + 10 * heads * length * length * lane,
        moved=2 * width * width + 8 * heads * length * length,
    )
    wide, y_back = lax.optimization_barrier((wide, y_back))
    wide = plane(wide)
    grad_tokens, gain_one_grad, grad_table = local_call(
        tokens_kernel,
        [((length, width), f32), ((1, width), f32), ((buckets, heads, lane), f32)],
        [d_proj, full, tokens, gain_one, d_residual, d_scores, bucket_ids],
        views={1: ((width, 3 * width), (0, 0))},
    )
    grad_router = dot(ffn_in, d_logits, 0, 0)

    small_parts = [
        grad_router.reshape(ns, -1),
        gain_one_grad.reshape(ns, -1),
        gain_two_grad.reshape(ns, -1),
        jnp.sum(grad_table, axis=-1).reshape(ns, -1),
    ]
    sizes = [v.shape[1] for v in small_parts]
    small = jnp.concatenate(small_parts, axis=1).astype(bf16)
    each = small.shape[1]
    srows = -(-each // columns)
    srows += -srows % 16
    room = srows * columns
    small = jnp.pad(small, ((0, 0), (0, room - each))).reshape(ns, srows, columns)
    share, *products = local_call(
        product_kernel,
        [((part + srows, columns), f32)] + [((part + srows, columns), bf16)] * (ns - 1),
        [place_ids, held, held_other, wide, small],
        scalars=1,
        room=32,
        scratch=[pltpu.VMEM((ne * length, columns), bf16), pltpu.VMEM((width, columns), f32)],
        flops=2 * ne * length * width * columns,
        moved=2 * ne * length * (width + columns),
    )
    products, y_back = lax.optimization_barrier((products, y_back))
    y_own, *y_pays = collect(y_back, hot_back, length)
    y_own = residual + y_own
    for k, v in enumerate(products):
        share = share + to_shift(v, k + 1).astype(f32)
    share, y_pays = lax.optimization_barrier((share.astype(bf16), y_pays))
    y_got = [to_shift(v, k + 1) for k, v in enumerate(y_pays)]
    by_core = columns % lane == 0
    if by_core:
        copies = jnp.broadcast_to(share[None], (ne // 2,) + share.shape)
        whole = lax.all_to_all(
            copies, "expert", split_axis=0, concat_axis=0, axis_index_groups=same, tiled=True
        )
        whole, y_got[1] = lax.optimization_barrier((whole, y_got[1]))
        whole = [whole, across(whole, 1)]
    else:
        whole = [plane(jnp.broadcast_to(share[None], (ne,) + share.shape))]
    out_qkv, out_out, small = local_call(
        unpack_kernel,
        [((part, 3 * width), f32), ((part, width), f32), ((srows, columns), f32)],
        [place_ids, *whole],
        scalars=1,
        room=32,
    )
    y_own, small = lax.optimization_barrier((y_own, small.reshape(-1)))
    smalls = []
    at = 0
    for size in sizes:
        smalls.append(small[at : at + size])
        at += size

    for v in y_got:
        y_own = y_own + v.astype(f32)
    return (
        y_own.astype(bf16),
        grad_tokens,
        out_qkv,
        out_out,
        smalls[0].reshape(part, experts),
        smalls[1],
        smalls[2],
        smalls[3].reshape(buckets // ns, heads),
        grad_w_in,
        grad_w_down,
    )


def solution(mesh):
    in_specs = (
        P(("expert", "shard"), None),
        P("shard", None),
        P("shard", None),
        P("shard", None),
        P("shard"),
        P("shard"),
        P("shard", None),
        P("expert", None, "shard"),
        P("expert", "shard", None),
        P(("expert", "shard"), None),
        P(("expert", "shard"), None),
        P(),
        P(("expert", "shard"), None),
    )
    out_specs = (
        P(("expert", "shard"), None),
        P(("expert", "shard"), None),
        P("shard", None),
        P("shard", None),
        P("shard", None),
        P("shard"),
        P("shard"),
        P("shard", None),
        P("expert", None, "shard"),
        P("expert", "shard", None),
    )
    return jax.shard_map(body, mesh=mesh, in_specs=in_specs, out_specs=out_specs, check_vma=False)
```

```python
import functools
import math

import jax
import jax.numpy as jnp
from jax import lax
from jax.experimental import pallas as pl
from jax.experimental.pallas import tpu as pltpu
from jax.sharding import PartitionSpec as P

norm_eps = 1e-06
f32 = jnp.float32
bf16 = jnp.bfloat16
lane = 128


def inverse_rms(values):
    return lax.rsqrt(jnp.mean(values * values, axis=-1, keepdims=True) + norm_eps)


def dot(a, b, ca=1, cb=0):
    return lax.dot_general(a, b, (((ca,), (cb,)), ((), ())), preferred_element_type=f32)


def split_two(v):
    high = v.astype(bf16)
    return high, (v - high.astype(f32)).astype(bf16)


def local_call(kernel, outs, args, scalars=0, views=None, scratch=(), direct=False, loose=0, flops=0, moved=0):
    def block(shape, where=None):
        where = where or (0,) * len(shape)
        return pl.BlockSpec(shape, lambda i: where)

    specs = [pl.BlockSpec(memory_space=pltpu.SMEM)] * scalars
    specs += [pl.BlockSpec(memory_space=pltpu.VMEM) if direct else block(v.shape) for v in args[scalars:]]
    for n, (shape, where) in (views or {}).items():
        specs[n] = block(shape, where)
    return pl.pallas_call(
        kernel,
        out_shape=[jax.ShapeDtypeStruct(shape, kind) for shape, kind in outs],
        grid=(1,),
        in_specs=specs,
        out_specs=[block(shape) for shape, _ in outs[: len(outs) - loose]]
        + [pl.BlockSpec(memory_space=pl.ANY)] * loose,
        scratch_shapes=list(scratch),
        compiler_params=pltpu.CompilerParams(vmem_limit_bytes=56 << 20),
        cost_estimate=pl.CostEstimate(flops=flops, bytes_accessed=moved, transcendentals=0),
    )(*args)


def join_blocks(e, s, parts, full_ref):
    count = 2 * parts[0].shape[1]
    rows, cols = parts[0].shape[2], parts[0].shape[3]
    for n, ref in enumerate(parts):
        bits = ((2, 4), (4, 2))[n // 4]
        for i in range(ref.shape[0]):
            differ = i * bits[0] + (n // 2 % 2) * bits[1] + n % 2
            col = pl.multiple_of(((e & 7) ^ differ) * cols, lane)
            for q in range(count // 2):
                source = lax.rem(s - (q + (n // 4) * (count // 2)) + count, count)
                row = pl.multiple_of(source * rows, 16)
                full_ref[pl.ds(row, rows), pl.ds(col, cols)] = ref[i, q]


def head_mask(shape, h, head_dim):
    return lax.broadcasted_iota(jnp.int32, shape, 1) // head_dim == h


def tables_kernel(row_ref, col_ref, route_ref, hot_ref, back_ref, tag_ref):
    total, tokens = hot_ref.shape
    one, zero = jnp.ones((), f32), jnp.zeros((), f32)
    ids = lax.broadcasted_iota(jnp.int32, (total, tokens), 0)
    hots = [jnp.where(ids == row_ref[i : i + 1, :], one, zero).astype(bf16) for i in range(2)]
    hot_ref[...] = hots[0] + hots[1]
    ids = lax.broadcasted_iota(jnp.int32, (tokens, total), 1)
    found = (ids == col_ref[:, 0:1]) | (ids == col_ref[:, 1:2])
    back_ref[...] = jnp.where(found, one, zero).astype(bf16)
    cols = lax.broadcasted_iota(jnp.int32, (tokens, lane), 1)
    tags = zero
    for i in range(2):
        tag = jnp.where(cols == 0, route_ref[:, 1 - i : 2 - i].astype(f32), jnp.where(cols == 1, float(i), 0.0))
        tags = tags + dot(hots[i], tag.astype(bf16))
    tag_ref[...] = tags.astype(bf16)


def spread_kernel(hot_ref, *refs):
    out_ref, rows_ref = refs[-2:]
    count, block, wide = out_ref.shape
    length, width = refs[0].shape
    line_refs = refs[: rows_ref.shape[0] // length]

    @pl.when(pl.program_id(0) == 0)
    def _():
        for k, ref in enumerate(line_refs):
            rows_ref[k * length : (k + 1) * length, :] = ref[...]

    out_ref[:, :, :width] = dot(hot_ref[...], rows_ref[...]).astype(bf16).reshape(count, block, width)
    if wide > width:
        out_ref[:, :, width:] = refs[-3][...].reshape(count, block, lane)


def spread(hot, line, shape, tags=None):
    length, width = line[0].shape
    count, block, wide = shape
    rows = 2 * block
    specs = [pl.BlockSpec((rows, hot.shape[1]), lambda i: (i, 0))]
    specs += [pl.BlockSpec((length, width), lambda i: (0, 0))] * len(line)
    args = [hot, *line]
    if tags is not None:
        specs.append(pl.BlockSpec((rows, lane), lambda i: (i, 0)))
        args.append(tags)
    return pl.pallas_call(
        spread_kernel,
        out_shape=jax.ShapeDtypeStruct(shape, bf16),
        grid=(count // 2,),
        in_specs=specs,
        out_specs=pl.BlockSpec((2, block, wide), lambda i: (i, 0, 0)),
        scratch_shapes=[pltpu.VMEM((len(line) * length, width), bf16)],
        compiler_params=pltpu.CompilerParams(vmem_limit_bytes=32 << 20),
        cost_estimate=pl.CostEstimate(flops=0, bytes_accessed=0, transcendentals=0),
    )(*args)


def attend_kernel(
    ids_ref, tok_ref, gain_ref, gain_two_ref, bias_ref, *refs,
):
    attn_ref, proj_ref, probs_ref, mixed_ref, res_ref, ffn_ref, out_ref, full_ref, sem = refs[-9:]
    join_blocks(ids_ref[0], ids_ref[1], refs[:-9], full_ref)
    keep_full = pltpu.make_async_copy(full_ref, out_ref, sem)
    keep_full.start()
    length, width = tok_ref.shape
    heads = bias_ref.shape[0]
    head_dim = width // heads
    pack = lane // head_dim
    x = tok_ref[...].astype(f32)
    low = (x * inverse_rms(x) * gain_ref[...]).astype(bf16)
    attn_ref[...] = low
    step = width // 2
    for c in range(6):
        cols = slice(c * step, (c + 1) * step)
        proj_ref[:, cols] = dot(low, full_ref[:, cols]).astype(bf16)
    for g in range(heads // pack):
        q = proj_ref[:, g * lane : (g + 1) * lane]
        k = proj_ref[:, width + g * lane : width + (g + 1) * lane]
        v = proj_ref[:, 2 * width + g * lane : 2 * width + (g + 1) * lane]
        total = jnp.zeros((length, lane), f32)
        for h in range(pack):
            keep = head_mask((length, lane), h, head_dim)
            s = dot(q, jnp.where(keep, k, jnp.zeros_like(k)), 1, 1) * 0.125 + bias_ref[g * pack + h]
            e = jnp.exp(s - jnp.max(s, axis=-1, keepdims=True))
            p = e / jnp.sum(e, axis=-1, keepdims=True)
            probs_ref[g * pack + h] = p
            total = total + dot(p.astype(bf16), jnp.where(keep, v, jnp.zeros_like(v)))
        mixed_ref[:, g * lane : (g + 1) * lane] = total.astype(bf16)
    res = x + dot(mixed_ref[...], full_ref[:, 3 * width :])
    res_ref[...] = res
    ffn_ref[...] = (res * inverse_rms(res) * gain_two_ref[...]).astype(bf16)
    keep_full.wait()


def expert_kernel(
    ids_ref, rows_ref, g_ref, wi_ref, wd_ref, router_ref,
    send_ref, y_ref, rows_out, hidden_out, dpre_out, dy_out,
):
    j = pl.program_id(0)
    count, per, width = rows_ref.shape
    total = count * per
    experts = router_ref.shape[1]
    x = rows_ref[...].reshape(total, width)
    rows_out[0] = x
    g = g_ref[:, :, :width].reshape(total, width).astype(f32)
    tags = g_ref[:, :, width:].reshape(total, lane).astype(f32)
    other, choice = tags[:, 0:1], tags[:, 1:2]
    logits = dot(x, router_ref[...])
    ids = lax.broadcasted_iota(jnp.int32, (total, experts), 1)
    own_logit = jnp.sum(jnp.where(ids == ids_ref[0] + j, logits, 0.0), -1, keepdims=True)
    other_logit = jnp.sum(jnp.where(ids.astype(f32) == other, logits, 0.0), -1, keepdims=True)
    gate = 1.0 / (1.0 + jnp.exp(other_logit - own_logit))
    d_y = (gate * g).astype(bf16)
    dy_out[0] = d_y
    pre = dot(x, wi_ref[0])
    square = pre * pre
    root = 0.7978845608028654
    gate_in = 0.5 + 0.5 * jnp.tanh(pre * (root + root * 0.044715 * square))
    hidden = (pre * gate_in).astype(bf16)
    hidden_out[0] = hidden
    slope = gate_in + gate_in * (1.0 - gate_in) * (
        pre * (2.0 * root + 6.0 * root * 0.044715 * square)
    )
    d_pre = (dot(d_y, wd_ref[0], 1, 1) * slope).astype(bf16)
    dpre_out[0] = d_pre
    d_rows = dot(d_pre, wi_ref[0], 1, 1).astype(bf16)
    send_ref[:, :, :width] = d_rows.reshape(count, per, width)
    y = dot(hidden, wd_ref[0])
    y_ref[...] = (gate * y).astype(bf16).reshape(count, per, width)
    d_gate = jnp.sum(g * y, axis=-1, keepdims=True)
    high = d_gate.astype(bf16).astype(f32)
    cols = lax.broadcasted_iota(jnp.int32, (total, lane), 1).astype(f32)
    tail = jnp.where(cols == choice, high, jnp.where(cols == choice + 2.0, d_gate - high, 0.0))
    send_ref[:, :, width:] = tail.astype(bf16).reshape(count, per, lane)


def collect_kernel(back_ref, hot_ref, own_ref, *refs):
    pay_refs, total_ref = refs[:-1], refs[-1]
    length = own_ref.shape[0]
    step = pl.program_id(0)
    got = dot(hot_ref[...], back_ref[...].reshape(-1, back_ref.shape[2]))

    @pl.when(step == 0)
    def _():
        total_ref[...] = got

    @pl.when(step > 0)
    def _():
        total_ref[...] += got

    @pl.when(step == pl.num_programs(0) - 1)
    def _():
        own_ref[...] = total_ref[:length, :]
        for k, ref in enumerate(pay_refs):
            ref[...] = total_ref[(k + 1) * length : (k + 2) * length, :].astype(bf16)


def collect(back, hot_back, length, flops=0):
    count, block, wide = back.shape
    step = math.lcm(block, lane) // block
    line = hot_back.shape[0] // length
    kinds = [f32] + [bf16] * (line - 1)
    return pl.pallas_call(
        collect_kernel,
        out_shape=[jax.ShapeDtypeStruct((length, wide), kind) for kind in kinds],
        grid=(count // step,),
        in_specs=[
            pl.BlockSpec((step, block, wide), lambda i: (i, 0, 0)),
            pl.BlockSpec((line * length, step * block), lambda i: (0, i)),
        ],
        out_specs=[pl.BlockSpec((length, wide), lambda i: (0, 0)) for _ in kinds],
        scratch_shapes=[pltpu.VMEM((line * length, wide), f32)],
        compiler_params=pltpu.CompilerParams(vmem_limit_bytes=32 << 20),
        cost_estimate=pl.CostEstimate(flops=flops, bytes_accessed=0, transcendentals=0),
    )(back, hot_back)


def backward_kernel(count, *refs):
    own_ref = refs[0]
    got_refs = refs[1 : 1 + count]
    (
        ffn_ref, res_ref, cot_ref, router_ref, routes_ref, gain_ref, full_ref, proj_ref, probs_ref,
        wide_ref, dres_ref, dlog_ref, gain_grad_ref, ds_ref, dproj_ref,
    ) = refs[1 + count :]
    length, width = ffn_ref.shape
    heads = probs_ref.shape[0]
    head_dim = width // heads
    pack = lane // head_dim
    experts = router_ref.shape[1]
    d = own_ref[...]
    for ref in got_refs:
        d = d + ref[...].astype(f32)
    tail = d[:, width:]
    d = d[:, :width]
    dg = [tail[:, i : i + 1] + tail[:, i + 2 : i + 3] for i in range(2)]
    logits = dot(ffn_ref[...], router_ref[...])
    e = jnp.exp(logits - jnp.max(logits, axis=-1, keepdims=True))
    router = e / jnp.sum(e, axis=-1, keepdims=True)
    ids = lax.broadcasted_iota(jnp.int32, (length, experts), 1)
    hots = [ids == routes_ref[:, i : i + 1] for i in range(2)]
    picked = [jnp.sum(jnp.where(h, router, 0.0), -1, keepdims=True) for h in hots]
    both = picked[0] + picked[1]
    mean = (dg[0] * picked[0] + dg[1] * picked[1]) / (both * both)
    d_router = sum(jnp.where(h, v / both - mean, 0.0) for h, v in zip(hots, dg))
    d_logits = router * (d_router - jnp.sum(router * d_router, -1, keepdims=True))
    d_logits = d_logits.astype(bf16)
    dlog_ref[...] = d_logits
    d_ffn = d + dot(d_logits, router_ref[...], 1, 1)
    res = res_ref[...]
    inv = inverse_rms(res)
    normed = res * inv
    gain_grad_ref[...] = jnp.sum(d_ffn * normed, axis=0, keepdims=True)
    d_norm = d_ffn * gain_ref[...]
    d_res = cot_ref[...].astype(f32) + inv * (
        d_norm - normed * jnp.mean(d_norm * normed, axis=-1, keepdims=True)
    )
    dres_ref[...] = d_res
    d_branch = d_res.astype(bf16)
    d_heads = dot(d_branch, full_ref[...], 1, 1).astype(bf16)
    for g in range(heads // pack):
        q = proj_ref[:, g * lane : (g + 1) * lane]
        k = proj_ref[:, width + g * lane : width + (g + 1) * lane]
        v = proj_ref[:, 2 * width + g * lane : 2 * width + (g + 1) * lane]
        dh = d_heads[:, g * lane : (g + 1) * lane]
        zero = jnp.zeros_like(q)
        sums = [jnp.zeros((length, lane), f32) for _ in range(3)]
        for h in range(pack):
            keep = head_mask((length, lane), h, head_dim)
            p = probs_ref[g * pack + h]
            dh_one = jnp.where(keep, dh, zero)
            d_probs = dot(dh_one, v, 1, 1)
            ds = p * (d_probs - jnp.sum(p * d_probs, axis=-1, keepdims=True))
            ds = ds.astype(bf16)
            ds_ref[g * pack + h] = ds.astype(f32)
            sums[0] = sums[0] + dot(ds, jnp.where(keep, k, zero))
            sums[1] = sums[1] + dot(ds, jnp.where(keep, q, zero), 0, 0)
            sums[2] = sums[2] + dot(p.astype(bf16), dh_one, 0, 0)
        for i, scale in enumerate((0.125, 0.125, 1.0)):
            dproj_ref[:, i * width + g * lane : i * width + (g + 1) * lane] = (sums[i] * scale).astype(bf16)
    columns = wide_ref.shape[2]
    split = 3 * width // columns
    for b in range(wide_ref.shape[0]):
        if b < split:
            wide_ref[b] = dproj_ref[:, b * columns : (b + 1) * columns]
        else:
            wide_ref[b] = d_branch[:, (b - split) * columns : (b - split + 1) * columns]


def product_kernel(ids_ref, own_ref, other_ref, wide_ref, small_ref, share_ref, *refs):
    pay_refs, order_ref, total_ref = refs[:-2], refs[-2], refs[-1]
    pairs, length, width = own_ref.shape
    e, s = ids_ref[0], ids_ref[1]
    count, part = small_ref.shape[0], width // small_ref.shape[0]
    for n in range(2):
        for i in range(pairs):
            at = (n * pairs + i) * length
            order_ref[at : at + length, :] = wide_ref[2 * i + ((e & 1) ^ n)]
    half = pairs * length
    total_ref[...] = dot(own_ref[...].reshape(half, width), order_ref[:half, :], 0, 0) + dot(
        other_ref[...].reshape(half, width), order_ref[half:, :], 0, 0
    )
    for k in range(count):
        target = lax.rem(s - k + count, count)
        rows = total_ref[pl.ds(pl.multiple_of(target * part, 16), part), :]
        ref = share_ref if k == 0 else pay_refs[k - 1]
        ref[:part, :] = rows.astype(ref.dtype)
        ref[part:, :] = small_ref[target].astype(ref.dtype)


def unpack_kernel(ids_ref, *refs):
    whole_refs, (qkv_ref, out_ref, small_ref) = refs[:-3], refs[-3:]
    part, width = out_ref.shape
    cols = small_ref.shape[1]
    split = 3 * width // cols
    pair = len(whole_refs)
    total = jnp.zeros(small_ref.shape, f32)
    for n, ref in enumerate(whole_refs):
        for i in range(ref.shape[0]):
            got = ref[i, :part, :].astype(f32)
            total = total + ref[i, part:, :].astype(f32)
            if pair * i < split:
                target, first = qkv_ref, pair * i
            else:
                target, first = out_ref, pair * i - split
            if pair == 1:
                target[:, first * cols : (first + 1) * cols] = got
            else:
                at = pl.multiple_of((first + ((ids_ref[0] & 1) ^ n)) * cols, lane)
                target[:, pl.ds(at, cols)] = got
    small_ref[...] = total


def tokens_kernel(
    dproj_ref, full_ref, tok_ref, gain_ref, dres_ref, ds_ref, ids_ref, out_ref, gain_grad_ref, table_ref
):
    ids = ids_ref[...]
    for b in range(table_ref.shape[0]):
        found = ids == b
        for h in range(table_ref.shape[1]):
            table_ref[b, h : h + 1, :] = jnp.sum(jnp.where(found, ds_ref[h], 0.0), axis=0, keepdims=True)
    d_in = dot(dproj_ref[...], full_ref[...], 1, 1)
    x = tok_ref[...].astype(f32)
    inv = inverse_rms(x)
    normed = x * inv
    gain_grad_ref[...] = jnp.sum(d_in * normed, axis=0, keepdims=True)
    d_norm = d_in * gain_ref[...]
    out_ref[...] = dres_ref[...] + inv * (
        d_norm - normed * jnp.mean(d_norm * normed, axis=-1, keepdims=True)
    )


def body(
    tokens,
    w_qkv,
    w_out,
    w_router,
    gain_attn,
    gain_ffn,
    bias_table,
    w_in,
    w_down,
    routes,
    slots,
    bucket_ids,
    cotangent,
):
    length, width = tokens.shape
    ne = lax.axis_size("expert")
    ns = lax.axis_size("shard")
    me_e = lax.axis_index("expert")
    me_s = lax.axis_index("shard")
    place_ids = jnp.stack([me_e, me_s]).astype(jnp.int32)
    exp_dev = w_in.shape[0]
    hidden_units = w_in.shape[2]
    experts = exp_dev * ne
    cap = 3 * length // experts
    per = ns * cap
    block = exp_dev * per
    total_rows = ne * block
    group_rows = ne * per
    heads = bias_table.shape[1]
    buckets = bias_table.shape[0] * ns
    part = width // ns

    def from_shift(v, k):
        return lax.ppermute(v, "shard", [(i, (i + k) % ns) for i in range(ns)])

    def to_shift(v, k):
        return lax.ppermute(v, "shard", [(i, (i - k) % ns) for i in range(ns)])

    def plane(v):
        return lax.all_to_all(v, "expert", split_axis=0, concat_axis=0, tiled=True)

    def across(v, bit):
        return lax.ppermute(v, "expert", [(i, i ^ bit) for i in range(ne)])

    cols = width // 2
    mine = me_e & 7
    weight = jnp.where(
        mine < 6,
        lax.dynamic_slice_in_dim(w_qkv, jnp.minimum(mine, 5) * cols, cols, 1),
        lax.dynamic_slice_in_dim(w_out, (jnp.maximum(mine, 6) - 6) * cols, cols, 1),
    )
    line = [weight] + [from_shift(weight, k) for k in range(1, ns)]

    smalls = (w_router, gain_attn, gain_ffn, bias_table, routes.astype(bf16), slots.astype(bf16))
    small = jnp.concatenate([v.reshape(-1) for v in smalls])
    small_rows = -(-small.size // lane)
    small_rows += -small_rows % 16
    small = jnp.pad(small, (0, small_rows * lane - small.size)).reshape(1, small_rows, lane)
    in_order = lax.all_to_all(
        jnp.broadcast_to(small, (ns, small_rows, lane)), "shard", split_axis=0, concat_axis=0, tiled=True
    ).reshape(ns, small_rows * lane)
    cotangent, line = lax.optimization_barrier((cotangent, line))
    halves = []
    for half, bit in ((line[: ns // 2], 2), (line[ns // 2 :], 4)):
        held = jnp.stack(half)[None]
        halves.append(jnp.concatenate([held, across(held, bit)], axis=0))
    halves, in_order = lax.optimization_barrier((halves, in_order))
    pieces = [(v, across(v, bit)) for v, bit in zip(halves, (4, 2))]

    line_g = [cotangent] + [from_shift(cotangent, k) for k in range(1, ns)]
    order = lax.rem(me_s - jnp.arange(ns, dtype=jnp.int32) + ns, ns)
    line_small = jnp.take(in_order, order, axis=0)

    cuts = []
    at = 0
    for v in smalls:
        cuts.append((at, at + v.size))
        at += v.size

    def cut(v, i):
        return v[:, cuts[i][0] : cuts[i][1]]

    full_router = cut(in_order, 0).reshape(width, experts)
    gain_one = cut(in_order, 1).reshape(1, width).astype(f32)
    gain_two = cut(in_order, 2).reshape(1, width).astype(f32)
    table = cut(in_order, 3).reshape(buckets, heads)
    line_g, table, gain_one, gain_two = lax.optimization_barrier((line_g, table, gain_one, gain_two))
    line_routes = cut(line_small, 4).reshape(ns * length, 2)
    line_slots = cut(line_small, 5).reshape(ns * length, 2).astype(jnp.int32)
    place = (
        line_routes.astype(jnp.int32) * per + jnp.repeat(order, length)[:, None] * cap + line_slots
    )
    causal = jnp.arange(length)[:, None] >= jnp.arange(length)[None, :]
    bucket_hot = (
        jnp.arange(buckets, dtype=jnp.int32)[:, None] == bucket_ids.reshape(1, -1)
    ).astype(bf16)
    pair_bias = dot(table, bucket_hot, 0, 0).reshape(heads, length, length)
    pair_bias = jnp.where(causal[None], pair_bias, -1e30)
    hot, hot_back, tags = local_call(
        tables_kernel,
        [((total_rows, ns * length), bf16), ((ns * length, total_rows), bf16), ((total_rows, lane), bf16)],
        [place.T, place, line_routes],
    )
    g_rows = spread(hot, line_g, (ne, block, width + lane), tags)
    last = [p[1] for p in pieces]
    pair_bias, g_rows, last, gain_one, gain_two, place_ids = lax.optimization_barrier(
        (pair_bias, g_rows, last, gain_one, gain_two, place_ids)
    )
    g_arrived = plane(g_rows)
    pieces = [v for p, q in zip(pieces, last) for v in (p[0], across(p[0], 1), q, across(q, 1))]
    attn_in, proj, probs, mixed_low, residual, ffn_in, full = local_call(
        attend_kernel,
        [
            ((length, width), bf16),
            ((length, 3 * width), bf16),
            ((heads, length, length), f32),
            ((length, width), bf16),
            ((length, width), f32),
            ((length, width), bf16),
            ((width, 4 * width), bf16),
        ],
        [place_ids, tokens, gain_one, gain_two, pair_bias, *pieces],
        scalars=1,
        loose=1,
        scratch=[pltpu.VMEM((width, 4 * width), bf16), pltpu.SemaphoreType.DMA],
    )

    line_ffn = [ffn_in] + [from_shift(ffn_in, k) for k in range(1, ns)]
    line_ffn, g_arrived = lax.optimization_barrier((line_ffn, g_arrived))
    sent = spread(hot, line_ffn, (ne, block, width))
    arrived = plane(sent)
    split_e = 3 * ne // 4
    same = [list(range(c, ne, 2)) for c in range(2)]
    factors = jnp.stack([attn_in] * (split_e // 2) + [mixed_low] * ((ne - split_e) // 2))
    arrived, factors = lax.optimization_barrier((arrived, factors))
    held = lax.all_to_all(
        factors, "expert", split_axis=0, concat_axis=0, axis_index_groups=same, tiled=True
    )

    wide_width = width + lane
    first_id = (me_e * exp_dev).astype(jnp.int32).reshape(1)
    send, y_send, rows, hidden, d_pre, d_y = pl.pallas_call(
        expert_kernel,
        out_shape=[
            jax.ShapeDtypeStruct((ne, block, wide_width), bf16),
            jax.ShapeDtypeStruct((ne, block, width), bf16),
            jax.ShapeDtypeStruct((exp_dev, group_rows, width), bf16),
            jax.ShapeDtypeStruct((exp_dev, group_rows, hidden_units), bf16),
            jax.ShapeDtypeStruct((exp_dev, group_rows, hidden_units), bf16),
            jax.ShapeDtypeStruct((exp_dev, group_rows, width), bf16),
        ],
        grid=(exp_dev, 2),
        in_specs=[
            pl.BlockSpec(memory_space=pltpu.SMEM),
            pl.BlockSpec((ne // 2, per, width), lambda j, h: (h, j, 0)),
            pl.BlockSpec((ne // 2, per, wide_width), lambda j, h: (h, j, 0)),
            pl.BlockSpec((1, width, hidden_units), lambda j, h: (j, 0, 0)),
            pl.BlockSpec((1, hidden_units, width), lambda j, h: (j, 0, 0)),
            pl.BlockSpec((width, experts), lambda j, h: (0, 0)),
        ],
        out_specs=[
            pl.BlockSpec((ne // 2, per, wide_width), lambda j, h: (h, j, 0)),
            pl.BlockSpec((ne // 2, per, width), lambda j, h: (h, j, 0)),
            pl.BlockSpec((1, group_rows // 2, width), lambda j, h: (j, h, 0)),
            pl.BlockSpec((1, group_rows // 2, hidden_units), lambda j, h: (j, h, 0)),
            pl.BlockSpec((1, group_rows // 2, hidden_units), lambda j, h: (j, h, 0)),
            pl.BlockSpec((1, group_rows // 2, width), lambda j, h: (j, h, 0)),
        ],
        compiler_params=pltpu.CompilerParams(vmem_limit_bytes=56 << 20),
        cost_estimate=pl.CostEstimate(
            flops=8 * exp_dev * group_rows * width * hidden_units,
            bytes_accessed=16 * exp_dev * group_rows * width,
            transcendentals=0,
        ),
    )(first_id, arrived, g_arrived, w_in, w_down, full_router)
    send, held = lax.optimization_barrier((send, held))
    held_other = across(held, 1)
    d_back = plane(send)
    grad_w_down = jnp.einsum("jrf,jrd->jfd", hidden, d_y, preferred_element_type=f32)
    grad_w_in = jnp.einsum("jrd,jrf->jdf", rows, d_pre, preferred_element_type=f32)
    d_back, grad_w_down, grad_w_in = lax.optimization_barrier((d_back, grad_w_down, grad_w_in))

    own_d, *pays = collect(d_back, hot_back, length, 2 * ns * length * total_rows * wide_width)
    got = [to_shift(v, k + 1) for k, v in enumerate(pays)]
    pays, y_send = lax.optimization_barrier((pays, y_send))
    y_back = plane(y_send)
    columns = 4 * width // ne
    wide, d_residual, d_logits, gain_two_grad, d_scores, d_proj = local_call(
        functools.partial(backward_kernel, ns - 1),
        [
            ((ne, length, columns), bf16),
            ((length, width), f32),
            ((length, experts), bf16),
            ((1, width), f32),
            ((heads, length, length), f32),
            ((length, 3 * width), bf16),
        ],
        [own_d, *got, ffn_in, residual, cotangent, full_router, routes, gain_two, full, proj, probs],
        views={ns + 6: ((width, width), (0, 3))},
        flops=2 * length * width * width + 10 * heads * length * length * lane,
        moved=2 * width * width + 8 * heads * length * length,
    )
    wide, y_back = lax.optimization_barrier((wide, y_back))
    wide = plane(wide)
    grad_tokens, gain_one_grad, grad_table = local_call(
        tokens_kernel,
        [((length, width), f32), ((1, width), f32), ((buckets, heads, lane), f32)],
        [d_proj, full, tokens, gain_one, d_residual, d_scores, bucket_ids],
        views={1: ((width, 3 * width), (0, 0))},
    )
    grad_router = dot(ffn_in, d_logits, 0, 0)

    small_parts = [
        grad_router.reshape(ns, -1),
        gain_one_grad.reshape(ns, -1),
        gain_two_grad.reshape(ns, -1),
        jnp.sum(grad_table, axis=-1).reshape(ns, -1),
    ]
    sizes = [v.shape[1] for v in small_parts]
    small = jnp.concatenate(small_parts, axis=1).astype(bf16)
    each = small.shape[1]
    srows = -(-each // columns)
    srows += -srows % 16
    room = srows * columns
    small = jnp.pad(small, ((0, 0), (0, room - each))).reshape(ns, srows, columns)
    share, *products = local_call(
        product_kernel,
        [((part + srows, columns), f32)] + [((part + srows, columns), bf16)] * (ns - 1),
        [place_ids, held, held_other, wide, small],
        scalars=1,
        scratch=[pltpu.VMEM((ne * length, columns), bf16), pltpu.VMEM((width, columns), f32)],
        flops=2 * ne * length * width * columns,
        moved=2 * ne * length * (width + columns),
    )
    products, y_back = lax.optimization_barrier((products, y_back))
    y_own, *y_pays = collect(y_back, hot_back, length)
    y_own = residual + y_own
    for k, v in enumerate(products):
        share = share + to_shift(v, k + 1).astype(f32)
    share, y_pays = lax.optimization_barrier((share.astype(bf16), y_pays))
    y_got = [to_shift(v, k + 1) for k, v in enumerate(y_pays)]
    by_core = columns % lane == 0
    if by_core:
        copies = jnp.broadcast_to(share[None], (ne // 2,) + share.shape)
        whole = lax.all_to_all(
            copies, "expert", split_axis=0, concat_axis=0, axis_index_groups=same, tiled=True
        )
        whole, y_got[1] = lax.optimization_barrier((whole, y_got[1]))
        whole = [whole, across(whole, 1)]
    else:
        whole = [plane(jnp.broadcast_to(share[None], (ne,) + share.shape))]
    out_qkv, out_out, small = local_call(
        unpack_kernel,
        [((part, 3 * width), f32), ((part, width), f32), ((srows, columns), f32)],
        [place_ids, *whole],
        scalars=1,
    )
    y_own, small = lax.optimization_barrier((y_own, small.reshape(-1)))
    smalls = []
    at = 0
    for size in sizes:
        smalls.append(small[at : at + size])
        at += size

    for v in y_got:
        y_own = y_own + v.astype(f32)
    return (
        y_own.astype(bf16),
        grad_tokens,
        out_qkv,
        out_out,
        smalls[0].reshape(part, experts),
        smalls[1],
        smalls[2],
        smalls[3].reshape(buckets // ns, heads),
        grad_w_in,
        grad_w_down,
    )


def solution(mesh):
    in_specs = (
        P(("expert", "shard"), None),
        P("shard", None),
        P("shard", None),
        P("shard", None),
        P("shard"),
        P("shard"),
        P("shard", None),
        P("expert", None, "shard"),
        P("expert", "shard", None),
        P(("expert", "shard"), None),
        P(("expert", "shard"), None),
        P(),
        P(("expert", "shard"), None),
    )
    out_specs = (
        P(("expert", "shard"), None),
        P(("expert", "shard"), None),
        P("shard", None),
        P("shard", None),
        P("shard", None),
        P("shard"),
        P("shard"),
        P("shard", None),
        P("expert", None, "shard"),
        P("expert", "shard", None),
    )
    return jax.shard_map(body, mesh=mesh, in_specs=in_specs, out_specs=out_specs, check_vma=False)
```
